32 devices in a mesh: doc: 4 (over x, core), topic: 4 (over z), vocab: 2 (over y).
Axes of the slice: x: 2, y: 2, z: 4, core: 2. Of those that a mesh axis runs over, the one named last changes fastest.
Arguments:
- doc_topics: bfloat16 [2048, 16384], P('doc', 'topic'), may hold values from 0 to 1, as said below
- word_logits: bfloat16 [512, 16384], P('vocab', 'topic'), may hold values from -6 to 11
- log_norm: float32 [16384], P('topic'), may hold values from 12 to 16
- tile_doc: int32 [128], P(('doc', 'vocab')), may hold values from 0 to 3, as said below
- tile_word: int32 [128], P(('doc', 'vocab')), may hold values from 0 to 3
- word_counts: int32 [128, 64, 128], P(('doc', 'vocab')), may hold values from 0 to 3, as said below
Outputs:
- doc_topic_grad: float32 [2048, 16384], P('doc', ('topic', 'vocab'))
- word_logit_grad: bfloat16 [512, 16384], P('vocab', 'topic')
The draws below stay inside these ranges and needn't reach their ends.
Inputs may be any that keep to these rules, and one draw needn't show every extreme that they name: `doc_topics`: each document's row is a softmax over the 16384 topics. Within the 16 slots of one doc and vocab index pair no (tile_doc, tile_word) pair repeats. `word_counts`: A slot whose counts are all zero is empty; occupied slots come first in each pair's list, and in every draw some pair has all 16 slots occupied.
All inputs are finite; a program needn't handle non-finite values.
Results may differ from the reference program's by a relative error of at most 0.018.
Values may be sent and summed in bfloat16 or wider, within the bound.
No kernel may reach another device: no remote copies, remote signals or barrier semaphores. Data moves between devices by JAX's collectives and lax.ppermute only.
A program may use at most 128 MiB of HBM per device.

```python
import jax
import jax.numpy as jnp
from jax import lax

K = 16384
DOC_TILE = 128
WORD_TILE = 64
DB_DEV = 4
WB_DEV = 4
TILES_DEV = 16
NDOC = 2048
VWIN = 512
ALL_TILES = 128
N_DOC = 4
N_VOCAB = 2


def tile_layout(key):
    base = jax.random.fold_in(key, 7)
    pair_total = ALL_TILES // TILES_DEV
    places_all = DB_DEV * WB_DEV
    keys = jax.random.split(base, pair_total)

    def pick_places(one_key):
        return jax.random.permutation(one_key, places_all)[:TILES_DEV]
    places = jax.vmap(pick_places)(keys).astype(jnp.int32)
    occupied = jax.random.randint(jax.random.fold_in(base, 11), (pair_total,), TILES_DEV // 4, TILES_DEV + 1)
    fullest = jax.random.randint(jax.random.fold_in(base, 13), (), 0, pair_total)
    occupied = jnp.where(jnp.arange(pair_total) == fullest, TILES_DEV, occupied)
    return (places, occupied)


def draw_tile_doc(key, part):
    places, occupied = tile_layout(key)
    return (places // WB_DEV).reshape(-1).astype(jnp.int32)


def draw_tile_word(key, part):
    places, occupied = tile_layout(key)
    return (places % WB_DEV).reshape(-1).astype(jnp.int32)


def draw_word_counts(key, part):
    places, occupied = tile_layout(key)
    live_slots = (jnp.arange(TILES_DEV)[None, :] < occupied[:, None]).reshape(-1).astype(jnp.int32)
    values = jax.random.randint(jax.random.fold_in(key, 21), (ALL_TILES, WORD_TILE, DOC_TILE), 1, 4)
    present = (jax.random.randint(jax.random.fold_in(key, 23), (ALL_TILES, WORD_TILE, DOC_TILE), 0, 3) == 0).astype(jnp.int32)
    return (values * present * live_slots[:, None, None]).astype(jnp.int32)


def draw_doc_topics(key, part):
    base = jax.random.fold_in(key, 31)
    spread_draw = jnp.clip(jax.random.normal(base, (NDOC, K), jnp.float32), -6.0, 6.0)
    logits = 3.0 * spread_draw
    return jax.nn.softmax(logits, axis=-1).astype(jnp.bfloat16)


def draw_word_logits(key, part):
    base = jax.random.fold_in(key, 41)
    raised = (jax.random.randint(jax.random.fold_in(base, 5), (VWIN, K), 0, 32) == 0).astype(jnp.float32)
    noise = jnp.clip(jax.random.normal(base, (VWIN, K), jnp.float32), -6.0, 6.0)
    lift = 4.0
    return (noise + lift * raised).astype(jnp.bfloat16)


def levels(own_key, shape, pieces, least, top_value):
    def one(dim, parts):
        heights = jax.random.uniform(jax.random.fold_in(jax.random.fold_in(own_key, 6), dim), (parts,), jnp.float32, least / len(pieces), top_value / len(pieces))
        return jnp.repeat(jnp.exp(heights), shape[dim] // parts).reshape((-1,) + (1,) * (len(shape) - dim - 1))

    loudness = one(*pieces[0])
    for cut in pieces[1:]:
        loudness = loudness * one(*cut)
    return loudness


def setup_inputs(seed: int = 0) -> dict:
    splits = jax.random.split(jax.random.key(seed), 7)
    return {
        "doc_topics": draw_doc_topics(jax.random.fold_in(splits[6], 71), 0),
        "word_logits": draw_word_logits(jax.random.fold_in(splits[6], 71), 0),
        "log_norm": jnp.clip(12.0 + 4.0 * jax.random.uniform(splits[2], (K,), jnp.float32) ** levels(splits[2], (K,), ((0, 4),), -0.2, 0.2), 12.0, 16.0),
        "tile_doc": draw_tile_doc(jax.random.fold_in(splits[6], 71), 0),
        "tile_word": draw_tile_word(jax.random.fold_in(splits[6], 71), 0),
        "word_counts": draw_word_counts(jax.random.fold_in(splits[6], 71), 0),
    }


def reference(doc_topics, word_logits, log_norm, tile_doc, tile_word, word_counts):
    word_prob = jnp.exp(word_logits.astype(jnp.float32) - log_norm[None, :]).astype(jnp.bfloat16)
    doc_span = DB_DEV * DOC_TILE
    word_span = WB_DEV * WORD_TILE
    pair_total = N_DOC * N_VOCAB

    def visit_pair(state_pair, pair):
        theta_acc, beta_acc = state_pair
        shard_doc = (pair // N_VOCAB).astype(jnp.int32)
        shard_word = (pair % N_VOCAB).astype(jnp.int32)
        doc_start = (shard_doc * doc_span).astype(jnp.int32)
        word_start = (shard_word * word_span).astype(jnp.int32)
        topic_rows = lax.dynamic_slice_in_dim(doc_topics, doc_start, doc_span, 0).astype(jnp.float32)
        topic_rows = topic_rows.reshape(DB_DEV, DOC_TILE, K)
        prob_shard = lax.dynamic_slice_in_dim(word_prob, word_start, word_span, 0)
        prob_rows = prob_shard.astype(jnp.float32).reshape(WB_DEV, WORD_TILE, K)
        slot_start = (pair * TILES_DEV).astype(jnp.int32)
        doc_index = lax.dynamic_slice_in_dim(tile_doc, slot_start, TILES_DEV, 0)
        word_index = lax.dynamic_slice_in_dim(tile_word, slot_start, TILES_DEV, 0)
        counted = lax.dynamic_slice_in_dim(word_counts, slot_start, TILES_DEV, 0).astype(jnp.float32)
        doc_part = topic_rows[doc_index]
        word_part = prob_rows[word_index]
        rate = jnp.einsum('gwk,gdk->gwd', word_part, doc_part)
        ratios = (counted / (WORD_TILE * rate)).astype(jnp.bfloat16)
        ratios = lax.optimization_barrier(ratios).astype(jnp.float32)
        toward_theta = jnp.einsum('gwd,gwk->gdk', ratios, word_part)
        toward_beta = jnp.einsum('gwd,gdk->gwk', ratios, doc_part)
        theta_sum = jnp.zeros((DB_DEV, DOC_TILE, K), jnp.float32).at[doc_index].add(toward_theta)
        beta_sum = jnp.zeros((WB_DEV, WORD_TILE, K), jnp.float32).at[word_index].add(toward_beta)
        theta_part = (-theta_sum.reshape(doc_span, K)).astype(jnp.bfloat16)
        theta_part = lax.optimization_barrier(theta_part).astype(jnp.float32)
        beta_part = (-prob_shard.astype(jnp.float32) * beta_sum.reshape(word_span, K)).astype(jnp.bfloat16)
        beta_part = lax.optimization_barrier(beta_part).astype(jnp.float32)
        old_theta = lax.dynamic_slice_in_dim(theta_acc, doc_start, doc_span, 0)
        theta_acc = lax.dynamic_update_slice_in_dim(theta_acc, old_theta + theta_part, doc_start, 0)
        old_beta = lax.dynamic_slice_in_dim(beta_acc, word_start, word_span, 0)
        beta_acc = lax.dynamic_update_slice_in_dim(beta_acc, old_beta + beta_part, word_start, 0)
        return (theta_acc, beta_acc), None

    initial = (jnp.zeros((NDOC, K), jnp.float32), jnp.zeros((VWIN, K), jnp.float32))
    (theta_acc, beta_acc), _ = lax.scan(visit_pair, initial, jnp.arange(pair_total, dtype=jnp.int32))
    return theta_acc, beta_acc.astype(jnp.bfloat16)
```

```python
import functools

import jax
import jax.numpy as jnp
from jax import lax
from jax.experimental import pallas as pl
from jax.experimental.pallas import tpu as pltpu
from jax.sharding import PartitionSpec as P

BF16 = jnp.bfloat16
F32 = jnp.float32
VMEM_LIMIT = 24 * 1024 * 1024


def block_width(width, most):
    return min(width, most)


def call_params():
    return pltpu.CompilerParams(vmem_limit_bytes=VMEM_LIMIT)


def rate_partial(doc_topics, word_logits, log_norm, place, n_topic):
    docs, width = doc_topics.shape
    words = word_logits.shape[0]
    step_width = block_width(width, 1024)
    steps = width // step_width
    chunk = words // n_topic

    def kernel(place_ref, doc_ref, logit_ref, norm_ref, *rest):
        outs, acc = rest[:-1], rest[-1]
        step = pl.program_id(0)
        prob = jnp.exp(logit_ref[...].astype(F32) - norm_ref[...]).astype(BF16)
        part = lax.dot_general(prob, doc_ref[...], (((1,), (1,)), ((), ())), preferred_element_type=F32)

        @pl.when(step == 0)
        def _():
            acc[...] = part

        @pl.when(step > 0)
        def _():
            acc[...] += part

        @pl.when(step == steps - 1)
        def _():
            for s in range(n_topic):
                owner = lax.rem(place_ref[0] + s, n_topic)
                outs[s][...] = acc[pl.ds(pl.multiple_of(owner * chunk, chunk), chunk), :].astype(BF16)

    return pl.pallas_call(
        kernel,
        out_shape=[jax.ShapeDtypeStruct((chunk, docs), BF16)] * n_topic,
        grid_spec=pltpu.PrefetchScalarGridSpec(
            num_scalar_prefetch=1,
            grid=(steps,),
            in_specs=[
                pl.BlockSpec((docs, step_width), lambda j, p: (0, j)),
                pl.BlockSpec((words, step_width), lambda j, p: (0, j)),
                pl.BlockSpec((1, step_width), lambda j, p: (0, j)),
            ],
            out_specs=[pl.BlockSpec((chunk, docs), lambda j, p: (0, 0))] * n_topic,
            scratch_shapes=[pltpu.VMEM((words, docs), F32)],
        ),
        compiler_params=call_params(),
        cost_estimate=pl.CostEstimate(
            flops=2 * words * docs * width, bytes_accessed=2 * (words + docs) * width, transcendentals=words * width
        ),
        name="rate_partial",
    )(place, doc_topics, word_logits, log_norm)


def chunk_counts(word_counts, tile_doc, tile_word, place, n_topic, docs, words):
    slots, word_tile, doc_tile = word_counts.shape
    chunk = words // n_topic

    def kernel(place_ref, doc_at, word_at, count_ref, out_ref):
        first = place_ref[0] * chunk
        block = first // word_tile
        row = pl.multiple_of(lax.rem(first, word_tile), chunk)
        out_ref[...] = jnp.zeros_like(out_ref)
        for s in range(slots):
            @pl.when(word_at[s] == block)
            def _():
                column = pl.multiple_of(doc_at[s] * doc_tile, doc_tile)
                out_ref[:, pl.ds(column, doc_tile)] = count_ref[s, pl.ds(row, chunk), :].astype(F32)

    return pl.pallas_call(
        kernel,
        out_shape=jax.ShapeDtypeStruct((chunk, docs), F32),
        grid_spec=pltpu.PrefetchScalarGridSpec(
            num_scalar_prefetch=3,
            grid=(1,),
            in_specs=[pl.BlockSpec(word_counts.shape, lambda j, *_: (0, 0, 0))],
            out_specs=pl.BlockSpec((chunk, docs), lambda j, *_: (0, 0)),
        ),
        compiler_params=call_params(),
        cost_estimate=pl.CostEstimate(flops=words * docs, bytes_accessed=4 * words * docs, transcendentals=0),
        name="chunk_counts",
    )(place, tile_doc, tile_word, word_counts)


def ratio_chunk(parts, counts, word_tile):
    def kernel(*refs):
        part_refs, count_ref, out_ref = refs[:-2], refs[-2], refs[-1]
        rate = part_refs[0][...].astype(F32)
        for ref in part_refs[1:]:
            rate += ref[...].astype(F32)
        out_ref[...] = (count_ref[...] / (word_tile * rate)).astype(BF16)

    return pl.pallas_call(
        kernel,
        out_shape=jax.ShapeDtypeStruct(counts.shape, BF16),
        compiler_params=call_params(),
        cost_estimate=pl.CostEstimate(flops=10 * counts.size, bytes_accessed=16 * counts.size, transcendentals=0),
        name="ratio_chunk",
    )(*parts, counts)


def join_ratio(chunks, place, n_topic):
    rows, docs = chunks[0].shape

    def kernel(place_ref, *refs):
        out_ref = refs[-1]
        for s in range(n_topic):
            owner = lax.rem(place_ref[0] + n_topic - s, n_topic)
            out_ref[pl.ds(pl.multiple_of(owner * rows, rows), rows), :] = refs[s][...]

    return pl.pallas_call(
        kernel,
        out_shape=jax.ShapeDtypeStruct((rows * n_topic, docs), BF16),
        grid_spec=pltpu.PrefetchScalarGridSpec(
            num_scalar_prefetch=1,
            grid=(1,),
            in_specs=[pl.BlockSpec((rows, docs), lambda j, p: (0, 0))] * n_topic,
            out_specs=pl.BlockSpec((rows * n_topic, docs), lambda j, p: (0, 0)),
        ),
        compiler_params=call_params(),
        cost_estimate=pl.CostEstimate(flops=0, bytes_accessed=4 * rows * docs * n_topic, transcendentals=0),
        name="join_ratio",
    )(place, *chunks)


def beta_piece(ratio, doc_topics, word_logits, log_norm, side, piece, pieces):
    docs, width = doc_topics.shape
    words = word_logits.shape[0]
    span = width // pieces
    half = words // 2

    def kernel(side_ref, ratio_ref, doc_ref, logit_ref, norm_ref, keep_ref, send_ref):
        for out_ref, which in ((send_ref, 1 - side_ref[0]), (keep_ref, side_ref[0])):
            rows = pl.ds(pl.multiple_of(which * half, half), half)
            summed = jnp.dot(ratio_ref[rows, :], doc_ref[...], preferred_element_type=F32)
            prob = jnp.exp(logit_ref[rows, :].astype(F32) - norm_ref[...]).astype(BF16).astype(F32)
            out_ref[...] = (-prob * summed).astype(BF16)

    return pl.pallas_call(
        kernel,
        out_shape=[jax.ShapeDtypeStruct((half, span), BF16)] * 2,
        grid_spec=pltpu.PrefetchScalarGridSpec(
            num_scalar_prefetch=1,
            grid=(1,),
            in_specs=[
                pl.BlockSpec((words, docs), lambda j, p: (0, 0)),
                pl.BlockSpec((docs, span), lambda j, p: (0, piece)),
                pl.BlockSpec((words, span), lambda j, p: (0, piece)),
                pl.BlockSpec((1, span), lambda j, p: (0, piece)),
            ],
            out_specs=[pl.BlockSpec((half, span), lambda j, p: (0, 0))] * 2,
        ),
        compiler_params=call_params(),
        cost_estimate=pl.CostEstimate(
            flops=2 * words * docs * span, bytes_accessed=2 * (2 * words + docs) * span, transcendentals=words * span
        ),
        name="beta_piece",
    )(side, ratio, doc_topics, word_logits, log_norm)


def theta_grad(ratios, logits, log_norm):
    words, docs = ratios[0].shape
    width = logits[0].shape[1]
    span = block_width(width, 512)
    count = len(ratios)

    def kernel(*refs):
        ratio_refs, logit_refs = refs[:count], refs[count : 2 * count]
        norm_ref, out_ref, turned = refs[2 * count :]

        @pl.when(pl.program_id(0) == 0)
        def _():
            for l in range(count):
                turned[:, l * words : (l + 1) * words] = (-ratio_refs[l][...].astype(F32)).T.astype(BF16)

        prob = jnp.concatenate(
            [jnp.exp(ref[...].astype(F32) - norm_ref[...]).astype(BF16) for ref in logit_refs], axis=0
        )
        out_ref[...] = jnp.dot(turned[...], prob, preferred_element_type=F32)

    return pl.pallas_call(
        kernel,
        out_shape=jax.ShapeDtypeStruct((docs, width), F32),
        grid=(width // span,),
        in_specs=[pl.BlockSpec((words, docs), lambda j: (0, 0))] * count
        + [pl.BlockSpec((words, span), lambda j: (0, j))] * count
        + [pl.BlockSpec((1, span), lambda j: (0, j))],
        out_specs=pl.BlockSpec((docs, span), lambda j: (0, j)),
        scratch_shapes=[pltpu.VMEM((docs, count * words), BF16)],
        compiler_params=call_params(),
        cost_estimate=pl.CostEstimate(
            flops=2 * count * words * docs * width,
            bytes_accessed=(4 * docs + 2 * count * words) * width,
            transcendentals=count * words * width,
        ),
        name="theta_grad",
    )(*ratios, *logits, log_norm)


def place_piece(own, other, side, piece, pieces, so_far):
    half, span = own.shape

    def kernel(side_ref, own_ref, other_ref, *rest):
        out_ref = rest[-1]
        step = pl.program_id(0)

        @pl.when(step == 0)
        def _():
            out_ref[...] = own_ref[...]

        @pl.when(step == 1)
        def _():
            out_ref[...] = other_ref[...]

    first = so_far is None
    return pl.pallas_call(
        kernel,
        out_shape=jax.ShapeDtypeStruct((2 * half, span * pieces), BF16),
        grid_spec=pltpu.PrefetchScalarGridSpec(
            num_scalar_prefetch=1,
            grid=(2,),
            in_specs=[pl.BlockSpec((half, span), lambda j, p: (0, 0))] * 2
            + ([] if first else [pl.BlockSpec(memory_space=pl.ANY)]),
            out_specs=pl.BlockSpec((half, span), lambda j, p: (lax.rem(p[0] + j, 2), piece)),
        ),
        input_output_aliases={} if first else {3: 0},
        compiler_params=call_params(),
        cost_estimate=pl.CostEstimate(flops=0, bytes_accessed=8 * half * span, transcendentals=0),
        name="place_piece",
    )(side, own, other, *([] if first else [so_far]))


def on_device(sizes, doc_topics, word_logits, log_norm, tile_doc, tile_word, word_counts):
    n_doc, n_topic, n_vocab = sizes
    docs, width = doc_topics.shape
    words = word_logits.shape[0]
    word_tile = word_counts.shape[1]
    norm = log_norm[None, :]
    topic_at = lax.axis_index("topic").astype(jnp.int32)
    vocab_at = lax.axis_index("vocab").astype(jnp.int32)
    place = topic_at[None]
    side = lax.rem(lax.axis_index("doc").astype(jnp.int32), 2)[None]

    def shift(array, axis, count, by):
        return lax.ppermute(array, axis, [(i, (i + by) % count) for i in range(count)])

    def swap(array, bit):
        return lax.ppermute(array, "doc", [(i, i ^ bit) for i in range(n_doc)])

    share = width // n_vocab
    own_logits = lax.dynamic_slice_in_dim(word_logits, vocab_at * share, share, 1)
    own_norm = lax.dynamic_slice_in_dim(norm, vocab_at * share, share, 1)
    logits_all = [own_logits]
    for s in range(1, n_vocab):
        target = lax.rem(vocab_at + s, n_vocab)
        logits_all.append(shift(lax.dynamic_slice_in_dim(word_logits, target * share, share, 1), "vocab", n_vocab, s))

    parts = rate_partial(doc_topics, word_logits, norm, place, n_topic)
    arrived = [parts[0]] + [shift(parts[s], "topic", n_topic, s) for s in range(1, n_topic)]
    counts = chunk_counts(word_counts, tile_doc, tile_word, place, n_topic, docs, words)
    own_ratio = ratio_chunk(arrived, counts, word_tile)
    chunks = [own_ratio] + [shift(own_ratio, "topic", n_topic, s) for s in range(1, n_topic)]
    ratio = join_ratio(chunks, place, n_topic)

    ratios = [ratio] + [shift(ratio, "vocab", n_vocab, s) for s in range(1, n_vocab)]

    pieces = 4
    out = None
    for piece in range(pieces):
        keep, send = beta_piece(ratio, doc_topics, word_logits, norm, side, piece, pieces)
        held = keep.astype(F32) + swap(send, 1).astype(F32)
        bit = 2
        while bit < n_doc:
            held = held.astype(BF16)
            held = held.astype(F32) + swap(held, bit).astype(F32)
            bit *= 2
        held = held.astype(BF16)
        out = place_piece(held, swap(held, 1), side, piece, pieces, out)

    theta = theta_grad(ratios, logits_all, own_norm)
    return theta, out


def solution(mesh):
    placed = (
        P("doc", "topic"),
        P("vocab", "topic"),
        P("topic"),
        P(("doc", "vocab")),
        P(("doc", "vocab")),
        P(("doc", "vocab"), None, None),
    )
    sizes = (mesh.shape["doc"], mesh.shape["topic"], mesh.shape["vocab"])
    return jax.shard_map(
        functools.partial(on_device, sizes),
        mesh=mesh,
        in_specs=placed,
        out_specs=(P("doc", ("topic", "vocab")), P("vocab", "topic")),
        check_vma=False,
    )
```

```python
import functools

import jax
import jax.numpy as jnp
from jax import lax
from jax.experimental import pallas as pl
from jax.experimental.pallas import tpu as pltpu
from jax.sharding import PartitionSpec as P

BF16 = jnp.bfloat16
F32 = jnp.float32
VMEM_LIMIT = 28 * 1024 * 1024
ANY = pl.BlockSpec(memory_space=pl.ANY)
HBM = pl.BlockSpec(memory_space=pltpu.HBM)
VMEM = pl.BlockSpec(memory_space=pltpu.VMEM)
SMEM = pl.BlockSpec(memory_space=pltpu.SMEM)


def call_params():
    return pltpu.CompilerParams(vmem_limit_bytes=VMEM_LIMIT)


def cost(flops, bytes_accessed, transcendentals=0):
    return pl.CostEstimate(flops=flops, bytes_accessed=bytes_accessed, transcendentals=transcendentals)


def in_hbm(array):
    return pltpu.with_memory_space_constraint(array, pltpu.HBM)


def first_row(index, rows):
    return pl.multiple_of(index * rows, rows)


def rate_partial(doc_topics, word_logits, log_norm, place, n_topic):
    docs, width = doc_topics.shape
    words = word_logits.shape[0]
    span = min(width, 1024)
    steps = width // span
    chunk = words // n_topic

    def kernel(place_ref, doc_in, logit_in, norm_ref, *rest):
        parts, (doc_ref, prob_ref, logit_ref, acc, sems) = rest[:n_topic], rest[n_topic:]
        copies = []
        for j in range(steps):
            at = pl.ds(j * span, span)
            copies.append(
                (
                    pltpu.make_async_copy(logit_in.at[:, at], logit_ref.at[:, at], sems.at[0, j]),
                    pltpu.make_async_copy(doc_in.at[:, at], doc_ref.at[:, at], sems.at[1, j]),
                )
            )
        for pair in copies:
            for copy in pair:
                copy.start()
        for j in range(steps):
            at = pl.ds(j * span, span)
            copies[j][0].wait()
            prob = jnp.exp(logit_ref[:, at].astype(F32) - norm_ref[:, at]).astype(BF16)
            prob_ref[:, at] = prob
            copies[j][1].wait()
            part = lax.dot_general(
                prob, doc_ref[:, at], (((1,), (1,)), ((), ())), preferred_element_type=F32
            )
            if j == 0:
                acc[...] = part
            else:
                acc[...] += part
        for s in range(n_topic):
            owner = lax.rem(place_ref[0] + s, n_topic)
            parts[s][...] = acc[pl.ds(first_row(owner, chunk), chunk), :].astype(BF16)

    out = pl.pallas_call(
        kernel,
        out_shape=[jax.ShapeDtypeStruct((chunk, docs), BF16)] * n_topic
        + [jax.ShapeDtypeStruct(doc_topics.shape, BF16), jax.ShapeDtypeStruct(word_logits.shape, BF16)],
        in_specs=[SMEM, HBM, HBM, VMEM],
        out_specs=[VMEM] * (n_topic + 2),
        scratch_shapes=[
            pltpu.VMEM(word_logits.shape, BF16),
            pltpu.VMEM((words, docs), F32),
            pltpu.SemaphoreType.DMA((2, steps)),
        ],
        compiler_params=call_params(),
        cost_estimate=cost(2 * words * docs * width, 2 * (words + docs) * width, words * width),
        name="rate_partial",
    )(place, in_hbm(doc_topics), in_hbm(word_logits), log_norm)
    return out[:n_topic], out[n_topic], out[n_topic + 1]


def chunk_counts(word_counts, tile_doc, tile_word, place, n_topic, docs, words):
    slots, word_tile, doc_tile = word_counts.shape
    chunk = words // n_topic

    def kernel(place_ref, doc_at, word_at, count_ref, out_ref):
        first = place_ref[0] * chunk
        block = first // word_tile
        row = pl.multiple_of(lax.rem(first, word_tile), chunk)
        out_ref[...] = jnp.zeros_like(out_ref)
        for s in range(slots):
            @pl.when(word_at[s] == block)
            def _():
                column = first_row(doc_at[s], doc_tile)
                out_ref[:, pl.ds(column, doc_tile)] = count_ref[s, pl.ds(row, chunk), :].astype(F32)

    return pl.pallas_call(
        kernel,
        out_shape=jax.ShapeDtypeStruct((chunk, docs), F32),
        in_specs=[SMEM, SMEM, SMEM, VMEM],
        out_specs=VMEM,
        compiler_params=call_params(),
        cost_estimate=cost(words * docs, 4 * words * docs),
        name="chunk_counts",
    )(place, tile_doc, tile_word, word_counts)


def ratio_chunk(parts, counts, word_tile):
    def kernel(*refs):
        part_refs, count_ref, out_ref = refs[:-2], refs[-2], refs[-1]
        rate = part_refs[0][...].astype(F32)
        for ref in part_refs[1:]:
            rate += ref[...].astype(F32)
        out_ref[...] = (count_ref[...] / (word_tile * rate)).astype(BF16)

    return pl.pallas_call(
        kernel,
        out_shape=jax.ShapeDtypeStruct(counts.shape, BF16),
        compiler_params=call_params(),
        cost_estimate=cost(10 * counts.size, 16 * counts.size),
        name="ratio_chunk",
    )(*parts, counts)


def join_ratio(chunks, place, n_topic):
    rows, docs = chunks[0].shape

    def kernel(place_ref, *refs):
        out_ref = refs[-1]
        for s in range(n_topic):
            owner = lax.rem(place_ref[0] + n_topic - s, n_topic)
            out_ref[pl.ds(first_row(owner, rows), rows), :] = refs[s][...]

    return pl.pallas_call(
        kernel,
        out_shape=jax.ShapeDtypeStruct((rows * n_topic, docs), BF16),
        in_specs=[SMEM] + [VMEM] * n_topic,
        out_specs=VMEM,
        compiler_params=call_params(),
        cost_estimate=cost(0, 4 * rows * docs * n_topic),
        name="join_ratio",
    )(place, *chunks)


def beta_piece(ratio, docs_held, prob_held, side, piece, pieces, after):
    docs, width = docs_held.shape
    words = prob_held.shape[0]
    span = width // pieces
    half = words // 2

    def kernel(side_ref, ratio_ref, doc_ref, prob_ref, *rest):
        keep_ref, send_ref = rest[-2:]
        for out_ref, which in ((send_ref, 1 - side_ref[0]), (keep_ref, side_ref[0])):
            rows = pl.ds(first_row(which, half), half)
            summed = jnp.dot(ratio_ref[rows, :], doc_ref[...], preferred_element_type=F32)
            out_ref[...] = (-prob_ref[rows, :].astype(F32) * summed).astype(BF16)

    return pl.pallas_call(
        kernel,
        out_shape=[jax.ShapeDtypeStruct((half, span), BF16)] * 2,
        grid=(1,),
        in_specs=[
            SMEM,
            pl.BlockSpec((words, docs), lambda j: (0, 0)),
            pl.BlockSpec((docs, span), lambda j: (0, piece)),
            pl.BlockSpec((words, span), lambda j: (0, piece)),
        ]
        + [ANY] * len(after),
        out_specs=[pl.BlockSpec((half, span), lambda j: (0, 0))] * 2,
        compiler_params=call_params(),
        cost_estimate=cost(2 * words * docs * span, 2 * (2 * words + docs) * span),
        name="beta_piece",
    )(side, ratio, docs_held, prob_held, *after)


def add_pair(own, other, after=()):
    def kernel(own_ref, other_ref, *rest):
        rest[-1][...] = (own_ref[...].astype(F32) + other_ref[...].astype(F32)).astype(BF16)

    return pl.pallas_call(
        kernel,
        out_shape=jax.ShapeDtypeStruct(own.shape, BF16),
        in_specs=[VMEM, VMEM] + [ANY] * len(after),
        out_specs=VMEM,
        compiler_params=call_params(),
        cost_estimate=cost(own.size, 6 * own.size),
        name="add_pair",
    )(own, other, *after)


def theta_grad(ratio, far_ratios, prob_held, far_logits, log_norm, vocab_at, side):
    words, docs = ratio.shape
    half = words // 2
    share = log_norm.shape[1]
    far = len(far_ratios)
    count = far + 1
    span = min(share, 512)

    def kernel(vocab_ref, side_ref, ratio_ref, *refs):
        far_refs, prob_ref = refs[:far], refs[far]
        logit_refs, norm_ref = refs[far + 1 : 3 * far + 1], refs[3 * far + 1]
        out_ref, done_ref, turned = refs[-3:]
        done_ref[...] = jnp.zeros_like(done_ref)

        @pl.when(pl.program_id(0) == 0)
        def _():
            def put(rows, at):
                turned[:, at : at + rows.shape[0]] = (-rows.astype(F32)).T.astype(BF16)

            put(ratio_ref[...], 0)
            for l in range(far):
                for h in range(2):
                    which = side_ref[0] if h == 0 else 1 - side_ref[0]
                    put(far_refs[l][pl.ds(first_row(which, half), half), :], (l + 1) * words + h * half)

        prob = jnp.concatenate(
            [prob_ref[...]] + [jnp.exp(ref[...].astype(F32) - norm_ref[...]).astype(BF16) for ref in logit_refs],
            axis=0,
        )
        out_ref[...] = jnp.dot(turned[...], prob, preferred_element_type=F32)

    blocks = share // span
    return pl.pallas_call(
        kernel,
        out_shape=[jax.ShapeDtypeStruct((docs, share), F32), jax.ShapeDtypeStruct((8, 128), F32)],
        grid_spec=pltpu.PrefetchScalarGridSpec(
            num_scalar_prefetch=2,
            grid=(blocks,),
            in_specs=[pl.BlockSpec((words, docs), lambda j, v, s: (0, 0))] * count
            + [pl.BlockSpec((words, span), lambda j, v, s: (0, v[0] * blocks + j))]
            + [pl.BlockSpec((half, span), lambda j, v, s: (0, j))] * (2 * far)
            + [pl.BlockSpec((1, span), lambda j, v, s: (0, j))],
            out_specs=[
                pl.BlockSpec((docs, span), lambda j, v, s: (0, j)),
                pl.BlockSpec((8, 128), lambda j, v, s: (0, 0)),
            ],
            scratch_shapes=[pltpu.VMEM((docs, count * words), BF16)],
        ),
        compiler_params=call_params(),
        cost_estimate=cost(
            2 * count * words * docs * share, (4 * docs + 2 * count * words) * share, count * words * share
        ),
        name="theta_grad",
    )(vocab_at, side, ratio, *far_ratios, prob_held, *far_logits, log_norm)


def place_pieces(own, other, side):
    pieces = len(own)
    half, span = own[0].shape

    def kernel(side_ref, *refs):
        out_ref, sems = refs[-2:]
        copies = []
        for p in range(pieces):
            for h, which in ((0, side_ref[0]), (1, 1 - side_ref[0])):
                target = out_ref.at[pl.ds(first_row(which, half), half), pl.ds(p * span, span)]
                copies.append(pltpu.make_async_copy(refs[h * pieces + p], target, sems.at[h, p]))
        for copy in copies:
            copy.start()
        for copy in copies:
            copy.wait()

    return pl.pallas_call(
        kernel,
        out_shape=jax.ShapeDtypeStruct((2 * half, span * pieces), BF16),
        in_specs=[SMEM] + [VMEM] * (2 * pieces),
        out_specs=HBM,
        scratch_shapes=[pltpu.SemaphoreType.DMA((2, pieces))],
        compiler_params=call_params(),
        cost_estimate=cost(0, 8 * half * span * pieces),
        name="place_pieces",
    )(side, *own, *other)


def on_device(sizes, doc_topics, word_logits, log_norm, tile_doc, tile_word, word_counts):
    n_doc, n_topic, n_vocab = sizes
    docs, width = doc_topics.shape
    words = word_logits.shape[0]
    word_tile = word_counts.shape[1]
    norm = log_norm[None, :]
    place = lax.axis_index("topic").astype(jnp.int32)[None]
    vocab_at = lax.axis_index("vocab").astype(jnp.int32)
    side = lax.rem(lax.axis_index("doc").astype(jnp.int32), 2)

    def shift(array, axis, count, by):
        return lax.ppermute(array, axis, [(i, (i + by) % count) for i in range(count)])

    def swap(array, bit):
        return lax.ppermute(array, "doc", [(i, i ^ bit) for i in range(n_doc)])

    share = width // n_vocab
    half = words // 2
    own_norm = lax.dynamic_slice_in_dim(norm, vocab_at * share, share, 1)
    far_logits = []
    for s in range(1, n_vocab):
        target = lax.rem(vocab_at + s, n_vocab)
        near_half = shift(
            lax.dynamic_slice(word_logits, (side * half, target * share), (half, share)), "vocab", n_vocab, s
        )
        far_logits += [near_half, swap(near_half, 1)]

    parts, docs_held, prob_held = rate_partial(doc_topics, word_logits, norm, place, n_topic)
    arrived = [parts[0]] + [shift(parts[s], "topic", n_topic, s) for s in range(1, n_topic)]
    counts = chunk_counts(word_counts, tile_doc, tile_word, place, n_topic, docs, words)
    own_ratio = ratio_chunk(arrived, counts, word_tile)
    chunks = [own_ratio] + [shift(own_ratio, "topic", n_topic, s) for s in range(1, n_topic)]
    ratio = join_ratio(chunks, place, n_topic)
    far_ratios = [shift(ratio, "vocab", n_vocab, s) for s in range(1, n_vocab)]
    theta, theta_done = theta_grad(ratio, far_ratios, prob_held, far_logits, own_norm, vocab_at[None], side[None])

    pieces = 4
    halves, sums = [], []
    for p in range(pieces):
        after = [sums[p - 2]] if p >= 2 else []
        keep, send = beta_piece(ratio, docs_held, prob_held, side[None], p, pieces, after)
        halves.append((keep, swap(send, 1)))
        if p >= 1:
            sums.append(add_pair(*halves[p - 1]))
    sums.append(add_pair(*halves[-1]))
    bit = 2
    while bit < n_doc:
        sums = [add_pair(part, swap(part, bit), [theta_done] if p == 2 else []) for p, part in enumerate(sums)]
        bit *= 2
    out = place_pieces(sums, [swap(part, 1) for part in sums], side[None])
    return theta, out


def solution(mesh):
    placed = (
        P("doc", "topic"),
        P("vocab", "topic"),
        P("topic"),
        P(("doc", "vocab")),
        P(("doc", "vocab")),
        P(("doc", "vocab"), None, None),
    )
    sizes = (mesh.shape["doc"], mesh.shape["topic"], mesh.shape["vocab"])
    return jax.shard_map(
        functools.partial(on_device, sizes),
        mesh=mesh,
        in_specs=placed,
        out_specs=(P("doc", ("topic", "vocab")), P("vocab", "topic")),
        check_vma=False,
    )
```

```python
import functools

import jax
import jax.numpy as jnp
from jax import lax
from jax.experimental import pallas as pl
from jax.experimental.pallas import tpu as pltpu
from jax.sharding import PartitionSpec as P

BF16 = jnp.bfloat16
F32 = jnp.float32
MIB = 1024 * 1024
ANY = pl.BlockSpec(memory_space=pl.ANY)
HBM = pl.BlockSpec(memory_space=pltpu.HBM)
VMEM = pl.BlockSpec(memory_space=pltpu.VMEM)
SMEM = pl.BlockSpec(memory_space=pltpu.SMEM)


def call_params(mib=8):
    return pltpu.CompilerParams(vmem_limit_bytes=mib * MIB)


def cost(flops, bytes_accessed, transcendentals=0):
    return pl.CostEstimate(flops=flops, bytes_accessed=bytes_accessed, transcendentals=transcendentals)


def in_hbm(array):
    return pltpu.with_memory_space_constraint(array, pltpu.HBM)


def first_row(index, rows):
    return pl.multiple_of(index * rows, rows)


def rate_partial(doc_topics, word_logits, log_norm, n_topic):
    docs, width = doc_topics.shape
    words = word_logits.shape[0]
    span = min(width, 1024)
    steps = width // span
    chunk = words // n_topic

    def kernel(doc_in, logit_in, norm_in, part_ref, doc_ref, prob_ref, norm_ref, logit_ref, acc, sems, norm_sem):
        norm_copy = pltpu.make_async_copy(norm_in, norm_ref, norm_sem)
        norm_copy.start()
        copies = []
        for j in range(steps):
            at = pl.ds(j * span, span)
            copies.append(
                (
                    pltpu.make_async_copy(logit_in.at[:, at], logit_ref.at[:, at], sems.at[0, j]),
                    pltpu.make_async_copy(doc_in.at[:, at], doc_ref.at[:, at], sems.at[1, j]),
                )
            )
        for pair in copies:
            for copy in pair:
                copy.start()
        norm_copy.wait()
        for j in range(steps):
            at = pl.ds(j * span, span)
            copies[j][0].wait()
            prob = jnp.exp(logit_ref[:, at].astype(F32) - norm_ref[:, at]).astype(BF16)
            prob_ref[:, at] = prob
            copies[j][1].wait()
            part = lax.dot_general(
                prob, doc_ref[:, at], (((1,), (1,)), ((), ())), preferred_element_type=F32
            )
            if j == 0:
                acc[...] = part
            else:
                acc[...] += part
        for s in range(n_topic):
            part_ref[s] = acc[s * chunk : (s + 1) * chunk, :].astype(BF16)

    return pl.pallas_call(
        kernel,
        out_shape=[
            jax.ShapeDtypeStruct((n_topic, chunk, docs), BF16),
            jax.ShapeDtypeStruct(doc_topics.shape, BF16),
            jax.ShapeDtypeStruct(word_logits.shape, BF16),
            jax.ShapeDtypeStruct(log_norm.shape, F32),
        ],
        in_specs=[HBM, HBM, HBM],
        out_specs=[VMEM] * 4,
        scratch_shapes=[
            pltpu.VMEM(word_logits.shape, BF16),
            pltpu.VMEM((words, docs), F32),
            pltpu.SemaphoreType.DMA((2, steps)),
            pltpu.SemaphoreType.DMA,
        ],
        compiler_params=call_params(16),
        cost_estimate=cost(2 * words * docs * width, 2 * (words + docs) * width, words * width),
        name="rate_partial",
    )(in_hbm(doc_topics), in_hbm(word_logits), in_hbm(log_norm))


def chunk_counts(word_counts, tile_doc, tile_word, place, n_topic, docs, words):
    slots, word_tile, doc_tile = word_counts.shape
    chunk = words // n_topic

    def kernel(place_ref, doc_at, word_at, count_ref, out_ref):
        first = place_ref[0] * chunk
        block = first // word_tile
        row = pl.multiple_of(lax.rem(first, word_tile), chunk)
        out_ref[...] = jnp.zeros_like(out_ref)
        for s in range(slots):
            @pl.when(word_at[s] == block)
            def _():
                column = first_row(doc_at[s], doc_tile)
                out_ref[:, pl.ds(column, doc_tile)] = count_ref[s, pl.ds(row, chunk), :].astype(F32)

    return pl.pallas_call(
        kernel,
        out_shape=jax.ShapeDtypeStruct((chunk, docs), F32),
        in_specs=[SMEM, SMEM, SMEM, VMEM],
        out_specs=VMEM,
        compiler_params=call_params(),
        cost_estimate=cost(words * docs, 4 * words * docs),
        name="chunk_counts",
    )(place, tile_doc, tile_word, word_counts)


def ratio_chunk(parts, counts, word_tile):
    n_topic = parts.shape[0]

    def kernel(part_ref, count_ref, out_ref):
        rate = part_ref[0].astype(F32)
        for s in range(1, n_topic):
            rate += part_ref[s].astype(F32)
        ratio = (count_ref[...] / (word_tile * rate)).astype(BF16)
        for s in range(n_topic):
            out_ref[s] = ratio

    return pl.pallas_call(
        kernel,
        out_shape=jax.ShapeDtypeStruct(parts.shape, BF16),
        compiler_params=call_params(),
        cost_estimate=cost(10 * counts.size, 4 * parts.size),
        name="ratio_chunk",
    )(parts, counts)


def beta_piece(ratio, docs_held, prob_held, side, piece, pieces, after):
    docs, width = docs_held.shape
    words = prob_held.shape[0]
    span = width // pieces
    half = words // 2

    def kernel(side_ref, ratio_ref, doc_ref, prob_ref, *rest):
        keep_ref, send_ref = rest[-2:]
        for out_ref, which in ((send_ref, 1 - side_ref[0]), (keep_ref, side_ref[0])):
            rows = pl.ds(first_row(which, half), half)
            summed = jnp.dot(ratio_ref[rows, :], doc_ref[...], preferred_element_type=F32)
            out_ref[...] = (-prob_ref[rows, :].astype(F32) * summed).astype(BF16)

    return pl.pallas_call(
        kernel,
        out_shape=[jax.ShapeDtypeStruct((half, span), BF16)] * 2,
        grid=(1,),
        in_specs=[
            SMEM,
            pl.BlockSpec((words, docs), lambda j: (0, 0)),
            pl.BlockSpec((docs, span), lambda j: (0, piece)),
            pl.BlockSpec((words, span), lambda j: (0, piece)),
        ]
        + [ANY] * len(after),
        out_specs=[pl.BlockSpec((half, span), lambda j: (0, 0))] * 2,
        compiler_params=call_params(),
        cost_estimate=cost(2 * words * docs * span, 2 * (2 * words + docs) * span),
        name="beta_piece",
    )(side, ratio, docs_held, prob_held, *after)


def add_pair(own, other, after=()):
    def kernel(own_ref, other_ref, *rest):
        rest[-1][...] = (own_ref[...].astype(F32) + other_ref[...].astype(F32)).astype(BF16)

    return pl.pallas_call(
        kernel,
        out_shape=jax.ShapeDtypeStruct(own.shape, BF16),
        in_specs=[VMEM, VMEM] + [ANY] * len(after),
        out_specs=VMEM,
        compiler_params=call_params(),
        cost_estimate=cost(own.size, 6 * own.size),
        name="add_pair",
    )(own, other, *after)


def theta_grad(ratio, far_ratios, prob_held, far_logits, log_norm, vocab_at, side):
    words, docs = ratio.shape
    half = words // 2
    share = far_logits[0].shape[1]
    far = len(far_ratios)
    count = far + 1
    span = min(share, 512)

    def kernel(vocab_ref, side_ref, ratio_ref, *refs):
        far_refs, prob_ref = refs[:far], refs[far]
        logit_refs, norm_ref = refs[far + 1 : 3 * far + 1], refs[3 * far + 1]
        out_ref, done_ref, turned = refs[-3:]
        done_ref[...] = jnp.zeros_like(done_ref)

        @pl.when(pl.program_id(0) == 0)
        def _():
            def put(rows, at):
                turned[:, at : at + rows.shape[0]] = (-rows.astype(F32)).T.astype(BF16)

            put(ratio_ref[...], 0)
            for l in range(far):
                for h in range(2):
                    which = side_ref[0] if h == 0 else 1 - side_ref[0]
                    put(far_refs[l][pl.ds(first_row(which, half), half), :], (l + 1) * words + h * half)

        prob = jnp.concatenate(
            [prob_ref[...]] + [jnp.exp(ref[...].astype(F32) - norm_ref[...]).astype(BF16) for ref in logit_refs],
            axis=0,
        )
        out_ref[...] = jnp.dot(turned[...], prob, preferred_element_type=F32)

    blocks = share // span
    return pl.pallas_call(
        kernel,
        out_shape=[jax.ShapeDtypeStruct((docs, share), F32), jax.ShapeDtypeStruct((8, 128), F32)],
        grid_spec=pltpu.PrefetchScalarGridSpec(
            num_scalar_prefetch=2,
            grid=(blocks,),
            in_specs=[pl.BlockSpec((words, docs), lambda j, v, s: (0, 0))] * count
            + [pl.BlockSpec((words, span), lambda j, v, s: (0, v[0] * blocks + j))]
            + [pl.BlockSpec((half, span), lambda j, v, s: (0, j))] * (2 * far)
            + [pl.BlockSpec((1, span), lambda j, v, s: (0, v[0] * blocks + j))],
            out_specs=[
                pl.BlockSpec((docs, span), lambda j, v, s: (0, j)),
                pl.BlockSpec((8, 128), lambda j, v, s: (0, 0)),
            ],
            scratch_shapes=[pltpu.VMEM((docs, count * words), BF16)],
        ),
        compiler_params=call_params(16),
        cost_estimate=cost(
            2 * count * words * docs * share, (4 * docs + 2 * count * words) * share, count * words * share
        ),
        name="theta_grad",
    )(vocab_at, side, ratio, *far_ratios, prob_held, *far_logits, log_norm)


def place_pieces(own, other, side):
    pieces = len(own)
    half, span = own[0].shape

    def kernel(side_ref, *refs):
        out_ref, sems = refs[-2:]
        copies = []
        for p in range(pieces):
            for h, which in ((0, side_ref[0]), (1, 1 - side_ref[0])):
                target = out_ref.at[pl.ds(first_row(which, half), half), pl.ds(p * span, span)]
                copies.append(pltpu.make_async_copy(refs[h * pieces + p], target, sems.at[h, p]))
        for copy in copies:
            copy.start()
        for copy in copies:
            copy.wait()

    return pl.pallas_call(
        kernel,
        out_shape=jax.ShapeDtypeStruct((2 * half, span * pieces), BF16),
        in_specs=[SMEM] + [VMEM] * (2 * pieces),
        out_specs=HBM,
        scratch_shapes=[pltpu.SemaphoreType.DMA((2, pieces))],
        compiler_params=call_params(),
        cost_estimate=cost(0, 8 * half * span * pieces),
        name="place_pieces",
    )(side, *own, *other)


def on_device(sizes, doc_topics, word_logits, log_norm, tile_doc, tile_word, word_counts):
    n_doc, n_topic, n_vocab = sizes
    docs, width = doc_topics.shape
    words = word_logits.shape[0]
    word_tile = word_counts.shape[1]
    norm = log_norm[None, :]
    place = lax.axis_index("topic").astype(jnp.int32)[None]
    vocab_at = lax.axis_index("vocab").astype(jnp.int32)
    side = lax.rem(lax.axis_index("doc").astype(jnp.int32), 2)

    def shift(array, axis, count, by):
        return lax.ppermute(array, axis, [(i, (i + by) % count) for i in range(count)])

    def swap(array, bit):
        return lax.ppermute(array, "doc", [(i, i ^ bit) for i in range(n_doc)])

    share = width // n_vocab
    half = words // 2
    far_logits = []
    for s in range(1, n_vocab):
        target = lax.rem(vocab_at + s, n_vocab)
        near_half = shift(
            lax.dynamic_slice(word_logits, (side * half, target * share), (half, share)), "vocab", n_vocab, s
        )
        far_logits += [near_half, swap(near_half, 1)]

    parts, docs_held, prob_held, norm_held = rate_partial(doc_topics, word_logits, norm, n_topic)
    parts = lax.all_to_all(parts, "topic", 0, 0)
    counts = chunk_counts(word_counts, tile_doc, tile_word, place, n_topic, docs, words)
    chunks = lax.all_to_all(ratio_chunk(parts, counts, word_tile), "topic", 0, 0)
    ratio = chunks.reshape(words, docs)
    far_ratios = [shift(ratio, "vocab", n_vocab, s) for s in range(1, n_vocab)]
    theta, theta_done = theta_grad(ratio, far_ratios, prob_held, far_logits, norm_held, vocab_at[None], side[None])

    pieces = 4
    halves, sums = [], []
    for p in range(pieces):
        after = [sums[p - 2]] if p >= 2 else []
        keep, send = beta_piece(ratio, docs_held, prob_held, side[None], p, pieces, after)
        halves.append((keep, swap(send, 1)))
        if p >= 1:
            sums.append(add_pair(*halves[p - 1]))
    sums.append(add_pair(*halves[-1]))
    bit = 2
    while bit < n_doc:
        sums = [add_pair(part, swap(part, bit), [theta_done] if p == 2 else []) for p, part in enumerate(sums)]
        bit *= 2
    out = place_pieces(sums, [swap(part, 1) for part in sums], side[None])
    return theta, out


def solution(mesh):
    placed = (
        P("doc", "topic"),
        P("vocab", "topic"),
        P("topic"),
        P(("doc", "vocab")),
        P(("doc", "vocab")),
        P(("doc", "vocab"), None, None),
    )
    sizes = (mesh.shape["doc"], mesh.shape["topic"], mesh.shape["vocab"])
    return jax.shard_map(
        functools.partial(on_device, sizes),
        mesh=mesh,
        in_specs=placed,
        out_specs=(P("doc", ("topic", "vocab")), P("vocab", "topic")),
        check_vma=False,
    )
```

```python
import functools

import jax
import jax.numpy as jnp
from jax import lax
from jax.experimental import pallas as pl
from jax.experimental.pallas import tpu as pltpu
from jax.sharding import PartitionSpec as P

BF16 = jnp.bfloat16
F32 = jnp.float32
MIB = 1024 * 1024
ANY = pl.BlockSpec(memory_space=pl.ANY)
HBM = pl.BlockSpec(memory_space=pltpu.HBM)
VMEM = pl.BlockSpec(memory_space=pltpu.VMEM)
SMEM = pl.BlockSpec(memory_space=pltpu.SMEM)


def call_params(mib=8):
    return pltpu.CompilerParams(vmem_limit_bytes=mib * MIB)


def cost(flops, bytes_accessed, transcendentals=0):
    return pl.CostEstimate(flops=flops, bytes_accessed=bytes_accessed, transcendentals=transcendentals)


def in_hbm(array):
    return pltpu.with_memory_space_constraint(array, pltpu.HBM)


def first_row(index, rows):
    return pl.multiple_of(index * rows, rows)


def fetch(doc_topics, word_logits, log_norm, vocab_at, side, n_vocab, early, plain):
    docs, width = doc_topics.shape
    half, share = word_logits.shape[0] // 2, width // n_vocab
    far = n_vocab - 1
    widths = [w for w in (early, plain) if w]

    def kernel(vocab_ref, side_ref, doc_in, logit_in, norm_in, *rest):
        outs, sems = rest[:-1], rest[-1]
        sources = []
        if early:
            sources.append(doc_in.at[:, pl.ds(first_row(vocab_ref[0], early), early)])
        if plain:
            sources.append(doc_in.at[:, pl.ds(early * n_vocab, plain)])
        for s in range(1, n_vocab):
            target = lax.rem(vocab_ref[0] + s, n_vocab)
            rows, columns = pl.ds(first_row(side_ref[0], half), half), pl.ds(first_row(target, share), share)
            sources.append(logit_in.at[rows, columns])
        sources.append(norm_in)
        copies = [pltpu.make_async_copy(source, out, sems.at[i]) for i, (source, out) in enumerate(zip(sources, outs))]
        for copy in copies:
            copy.start()
        for copy in copies:
            copy.wait()

    count = len(widths) + far + 1
    out = pl.pallas_call(
        kernel,
        out_shape=[jax.ShapeDtypeStruct((docs, w), BF16) for w in widths]
        + [jax.ShapeDtypeStruct((half, share), BF16)] * far
        + [jax.ShapeDtypeStruct(log_norm.shape, F32)],
        in_specs=[SMEM, SMEM, HBM, HBM, HBM],
        out_specs=[VMEM] * count,
        scratch_shapes=[pltpu.SemaphoreType.DMA((count,))],
        compiler_params=call_params(),
        cost_estimate=cost(0, 4 * docs * sum(widths) + 4 * half * share * far),
        name="fetch",
    )(vocab_at, side, in_hbm(doc_topics), in_hbm(word_logits), in_hbm(log_norm))
    return out[: len(widths)], out[len(widths) : -1], out[-1]


def rate_partial(doc_topics, word_logits, log_norm, bit):
    docs, width = doc_topics.shape
    words = word_logits.shape[0]
    span = min(width, 1024)
    steps = width // span
    half = words // 2

    def kernel(bit_ref, doc_in, logit_in, norm_ref, keep_ref, send_ref, doc_ref, prob_ref, logit_ref, acc, sems):
        copies = []
        for j in range(steps):
            at = pl.ds(j * span, span)
            copies.append(
                (
                    pltpu.make_async_copy(logit_in.at[:, at], logit_ref.at[:, at], sems.at[0, j]),
                    pltpu.make_async_copy(doc_in.at[:, at], doc_ref.at[:, at], sems.at[1, j]),
                )
            )
        for pair in copies:
            for copy in pair:
                copy.start()
        for j in range(steps):
            at = pl.ds(j * span, span)
            copies[j][0].wait()
            prob = jnp.exp(logit_ref[:, at].astype(F32) - norm_ref[:, at]).astype(BF16)
            prob_ref[:, at] = prob
            copies[j][1].wait()
            part = lax.dot_general(
                prob, doc_ref[:, at], (((1,), (1,)), ((), ())), preferred_element_type=F32
            )
            if j == 0:
                acc[...] = part
            else:
                acc[...] += part
        send_ref[...] = acc[pl.ds(first_row(1 - bit_ref[0], half), half), :].astype(BF16)
        keep_ref[...] = acc[pl.ds(first_row(bit_ref[0], half), half), :]

    return pl.pallas_call(
        kernel,
        out_shape=[
            jax.ShapeDtypeStruct((half, docs), F32),
            jax.ShapeDtypeStruct((half, docs), BF16),
            jax.ShapeDtypeStruct(doc_topics.shape, BF16),
            jax.ShapeDtypeStruct(word_logits.shape, BF16),
        ],
        in_specs=[SMEM, HBM, HBM, VMEM],
        out_specs=[VMEM] * 4,
        scratch_shapes=[
            pltpu.VMEM(word_logits.shape, BF16),
            pltpu.VMEM((words, docs), F32),
            pltpu.SemaphoreType.DMA((2, steps)),
        ],
        compiler_params=call_params(16),
        cost_estimate=cost(2 * words * docs * width, 2 * (words + docs) * width, words * width),
        name="rate_partial",
    )(bit, in_hbm(doc_topics), in_hbm(word_logits), log_norm)


def fold_rates(own, other, bit):
    rows, docs = own.shape
    half = rows // 2

    def kernel(bit_ref, own_ref, other_ref, keep_ref, send_ref):
        for which, out_ref in ((1 - bit_ref[0], send_ref), (bit_ref[0], keep_ref)):
            at = pl.ds(first_row(which, half), half)
            out_ref[...] = (own_ref[at, :] + other_ref[at, :].astype(F32)).astype(out_ref.dtype)

    return pl.pallas_call(
        kernel,
        out_shape=[jax.ShapeDtypeStruct((half, docs), F32), jax.ShapeDtypeStruct((half, docs), BF16)],
        in_specs=[SMEM, VMEM, VMEM],
        out_specs=[VMEM, VMEM],
        compiler_params=call_params(),
        cost_estimate=cost(own.size, 8 * own.size),
        name="fold_rates",
    )(bit, own, other)


def chunk_counts(word_counts, tile_doc, tile_word, place, n_topic, docs, words):
    slots, word_tile, doc_tile = word_counts.shape
    chunk = words // n_topic

    def kernel(place_ref, doc_at, word_at, count_ref, out_ref):
        first = place_ref[0] * chunk
        block = first // word_tile
        row = pl.multiple_of(lax.rem(first, word_tile), chunk)
        out_ref[...] = jnp.zeros_like(out_ref)
        for s in range(slots):
            @pl.when(word_at[s] == block)
            def _():
                column = first_row(doc_at[s], doc_tile)
                out_ref[:, pl.ds(column, doc_tile)] = count_ref[s, pl.ds(row, chunk), :].astype(F32)

    return pl.pallas_call(
        kernel,
        out_shape=jax.ShapeDtypeStruct((chunk, docs), F32),
        in_specs=[SMEM, SMEM, SMEM, VMEM],
        out_specs=VMEM,
        compiler_params=call_params(),
        cost_estimate=cost(words * docs, 4 * words * docs),
        name="chunk_counts",
    )(place, tile_doc, tile_word, word_counts)


def ratio_chunk(own, other, counts, word_tile):
    def kernel(own_ref, other_ref, count_ref, out_ref):
        rate = own_ref[...] + other_ref[...].astype(F32)
        out_ref[...] = (count_ref[...] / (word_tile * rate)).astype(BF16)

    return pl.pallas_call(
        kernel,
        out_shape=jax.ShapeDtypeStruct(counts.shape, BF16),
        in_specs=[VMEM] * 3,
        out_specs=VMEM,
        compiler_params=call_params(),
        cost_estimate=cost(10 * counts.size, 12 * counts.size),
        name="ratio_chunk",
    )(own, other, counts)


def join_rows(own, other, bit, after=()):
    rows, docs = own.shape

    def kernel(bit_ref, own_ref, other_ref, *rest):
        out_ref = rest[-1]
        out_ref[pl.ds(first_row(bit_ref[0], rows), rows), :] = own_ref[...]
        out_ref[pl.ds(first_row(1 - bit_ref[0], rows), rows), :] = other_ref[...]

    return pl.pallas_call(
        kernel,
        out_shape=jax.ShapeDtypeStruct((2 * rows, docs), BF16),
        in_specs=[SMEM, VMEM, VMEM] + [ANY] * len(after),
        out_specs=VMEM,
        compiler_params=call_params(),
        cost_estimate=cost(0, 8 * own.size),
        name="join_rows",
    )(bit, own, other, *after)


def hold(array, after):
    def kernel(in_ref, *rest):
        rest[-1][...] = in_ref[...]

    return pl.pallas_call(
        kernel,
        out_shape=jax.ShapeDtypeStruct(array.shape, array.dtype),
        in_specs=[VMEM] + [ANY] * len(after),
        out_specs=VMEM,
        compiler_params=call_params(),
        cost_estimate=cost(0, 4 * array.size),
        name="hold",
    )(array, *after)


def beta_piece(ratios, docs_held, far_docs, prob_held, side, column, span, after=()):
    docs = docs_held.shape[0]
    words = prob_held.shape[0]
    half = words // 2
    count = len(ratios)

    def kernel(column_ref, side_ref, *refs):
        ratio_refs, doc_ref, prob_ref, far_refs = refs[:count], refs[count], refs[count + 1], refs[count + 2 :]
        keep_ref, send_ref = refs[-2:]
        at = pl.ds(pl.multiple_of(column_ref[0], 128), span)
        for out_ref, which in ((send_ref, 1 - side_ref[0]), (keep_ref, side_ref[0])):
            rows = pl.ds(first_row(which, half), half)
            summed = jnp.dot(ratio_refs[0][rows, :], doc_ref[:, at], preferred_element_type=F32)
            if count > 1:
                summed += jnp.dot(ratio_refs[1][rows, :], far_refs[0][...], preferred_element_type=F32)
            out_ref[...] = (-prob_ref[rows, at].astype(F32) * summed).astype(BF16)

    return pl.pallas_call(
        kernel,
        out_shape=[jax.ShapeDtypeStruct((half, span), BF16)] * 2,
        in_specs=[SMEM, SMEM] + [VMEM] * (count + 2 + len(far_docs)) + [ANY] * len(after),
        out_specs=[VMEM, VMEM],
        compiler_params=call_params(16),
        cost_estimate=cost(2 * count * words * docs * span, 2 * (2 * words + count * docs) * span),
        name="beta_piece",
    )(column, side, *ratios, docs_held, prob_held, *far_docs, *after)


def add_pair(own, other, after=()):
    def kernel(own_ref, other_ref, *rest):
        rest[-1][...] = (own_ref[...].astype(F32) + other_ref[...].astype(F32)).astype(BF16)

    return pl.pallas_call(
        kernel,
        out_shape=jax.ShapeDtypeStruct(own.shape, BF16),
        in_specs=[VMEM, VMEM] + [ANY] * len(after),
        out_specs=VMEM,
        compiler_params=call_params(),
        cost_estimate=cost(own.size, 6 * own.size),
        name="add_pair",
    )(own, other, *after)


def theta_grad(ratio, far_ratios, prob_held, far_logits, log_norm, vocab_at, side, after):
    words, docs = ratio.shape
    half = words // 2
    share = far_logits[0].shape[1]
    far = len(far_ratios)
    count = far + 1
    span = min(share, 512)

    def kernel(vocab_ref, side_ref, ratio_ref, *refs):
        far_refs, prob_ref = refs[:far], refs[far]
        logit_refs, norm_ref = refs[far + 1 : 3 * far + 1], refs[3 * far + 1]
        out_ref, done_ref, turned = refs[-3:]
        done_ref[...] = jnp.zeros_like(done_ref)

        @pl.when(pl.program_id(0) == 0)
        def _():
            def put(rows, at):
                turned[:, at : at + rows.shape[0]] = (-rows.astype(F32)).T.astype(BF16)

            put(ratio_ref[...], 0)
            for l in range(far):
                for h in range(2):
                    which = side_ref[0] if h == 0 else 1 - side_ref[0]
                    put(far_refs[l][pl.ds(first_row(which, half), half), :], (l + 1) * words + h * half)

        prob = jnp.concatenate(
            [prob_ref[...]] + [jnp.exp(ref[...].astype(F32) - norm_ref[...]).astype(BF16) for ref in logit_refs],
            axis=0,
        )
        out_ref[...] = jnp.dot(turned[...], prob, preferred_element_type=F32)

    blocks = share // span
    return pl.pallas_call(
        kernel,
        out_shape=[jax.ShapeDtypeStruct((docs, share), F32), jax.ShapeDtypeStruct((8, 128), F32)],
        grid_spec=pltpu.PrefetchScalarGridSpec(
            num_scalar_prefetch=2,
            grid=(blocks,),
            in_specs=[pl.BlockSpec((words, docs), lambda j, v, s: (0, 0))] * count
            + [pl.BlockSpec((words, span), lambda j, v, s: (0, v[0] * blocks + j))]
            + [pl.BlockSpec((half, span), lambda j, v, s: (0, j))] * (2 * far)
            + [pl.BlockSpec((1, span), lambda j, v, s: (0, v[0] * blocks + j))]
            + [ANY] * len(after),
            out_specs=[
                pl.BlockSpec((docs, span), lambda j, v, s: (0, j)),
                pl.BlockSpec((8, 128), lambda j, v, s: (0, 0)),
            ],
            scratch_shapes=[pltpu.VMEM((docs, count * words), BF16)],
        ),
        compiler_params=call_params(16),
        cost_estimate=cost(
            2 * count * words * docs * share, (4 * docs + 2 * count * words) * share, count * words * share
        ),
        name="theta_grad",
    )(vocab_at, side, ratio, *far_ratios, prob_held, *far_logits, log_norm, *after)


def place_pieces(own, other, starts, side, shape):
    pieces = len(own)
    half = own[0].shape[0]

    def kernel(side_ref, *refs):
        start_refs, own_refs, other_refs = (refs[i * pieces : (i + 1) * pieces] for i in range(3))
        out_ref, sems = refs[-2:]
        copies = []
        for p in range(pieces):
            span = own_refs[p].shape[1]
            columns = pl.ds(pl.multiple_of(start_refs[p][0], 128), span)
            for h, (ref, which) in enumerate(((own_refs[p], side_ref[0]), (other_refs[p], 1 - side_ref[0]))):
                target = out_ref.at[pl.ds(first_row(which, half), half), columns]
                copies.append(pltpu.make_async_copy(ref, target, sems.at[h, p]))
        for copy in copies:
            copy.start()
        for copy in copies:
            copy.wait()

    return pl.pallas_call(
        kernel,
        out_shape=jax.ShapeDtypeStruct(shape, BF16),
        in_specs=[SMEM] * (1 + pieces) + [VMEM] * (2 * pieces),
        out_specs=HBM,
        scratch_shapes=[pltpu.SemaphoreType.DMA((2, pieces))],
        compiler_params=call_params(),
        cost_estimate=cost(0, 4 * shape[0] * shape[1]),
        name="place_pieces",
    )(side, *starts, *own, *other)


def on_device(sizes, doc_topics, word_logits, log_norm, tile_doc, tile_word, word_counts):
    n_doc, n_topic, n_vocab = sizes
    docs, width = doc_topics.shape
    words = word_logits.shape[0]
    word_tile = word_counts.shape[1]
    topic_at = lax.axis_index("topic").astype(jnp.int32)
    vocab_at = lax.axis_index("vocab").astype(jnp.int32)[None]
    side = lax.rem(lax.axis_index("doc").astype(jnp.int32), 2)[None]
    levels = n_topic.bit_length() - 1
    assert n_topic == 1 << levels and levels > 0
    bits = [lax.rem(lax.div(topic_at, jnp.int32(1 << b)), 2)[None] for b in range(levels)]
    place = sum(bits[b] << (levels - 1 - b) for b in range(levels))

    def shift(array, by):
        return lax.ppermute(array, "vocab", [(i, (i + by) % n_vocab) for i in range(n_vocab)])

    def swap(array, bit):
        return lax.ppermute(array, "doc", [(i, i ^ bit) for i in range(n_doc)])

    def swap_topic(array, level):
        return lax.ppermute(array, "topic", [(i, i ^ (1 << level)) for i in range(n_topic)])

    early, plain = width * 3 // 8 // n_vocab // 128 * 128, width // 16 // 128 * 128
    if n_doc != 4:
        early = plain = 0
    near_docs, near_logits, norm = fetch(
        doc_topics, word_logits, log_norm[None, :], vocab_at, side, n_vocab, early, plain
    )
    passed = [swap(part, 2) for part in near_docs]
    far_logits = []
    for s in range(1, n_vocab):
        part = shift(near_logits[s - 1], s)
        far_logits += [part, swap(part, 1)]

    keep, send, docs_held, prob_held = rate_partial(doc_topics, word_logits, norm, bits[0])
    for level in range(1, levels):
        keep, send = fold_rates(keep, swap_topic(send, level - 1), bits[level])
    counts = chunk_counts(word_counts, tile_doc, tile_word, place, n_topic, docs, words)
    own_ratio = ratio_chunk(keep, swap_topic(send, levels - 1), counts, word_tile)

    def gather(chunk, after=()):
        for level in reversed(range(levels)):
            chunk = join_rows(chunk, swap_topic(chunk, level), bits[level], () if level else after)
        return chunk

    ratio = gather(own_ratio, passed[1:])
    far_ratios = [shift(ratio, s) for s in range(1, n_vocab)]

    begin = early * n_vocab + plain
    pieces = 2 if begin else 4
    span = (width - begin) // pieces
    starts = [jnp.full((1,), begin + p * span, jnp.int32) for p in range(pieces)]
    halves, sums = [], []
    for p in range(pieces):
        after = [sums[p - 2]] if p >= 2 else []
        keep, send = beta_piece([ratio], docs_held, [], prob_held, side, starts[p], span, after)
        halves.append((keep, swap(send, 1)))
        if p >= 1:
            sums.append(add_pair(*halves[p - 1]))
    sums.append(add_pair(*halves[-1]))

    near_sums = []
    if begin:
        far_ratio = gather(hold(swap(own_ratio, 2), [sums[-1]]))
        groups = []
        if plain:
            groups.append((jnp.full((1,), early * n_vocab, jnp.int32), passed[-1]))
        if early:
            groups.append((vocab_at * early, passed[0]))
            ready = hold(passed[0], [own_ratio])
            for s in range(1, n_vocab):
                groups.append((lax.rem(vocab_at + n_vocab - s, n_vocab) * early, shift(ready, s)))
        for start, part in groups:
            keep, send = beta_piece([ratio, far_ratio], docs_held, [part], prob_held, side, start, part.shape[1])
            near_sums.append(add_pair(keep, swap(send, 1)))
            starts.append(start)
    theta, theta_done = theta_grad(
        ratio, far_ratios, prob_held, far_logits, norm, vocab_at, side, near_sums[: len(passed)]
    )
    bit = 2
    while bit < n_doc:
        sums = [
            add_pair(part, swap(part, bit), [theta_done] if p == pieces - 1 else []) for p, part in enumerate(sums)
        ]
        bit *= 2
    sums += near_sums
    out = place_pieces(sums, [swap(part, 1) for part in sums], starts, side, word_logits.shape)
    return theta, out


def solution(mesh):
    placed = (
        P("doc", "topic"),
        P("vocab", "topic"),
        P("topic"),
        P(("doc", "vocab")),
        P(("doc", "vocab")),
        P(("doc", "vocab"), None, None),
    )
    sizes = (mesh.shape["doc"], mesh.shape["topic"], mesh.shape["vocab"])
    return jax.shard_map(
        functools.partial(on_device, sizes),
        mesh=mesh,
        in_specs=placed,
        out_specs=(P("doc", ("topic", "vocab")), P("vocab", "topic")),
        check_vma=False,
    )
```

```python
import functools

import jax
import jax.numpy as jnp
from jax import lax
from jax.experimental import pallas as pl
from jax.experimental.pallas import tpu as pltpu
from jax.sharding import PartitionSpec as P

BF16 = jnp.bfloat16
F32 = jnp.float32
MIB = 1024 * 1024
ANY = pl.BlockSpec(memory_space=pl.ANY)
HBM = pl.BlockSpec(memory_space=pltpu.HBM)
VMEM = pl.BlockSpec(memory_space=pltpu.VMEM)
SMEM = pl.BlockSpec(memory_space=pltpu.SMEM)


def call_params(mib=16):
    return pltpu.CompilerParams(vmem_limit_bytes=mib * MIB)


def cost(flops, bytes_accessed, transcendentals=0):
    return pl.CostEstimate(flops=flops, bytes_accessed=bytes_accessed, transcendentals=transcendentals)


def in_hbm(array):
    return pltpu.with_memory_space_constraint(array, pltpu.HBM)


def window(index, size):
    return pl.ds(pl.multiple_of(index * size, size), size)


class Sizes:
    def __init__(self, mesh):
        self.doc, self.topic, self.vocab = (mesh.shape[axis] for axis in ("doc", "topic", "vocab"))

    def vocab_at(self, here_ref):
        return lax.rem(here_ref[0], self.vocab)

    def topic_at(self, here_ref):
        return lax.rem(lax.div(here_ref[0], self.vocab), self.topic)

    def side(self, here_ref):
        return lax.rem(lax.div(here_ref[0], self.vocab * self.topic), 2)


def rate_partial(sizes, here, doc_topics, word_logits, log_norm):
    docs, width = doc_topics.shape
    words = word_logits.shape[0]
    side_width = width // 2
    span = min(side_width, 1024)
    steps = side_width // span
    count, far = sizes.topic, sizes.vocab - 1
    chunk, half, share = words // count, words // 2, width // sizes.vocab

    def kernel(here_ref, doc_in, logit_in, norm_in, *rest):
        parts, halves = rest[:count], rest[count : count + far]
        own_ref, sibling_ref, prob_ref, norm_ref, logit_ref, acc, sems, norm_sem = rest[count + far :]
        side = sizes.side(here_ref)
        norm_copy = pltpu.make_async_copy(norm_in, norm_ref, norm_sem)
        norm_copy.start()
        blocks = []
        for which, doc_ref in ((1 - side, sibling_ref), (side, own_ref)):
            for j in range(steps):
                at = window(which * steps + j, span)
                i = len(blocks)
                logit_copy = pltpu.make_async_copy(logit_in.at[:, at], logit_ref.at[:, at], sems.at[0, i])
                held = doc_ref.at[:, pl.ds(j * span, span)]
                doc_copy = pltpu.make_async_copy(doc_in.at[:, at], held, sems.at[1, i])
                blocks.append((at, logit_copy, doc_copy, held))
        for _, logit_copy, doc_copy, _ in blocks:
            logit_copy.start()
            doc_copy.start()
        norm_copy.wait()
        for i, (at, logit_copy, doc_copy, held) in enumerate(blocks):
            logit_copy.wait()
            prob = jnp.exp(logit_ref[:, at].astype(F32) - norm_ref[:, at]).astype(BF16)
            prob_ref[:, at] = prob
            doc_copy.wait()
            part = lax.dot_general(
                prob, held[...], (((1,), (1,)), ((), ())), preferred_element_type=F32
            )
            if i == 0:
                acc[...] = part
            else:
                acc[...] += part
        topic_at = sizes.topic_at(here_ref)
        for s in range(count):
            parts[s][...] = acc[window(topic_at ^ s, chunk), :].astype(BF16)
        rows = window(side, half)
        for s in range(far):
            target = lax.rem(sizes.vocab_at(here_ref) + s + 1, sizes.vocab)
            halves[s][...] = logit_ref[rows, window(target, share)]

    out = pl.pallas_call(
        kernel,
        out_shape=[jax.ShapeDtypeStruct((chunk, docs), BF16)] * count
        + [jax.ShapeDtypeStruct((half, share), BF16)] * far
        + [
            jax.ShapeDtypeStruct((docs, side_width), BF16),
            jax.ShapeDtypeStruct((docs, side_width), BF16),
            jax.ShapeDtypeStruct(word_logits.shape, BF16),
            jax.ShapeDtypeStruct(log_norm.shape, F32),
        ],
        in_specs=[SMEM, HBM, HBM, HBM],
        out_specs=[VMEM] * (count + far + 4),
        scratch_shapes=[
            pltpu.VMEM(word_logits.shape, BF16),
            pltpu.VMEM((words, docs), F32),
            pltpu.SemaphoreType.DMA((2, 2 * steps)),
            pltpu.SemaphoreType.DMA,
        ],
        compiler_params=call_params(),
        cost_estimate=cost(2 * words * docs * width, 2 * (words + docs) * width, words * width),
        name="rate_partial",
    )(here, in_hbm(doc_topics), in_hbm(word_logits), in_hbm(log_norm))
    return out[:count], out[count : count + far], *out[count + far :]


def chunk_counts(sizes, here, word_counts, tile_doc, tile_word, docs, words):
    slots, word_tile, doc_tile = word_counts.shape
    chunk = words // sizes.topic

    def kernel(here_ref, doc_at, word_at, count_in, out_ref, held, sem):
        copy = pltpu.make_async_copy(count_in, held, sem)
        copy.start()
        first = sizes.topic_at(here_ref) * chunk
        block = first // word_tile
        row = pl.multiple_of(lax.rem(first, word_tile), chunk)
        out_ref[...] = jnp.zeros_like(out_ref)
        copy.wait()
        for s in range(slots):
            @pl.when(word_at[s] == block)
            def _():
                out_ref[:, window(doc_at[s], doc_tile)] = held[s, pl.ds(row, chunk), :].astype(F32)

    return pl.pallas_call(
        kernel,
        out_shape=jax.ShapeDtypeStruct((chunk, docs), F32),
        in_specs=[SMEM, SMEM, SMEM, HBM],
        out_specs=VMEM,
        scratch_shapes=[pltpu.VMEM(word_counts.shape, jnp.int32), pltpu.SemaphoreType.DMA],
        compiler_params=call_params(),
        cost_estimate=cost(words * docs, 4 * words * docs),
        name="chunk_counts",
    )(here, in_hbm(tile_doc), in_hbm(tile_word), in_hbm(word_counts))


def ratio_chunk(parts, counts, word_tile):
    def kernel(*refs):
        part_refs, count_ref, out_ref = refs[:-2], refs[-2], refs[-1]
        rate = part_refs[0][...].astype(F32)
        for ref in part_refs[1:]:
            rate += ref[...].astype(F32)
        out_ref[...] = (count_ref[...] / (word_tile * rate)).astype(BF16)

    return pl.pallas_call(
        kernel,
        out_shape=jax.ShapeDtypeStruct(counts.shape, BF16),
        in_specs=[VMEM] * (len(parts) + 1),
        out_specs=VMEM,
        compiler_params=call_params(),
        cost_estimate=cost(10 * counts.size, 16 * counts.size),
        name="ratio_chunk",
    )(*parts, counts)


def join_ratio(sizes, here, chunks, after):
    rows, docs = chunks[0].shape
    count = sizes.topic

    def kernel(here_ref, *refs):
        topic_at = sizes.topic_at(here_ref)
        for s in range(count):
            refs[-1][window(topic_at ^ s, rows), :] = refs[s][...]

    return pl.pallas_call(
        kernel,
        out_shape=jax.ShapeDtypeStruct((rows * count, docs), BF16),
        in_specs=[SMEM] + [VMEM] * count + [ANY] * len(after),
        out_specs=VMEM,
        compiler_params=call_params(),
        cost_estimate=cost(0, 4 * rows * docs * count),
        name="join_ratio",
    )(here, *chunks, *after)


def own_product(ratio, docs_held):
    words, docs = ratio.shape
    width = docs_held.shape[1]

    def kernel(ratio_ref, doc_ref, out_ref):
        out_ref[...] = jnp.dot(ratio_ref[...], doc_ref[...], preferred_element_type=F32)

    return pl.pallas_call(
        kernel,
        out_shape=jax.ShapeDtypeStruct((words, width), F32),
        in_specs=[VMEM, VMEM],
        out_specs=VMEM,
        compiler_params=call_params(),
        cost_estimate=cost(2 * words * docs * width, 2 * docs * width + 4 * words * width),
        name="own_product",
    )(ratio, docs_held)


def beta_piece(sizes, here, product, ratio, docs_held, prob_held, start, spans, after):
    words, side_width = product.shape
    docs, width = docs_held.shape[0], sum(spans)

    def kernel(here_ref, product_ref, ratio_ref, doc_ref, prob_ref, *rest):
        side = sizes.side(here_ref)
        begin = start
        for out_ref, span in zip(rest[len(after) :], spans):
            at = pl.ds(begin, span)
            prob_at = pl.ds(pl.multiple_of(side * side_width + begin, 128), span)
            summed = product_ref[:, at] + jnp.dot(ratio_ref[...], doc_ref[:, at], preferred_element_type=F32)
            out_ref[...] = (-prob_ref[:, prob_at].astype(F32) * summed).astype(BF16)
            begin += span

    return pl.pallas_call(
        kernel,
        out_shape=[jax.ShapeDtypeStruct((words, span), BF16) for span in spans],
        in_specs=[SMEM] + [VMEM] * 4 + [ANY] * len(after),
        out_specs=[VMEM] * len(spans),
        compiler_params=call_params(),
        cost_estimate=cost(2 * words * docs * width, 2 * (4 * words + docs) * width),
        name="beta_piece",
    )(here, product, ratio, docs_held, prob_held, *after)


def add_pair(own, other, after=()):
    def kernel(own_ref, other_ref, *rest):
        rest[-1][...] = (own_ref[...].astype(F32) + other_ref[...].astype(F32)).astype(BF16)

    return pl.pallas_call(
        kernel,
        out_shape=jax.ShapeDtypeStruct(own.shape, BF16),
        in_specs=[VMEM, VMEM] + [ANY] * len(after),
        out_specs=VMEM,
        compiler_params=call_params(),
        cost_estimate=cost(own.size, 6 * own.size),
        name="add_pair",
    )(own, other, *after)


def hold(array, after):
    def kernel(in_ref, *rest):
        rest[-1][...] = in_ref[...]

    return pl.pallas_call(
        kernel,
        out_shape=jax.ShapeDtypeStruct(array.shape, array.dtype),
        in_specs=[VMEM] + [ANY] * len(after),
        out_specs=VMEM,
        compiler_params=call_params(),
        cost_estimate=cost(0, 4 * array.size),
        name="hold",
    )(array, *after)


def theta_grad(sizes, here, ratio, far_ratios, prob_held, far_logits, log_norm, after):
    words, docs = ratio.shape
    half = words // 2
    share = far_logits[0].shape[1]
    far = len(far_ratios)
    count = far + 1
    span = min(share, 512)
    blocks = share // span

    def kernel(here_ref, ratio_ref, *refs):
        far_refs, prob_ref = refs[:far], refs[far]
        logit_refs, norm_ref = refs[far + 1 : 3 * far + 1], refs[3 * far + 1]
        out_ref, done_ref, turned = refs[-3:]
        done_ref[...] = jnp.zeros_like(done_ref)
        side = sizes.side(here_ref)

        @pl.when(pl.program_id(0) == 0)
        def _():
            def put(rows, at):
                turned[:, at : at + rows.shape[0]] = (-rows.astype(F32)).T.astype(BF16)

            put(ratio_ref[...], 0)
            for l in range(far):
                for h in range(2):
                    which = side if h == 0 else 1 - side
                    put(far_refs[l][window(which, half), :], (l + 1) * words + h * half)

        prob = jnp.concatenate(
            [prob_ref[...]] + [jnp.exp(ref[...].astype(F32) - norm_ref[...]).astype(BF16) for ref in logit_refs],
            axis=0,
        )
        out_ref[...] = jnp.dot(turned[...], prob, preferred_element_type=F32)

    whole = lambda j, h: (0, 0)
    held = lambda j, h: (0, lax.rem(h[0], sizes.vocab) * blocks + j)
    column = lambda j, h: (0, j)
    return pl.pallas_call(
        kernel,
        out_shape=[jax.ShapeDtypeStruct((docs, share), F32), jax.ShapeDtypeStruct((8, 128), F32)],
        grid_spec=pltpu.PrefetchScalarGridSpec(
            num_scalar_prefetch=1,
            grid=(blocks,),
            in_specs=[pl.BlockSpec((words, docs), whole)] * count
            + [pl.BlockSpec((words, span), held)]
            + [pl.BlockSpec((half, span), column)] * (2 * far)
            + [pl.BlockSpec((1, span), held)]
            + [ANY] * len(after),
            out_specs=[pl.BlockSpec((docs, span), column), pl.BlockSpec((8, 128), whole)],
            scratch_shapes=[pltpu.VMEM((docs, count * words), BF16)],
        ),
        compiler_params=call_params(),
        cost_estimate=cost(
            20 * count * words * docs * share, (40 * docs + 20 * count * words) * share, 10 * count * words * share
        ),
        name="theta_grad",
    )(here, ratio, *far_ratios, prob_held, *far_logits, log_norm, *after)


def place_pieces(sizes, here, own, other, starts, shape, so_far=None):
    pieces = len(own)
    side_width = shape[1] // 2
    before = [] if so_far is None else [so_far]

    def kernel(here_ref, *refs):
        own_refs, other_refs, (out_ref, done_ref, sems) = refs[:pieces], refs[pieces : 2 * pieces], refs[-3:]
        done_ref[...] = jnp.zeros_like(done_ref)
        side = sizes.side(here_ref)
        copies = []
        for p in range(pieces):
            for h, (ref, which) in enumerate(((own_refs[p], side), (other_refs[p], 1 - side))):
                column = pl.multiple_of(which * side_width + starts[p], 128)
                target = out_ref.at[:, pl.ds(column, ref.shape[1])]
                copies.append(pltpu.make_async_copy(ref, target, sems.at[h, p]))
        for copy in copies:
            copy.start()
        for copy in copies:
            copy.wait()

    return pl.pallas_call(
        kernel,
        out_shape=[jax.ShapeDtypeStruct(shape, BF16), jax.ShapeDtypeStruct((8, 128), F32)],
        in_specs=[SMEM] + [VMEM] * (2 * pieces) + [HBM] * len(before),
        out_specs=[HBM, VMEM],
        scratch_shapes=[pltpu.SemaphoreType.DMA((2, pieces))],
        input_output_aliases={2 * pieces + 1: 0} if before else {},
        compiler_params=call_params(),
        cost_estimate=cost(0, 4 * sum(part.size for part in own)),
        name="place_pieces",
    )(here, *own, *other, *before)


def on_device(sizes, doc_topics, word_logits, log_norm, tile_doc, tile_word, word_counts):
    docs, width = doc_topics.shape
    words = word_logits.shape[0]
    word_tile = word_counts.shape[1]
    here = lax.axis_index(("doc", "topic", "vocab")).astype(jnp.int32)[None]

    def shift(array, by):
        return lax.ppermute(array, "vocab", [(i, (i + by) % sizes.vocab) for i in range(sizes.vocab)])

    def swap(array, axis, bits):
        count = {"doc": sizes.doc, "topic": sizes.topic}[axis]
        return lax.ppermute(array, axis, [(i, i ^ bits) for i in range(count)])

    parts, near_logits, docs_held, docs_sent, prob_held, norm_held = rate_partial(
        sizes, here, doc_topics, word_logits, log_norm[None, :]
    )
    near_logits = [shift(part, s) for s, part in enumerate(near_logits, 1)]
    sibling_docs = swap(docs_sent, "doc", 1)
    order = sorted(range(1, sizes.topic), key=lambda s: s < sizes.topic // 2)
    arrived = [swap(parts[s], "topic", s) for s in order]
    counts = chunk_counts(sizes, here, word_counts, tile_doc, tile_word, docs, words)
    own_ratio = ratio_chunk([parts[0]] + arrived, counts, word_tile)
    gathered = {s: swap(own_ratio, "topic", s) for s in order}
    ratio = join_ratio(
        sizes, here, [own_ratio] + [gathered[s] for s in range(1, sizes.topic)], near_logits + [sibling_docs]
    )
    sibling_ratio = swap(ratio, "doc", 1)
    far_ratios = [shift(ratio, s) for s in range(1, sizes.vocab)]

    side_width = width // 2
    spans = [side_width // 4, side_width // 2, side_width // 4]
    starts = [0, spans[0], spans[0] + spans[1]]
    product = own_product(ratio, docs_held)
    sibling = (sibling_ratio, sibling_docs, prob_held)
    sums = list(beta_piece(sizes, here, product, *sibling, 0, spans[:1], []))
    sums += beta_piece(sizes, here, product, *sibling, spans[0], spans[1:], sums)

    far_logits = []
    for part in near_logits:
        part = hold(part, sums[-1:])
        far_logits += [part, swap(part, "doc", 1)]

    bit = 2
    while 2 * bit < sizes.doc:
        sums = [add_pair(part, swap(part, "doc", bit)) for part in sums]
        bit *= 2
    others = [swap(part, "doc", bit) for part in sums]
    first = add_pair(sums[0], others[0], far_ratios)
    theta, theta_done = theta_grad(sizes, here, ratio, far_ratios, prob_held, far_logits, norm_held, [first])
    early = [first, add_pair(sums[1], others[1])]
    out, early_done = place_pieces(
        sizes, here, early, [swap(part, "doc", 1) for part in early], starts[:-1], word_logits.shape
    )
    last = add_pair(sums[-1], others[-1], [theta_done, early_done])
    out, _ = place_pieces(sizes, here, [last], [swap(last, "doc", 1)], starts[-1:], word_logits.shape, out)
    return theta, out


def solution(mesh):
    placed = (
        P("doc", "topic"),
        P("vocab", "topic"),
        P("topic"),
        P(("doc", "vocab")),
        P(("doc", "vocab")),
        P(("doc", "vocab"), None, None),
    )
    return jax.shard_map(
        functools.partial(on_device, Sizes(mesh)),
        mesh=mesh,
        in_specs=placed,
        out_specs=(P("doc", ("topic", "vocab")), P("vocab", "topic")),
        check_vma=False,
    )
```

```python
import functools

import jax
import jax.numpy as jnp
from jax import lax
from jax.experimental import pallas as pl
from jax.experimental.pallas import tpu as pltpu
from jax.sharding import PartitionSpec as P

BF16 = jnp.bfloat16
F32 = jnp.float32
MIB = 1024 * 1024
ANY = pl.BlockSpec(memory_space=pl.ANY)
HBM = pl.BlockSpec(memory_space=pltpu.HBM)
VMEM = pl.BlockSpec(memory_space=pltpu.VMEM)
SMEM = pl.BlockSpec(memory_space=pltpu.SMEM)


def call_params(mib=16):
    return pltpu.CompilerParams(vmem_limit_bytes=mib * MIB)


def cost(flops, bytes_accessed, transcendentals=0):
    return pl.CostEstimate(flops=flops, bytes_accessed=bytes_accessed, transcendentals=transcendentals)


def in_hbm(array):
    return pltpu.with_memory_space_constraint(array, pltpu.HBM)


def window(index, size):
    return pl.ds(pl.multiple_of(index * size, size), size)


class Sizes:
    def __init__(self, mesh):
        self.doc, self.topic, self.vocab = (mesh.shape[axis] for axis in ("doc", "topic", "vocab"))

    def vocab_at(self, here_ref):
        return lax.rem(here_ref[0], self.vocab)

    def topic_at(self, here_ref):
        return lax.rem(lax.div(here_ref[0], self.vocab), self.topic)

    def side(self, here_ref):
        return lax.rem(lax.div(here_ref[0], self.vocab * self.topic), 2)


def rate_partial(sizes, here, doc_topics, word_logits, log_norm):
    docs, width = doc_topics.shape
    words = word_logits.shape[0]
    side_width = width // 2
    span = min(side_width, 1024)
    steps = side_width // span
    count, far = sizes.topic, sizes.vocab - 1
    chunk, half, share = words // count, words // 2, width // sizes.vocab

    def kernel(here_ref, doc_in, logit_in, norm_in, *rest):
        parts, halves = rest[:count], rest[count : count + far]
        own_ref, sibling_ref, prob_ref, norm_ref, logit_ref, acc, sems, norm_sem = rest[count + far :]
        side = sizes.side(here_ref)
        norm_copy = pltpu.make_async_copy(norm_in, norm_ref, norm_sem)
        norm_copy.start()
        blocks = []
        for which, doc_ref in ((1 - side, sibling_ref), (side, own_ref)):
            for j in range(steps):
                at = window(which * steps + j, span)
                i = len(blocks)
                logit_copy = pltpu.make_async_copy(logit_in.at[:, at], logit_ref.at[:, at], sems.at[0, i])
                held = doc_ref.at[:, pl.ds(j * span, span)]
                doc_copy = pltpu.make_async_copy(doc_in.at[:, at], held, sems.at[1, i])
                blocks.append((at, logit_copy, doc_copy, held))
        for _, logit_copy, doc_copy, _ in blocks:
            logit_copy.start()
            doc_copy.start()
        norm_copy.wait()
        for i, (at, logit_copy, doc_copy, held) in enumerate(blocks):
            logit_copy.wait()
            prob = jnp.exp(logit_ref[:, at].astype(F32) - norm_ref[:, at]).astype(BF16)
            prob_ref[:, at] = prob
            doc_copy.wait()
            part = lax.dot_general(
                prob, held[...], (((1,), (1,)), ((), ())), preferred_element_type=F32
            )
            if i == 0:
                acc[...] = part
            else:
                acc[...] += part
        topic_at = sizes.topic_at(here_ref)
        for s in range(count):
            parts[s][...] = acc[window(topic_at ^ s, chunk), :].astype(BF16)
        rows = window(side, half)
        for s in range(far):
            target = lax.rem(sizes.vocab_at(here_ref) + s + 1, sizes.vocab)
            halves[s][...] = logit_ref[rows, window(target, share)]

    out = pl.pallas_call(
        kernel,
        out_shape=[jax.ShapeDtypeStruct((chunk, docs), BF16)] * count
        + [jax.ShapeDtypeStruct((half, share), BF16)] * far
        + [
            jax.ShapeDtypeStruct((docs, side_width), BF16),
            jax.ShapeDtypeStruct((docs, side_width), BF16),
            jax.ShapeDtypeStruct(word_logits.shape, BF16),
            jax.ShapeDtypeStruct(log_norm.shape, F32),
        ],
        in_specs=[SMEM, HBM, HBM, HBM],
        out_specs=[VMEM] * (count + far + 4),
        scratch_shapes=[
            pltpu.VMEM(word_logits.shape, BF16),
            pltpu.VMEM((words, docs), F32),
            pltpu.SemaphoreType.DMA((2, 2 * steps)),
            pltpu.SemaphoreType.DMA,
        ],
        compiler_params=call_params(),
        cost_estimate=cost(2 * words * docs * width, 2 * (words + docs) * width, words * width),
        name="rate_partial",
    )(here, in_hbm(doc_topics), in_hbm(word_logits), in_hbm(log_norm))
    return out[:count], out[count : count + far], *out[count + far :]


def chunk_counts(sizes, here, word_counts, tile_doc, tile_word, docs, words):
    slots, word_tile, doc_tile = word_counts.shape
    chunk = words // sizes.topic

    def kernel(here_ref, doc_at, word_at, count_ref, out_ref):
        first = sizes.topic_at(here_ref) * chunk
        block = first // word_tile
        row = pl.multiple_of(lax.rem(first, word_tile), chunk)
        out_ref[...] = jnp.zeros_like(out_ref)
        for s in range(slots):
            @pl.when(word_at[s] == block)
            def _():
                out_ref[:, window(doc_at[s], doc_tile)] = count_ref[s, pl.ds(row, chunk), :].astype(F32)

    return pl.pallas_call(
        kernel,
        out_shape=jax.ShapeDtypeStruct((chunk, docs), F32),
        in_specs=[SMEM, SMEM, SMEM, VMEM],
        out_specs=VMEM,
        compiler_params=call_params(),
        cost_estimate=cost(words * docs, 4 * words * docs),
        name="chunk_counts",
    )(here, in_hbm(tile_doc), in_hbm(tile_word), word_counts)


def ratio_chunk(parts, counts, word_tile):
    def kernel(*refs):
        part_refs, count_ref, out_ref = refs[:-2], refs[-2], refs[-1]
        rate = part_refs[0][...].astype(F32)
        for ref in part_refs[1:]:
            rate += ref[...].astype(F32)
        out_ref[...] = (count_ref[...] / (word_tile * rate)).astype(BF16)

    return pl.pallas_call(
        kernel,
        out_shape=jax.ShapeDtypeStruct(counts.shape, BF16),
        in_specs=[VMEM] * (len(parts) + 1),
        out_specs=VMEM,
        compiler_params=call_params(),
        cost_estimate=cost(10 * counts.size, 16 * counts.size),
        name="ratio_chunk",
    )(*parts, counts)


def join_ratio(sizes, here, chunks, order, after):
    rows, docs = chunks[0].shape
    count = sizes.topic

    def kernel(here_ref, *refs):
        topic_at = sizes.topic_at(here_ref)
        for s, ref in zip(order, refs):
            refs[-1][window(topic_at ^ s, rows), :] = ref[...]

    return pl.pallas_call(
        kernel,
        out_shape=jax.ShapeDtypeStruct((rows * count, docs), BF16),
        in_specs=[SMEM] + [VMEM] * count + [ANY] * len(after),
        out_specs=VMEM,
        compiler_params=call_params(),
        cost_estimate=cost(0, 4 * rows * docs * count),
        name="join_ratio",
    )(here, *chunks, *after)


def own_product(ratio, docs_held):
    words, docs = ratio.shape
    width = docs_held.shape[1]

    def kernel(ratio_ref, doc_ref, out_ref):
        out_ref[...] = jnp.dot(ratio_ref[...], doc_ref[...], preferred_element_type=F32)

    return pl.pallas_call(
        kernel,
        out_shape=jax.ShapeDtypeStruct((words, width), F32),
        in_specs=[VMEM, VMEM],
        out_specs=VMEM,
        compiler_params=call_params(),
        cost_estimate=cost(2 * words * docs * width, 2 * docs * width + 4 * words * width),
        name="own_product",
    )(ratio, docs_held)


def beta_piece(sizes, here, product, ratio, docs_held, prob_held, start, spans, after):
    words, side_width = product.shape
    docs, width = docs_held.shape[0], sum(spans)

    def kernel(here_ref, product_ref, ratio_ref, doc_ref, prob_ref, *rest):
        side = sizes.side(here_ref)
        begin = start
        for out_ref, span in zip(rest[len(after) :], spans):
            at = pl.ds(begin, span)
            prob_at = pl.ds(pl.multiple_of(side * side_width + begin, 128), span)
            summed = product_ref[:, at] + jnp.dot(ratio_ref[...], doc_ref[:, at], preferred_element_type=F32)
            out_ref[...] = (-prob_ref[:, prob_at].astype(F32) * summed).astype(BF16)
            begin += span

    return pl.pallas_call(
        kernel,
        out_shape=[jax.ShapeDtypeStruct((words, span), BF16) for span in spans],
        in_specs=[SMEM] + [VMEM] * 4 + [ANY] * len(after),
        out_specs=[VMEM] * len(spans),
        compiler_params=call_params(),
        cost_estimate=cost(2 * words * docs * width, 2 * (4 * words + docs) * width),
        name="beta_piece",
    )(here, product, ratio, docs_held, prob_held, *after)


def add_pair(own, other, after=()):
    def kernel(own_ref, other_ref, *rest):
        rest[-1][...] = (own_ref[...].astype(F32) + other_ref[...].astype(F32)).astype(BF16)

    return pl.pallas_call(
        kernel,
        out_shape=jax.ShapeDtypeStruct(own.shape, BF16),
        in_specs=[VMEM, VMEM] + [ANY] * len(after),
        out_specs=VMEM,
        compiler_params=call_params(),
        cost_estimate=cost(own.size, 6 * own.size),
        name="add_pair",
    )(own, other, *after)


def hold(array, after):
    def kernel(in_ref, *rest):
        rest[-1][...] = in_ref[...]

    return pl.pallas_call(
        kernel,
        out_shape=jax.ShapeDtypeStruct(array.shape, array.dtype),
        in_specs=[VMEM] + [ANY] * len(after),
        out_specs=VMEM,
        compiler_params=call_params(),
        cost_estimate=cost(0, 4 * array.size),
        name="hold",
    )(array, *after)


def theta_grad(sizes, here, ratio, far_ratios, prob_held, far_logits, log_norm):
    words, docs = ratio.shape
    half = words // 2
    share = far_logits[0].shape[1]
    far = len(far_ratios)
    count = far + 1
    span = min(share, 512)
    blocks = share // span

    def kernel(here_ref, ratio_ref, *refs):
        far_refs, prob_ref = refs[:far], refs[far]
        logit_refs, norm_ref = refs[far + 1 : 3 * far + 1], refs[3 * far + 1]
        out_ref, done_ref, turned = refs[-3:]
        done_ref[...] = jnp.zeros_like(done_ref)
        side = sizes.side(here_ref)

        @pl.when(pl.program_id(0) == 0)
        def _():
            def put(rows, at):
                turned[:, at : at + rows.shape[0]] = (-rows.astype(F32)).T.astype(BF16)

            put(ratio_ref[...], 0)
            for l in range(far):
                for h in range(2):
                    which = side if h == 0 else 1 - side
                    put(far_refs[l][window(which, half), :], (l + 1) * words + h * half)

        prob = jnp.concatenate(
            [prob_ref[...]] + [jnp.exp(ref[...].astype(F32) - norm_ref[...]).astype(BF16) for ref in logit_refs],
            axis=0,
        )
        out_ref[...] = jnp.dot(turned[...], prob, preferred_element_type=F32)

    whole = lambda j, h: (0, 0)
    held = lambda j, h: (0, lax.rem(h[0], sizes.vocab) * blocks + j)
    column = lambda j, h: (0, j)
    return pl.pallas_call(
        kernel,
        out_shape=[jax.ShapeDtypeStruct((docs, share), F32), jax.ShapeDtypeStruct((8, 128), F32)],
        grid_spec=pltpu.PrefetchScalarGridSpec(
            num_scalar_prefetch=1,
            grid=(blocks,),
            in_specs=[pl.BlockSpec((words, docs), whole)] * count
            + [pl.BlockSpec((words, span), held)]
            + [pl.BlockSpec((half, span), column)] * (2 * far)
            + [pl.BlockSpec((1, span), held)],
            out_specs=[pl.BlockSpec((docs, span), column), pl.BlockSpec((8, 128), whole)],
            scratch_shapes=[pltpu.VMEM((docs, count * words), BF16)],
        ),
        compiler_params=call_params(),
        cost_estimate=cost(
            20 * count * words * docs * share, (40 * docs + 20 * count * words) * share, 10 * count * words * share
        ),
        name="theta_grad",
    )(here, ratio, *far_ratios, prob_held, *far_logits, log_norm)


def place_pieces(sizes, here, own, other, starts, shape):
    pieces = len(own)
    side_width = shape[1] // 2

    def kernel(here_ref, *refs):
        own_refs, other_refs, (out_ref, sems) = refs[:pieces], refs[pieces : 2 * pieces], refs[-2:]
        side = sizes.side(here_ref)
        copies = []
        for p in range(pieces):
            for h, (ref, which) in enumerate(((own_refs[p], side), (other_refs[p], 1 - side))):
                column = pl.multiple_of(which * side_width + starts[p], 128)
                target = out_ref.at[:, pl.ds(column, ref.shape[1])]
                copies.append(pltpu.make_async_copy(ref, target, sems.at[h, p]))
        for copy in copies:
            copy.start()
        for copy in copies:
            copy.wait()

    return pl.pallas_call(
        kernel,
        out_shape=jax.ShapeDtypeStruct(shape, BF16),
        in_specs=[SMEM] + [VMEM] * (2 * pieces),
        out_specs=HBM,
        scratch_shapes=[pltpu.SemaphoreType.DMA((2, pieces))],
        compiler_params=call_params(),
        cost_estimate=cost(0, 4 * shape[0] * shape[1]),
        name="place_pieces",
    )(here, *own, *other)


def on_device(sizes, doc_topics, word_logits, log_norm, tile_doc, tile_word, word_counts):
    docs, width = doc_topics.shape
    words = word_logits.shape[0]
    word_tile = word_counts.shape[1]
    here = lax.axis_index(("doc", "topic", "vocab")).astype(jnp.int32)[None]

    def shift(array, by):
        return lax.ppermute(array, "vocab", [(i, (i + by) % sizes.vocab) for i in range(sizes.vocab)])

    def swap(array, axis, bits):
        count = {"doc": sizes.doc, "topic": sizes.topic}[axis]
        return lax.ppermute(array, axis, [(i, i ^ bits) for i in range(count)])

    parts, near_logits, docs_held, docs_sent, prob_held, norm_held = rate_partial(
        sizes, here, doc_topics, word_logits, log_norm[None, :]
    )
    near_logits = [shift(part, s) for s, part in enumerate(near_logits, 1)]
    sibling_docs = swap(docs_sent, "doc", 1)
    order = sorted(range(1, sizes.topic), key=lambda s: s < sizes.topic // 2)
    arrived = [swap(parts[s], "topic", s) for s in order]
    counts = chunk_counts(sizes, here, word_counts, tile_doc, tile_word, docs, words)
    own_ratio = ratio_chunk([parts[0]] + arrived, counts, word_tile)
    gathered = [own_ratio] + [swap(own_ratio, "topic", s) for s in order]
    ratio = join_ratio(sizes, here, gathered, [0] + order, near_logits + [sibling_docs])
    sibling_ratio = swap(ratio, "doc", 1)
    far_ratios = [shift(ratio, s) for s in range(1, sizes.vocab)]

    side_width = width // 2
    spans = [side_width // 4, side_width // 2, side_width // 4]
    starts = [0, spans[0], spans[0] + spans[1]]
    product = own_product(ratio, docs_held)
    sibling = (sibling_ratio, sibling_docs, prob_held)
    sums = list(beta_piece(sizes, here, product, *sibling, 0, spans[:1], []))
    sums += beta_piece(sizes, here, product, *sibling, spans[0], spans[1:], sums)

    far_logits = []
    for part in near_logits:
        part = hold(part, sums[-1:])
        far_logits += [part, swap(part, "doc", 1)]

    bit = 2
    while 2 * bit < sizes.doc:
        sums = [add_pair(part, swap(part, "doc", bit)) for part in sums]
        bit *= 2
    others = [swap(part, "doc", bit) for part in sums]
    theta, theta_done = theta_grad(sizes, here, ratio, far_ratios, prob_held, far_logits, norm_held)
    sums = [add_pair(*pair, [theta_done]) for pair in zip(sums, others)]
    out = place_pieces(sizes, here, sums, [swap(part, "doc", 1) for part in sums], starts, word_logits.shape)
    return theta, out


def solution(mesh):
    placed = (
        P("doc", "topic"),
        P("vocab", "topic"),
        P("topic"),
        P(("doc", "vocab")),
        P(("doc", "vocab")),
        P(("doc", "vocab"), None, None),
    )
    return jax.shard_map(
        functools.partial(on_device, Sizes(mesh)),
        mesh=mesh,
        in_specs=placed,
        out_specs=(P("doc", ("topic", "vocab")), P("vocab", "topic")),
        check_vma=False,
    )
```

```python
import functools

import jax
import jax.numpy as jnp
from jax import lax
from jax.experimental import pallas as pl
from jax.experimental.pallas import tpu as pltpu
from jax.sharding import PartitionSpec as P

BF16 = jnp.bfloat16
F32 = jnp.float32
MIB = 1024 * 1024
ANY = pl.BlockSpec(memory_space=pl.ANY)
HBM = pl.BlockSpec(memory_space=pltpu.HBM)
VMEM = pl.BlockSpec(memory_space=pltpu.VMEM)
SMEM = pl.BlockSpec(memory_space=pltpu.SMEM)


def call_params(mib=16):
    return pltpu.CompilerParams(vmem_limit_bytes=mib * MIB)


def cost(flops, bytes_accessed, transcendentals=0):
    return pl.CostEstimate(flops=flops, bytes_accessed=bytes_accessed, transcendentals=transcendentals)


def in_hbm(array):
    return pltpu.with_memory_space_constraint(array, pltpu.HBM)


def window(index, size):
    return pl.ds(pl.multiple_of(index * size, size), size)


class Sizes:
    def __init__(self, mesh):
        self.doc, self.topic, self.vocab = (mesh.shape[axis] for axis in ("doc", "topic", "vocab"))

    def vocab_at(self, here_ref):
        return lax.rem(here_ref[0], self.vocab)

    def topic_at(self, here_ref):
        return lax.rem(lax.div(here_ref[0], self.vocab), self.topic)

    def side(self, here_ref):
        return lax.rem(lax.div(here_ref[0], self.vocab * self.topic), 2)


def rate_partial(sizes, here, doc_topics, word_logits, log_norm, groups):
    docs, width = doc_topics.shape
    words = word_logits.shape[0]
    side_width = width // 2
    span = min(side_width, 1024)
    steps = side_width // span
    count, far = groups * sizes.topic, sizes.vocab - 1
    chunk, half, share = words // count, words // 2, width // sizes.vocab

    def kernel(here_ref, doc_in, logit_in, norm_in, *rest):
        parts, halves = rest[:count], rest[count : count + far]
        own_ref, sibling_ref, prob_ref, norm_ref, logit_ref, acc, sems, norm_sem = rest[count + far :]
        side = sizes.side(here_ref)
        norm_copy = pltpu.make_async_copy(norm_in, norm_ref, norm_sem)
        norm_copy.start()
        blocks = []
        for which, doc_ref in ((1 - side, sibling_ref), (side, own_ref)):
            for j in range(steps):
                at = window(which * steps + j, span)
                i = len(blocks)
                logit_copy = pltpu.make_async_copy(logit_in.at[:, at], logit_ref.at[:, at], sems.at[0, i])
                held = doc_ref.at[:, pl.ds(j * span, span)]
                doc_copy = pltpu.make_async_copy(doc_in.at[:, at], held, sems.at[1, i])
                blocks.append((at, logit_copy, doc_copy, held))
        for _, logit_copy, doc_copy, _ in blocks:
            logit_copy.start()
            doc_copy.start()
        norm_copy.wait()
        for i, (at, logit_copy, doc_copy, held) in enumerate(blocks):
            logit_copy.wait()
            prob = jnp.exp(logit_ref[:, at].astype(F32) - norm_ref[:, at]).astype(BF16)
            prob_ref[:, at] = prob
            doc_copy.wait()
            part = lax.dot_general(
                prob, held[...], (((1,), (1,)), ((), ())), preferred_element_type=F32
            )
            if i == 0:
                acc[...] = part
            else:
                acc[...] += part
        topic_at = sizes.topic_at(here_ref)
        for i in range(count):
            g, s = divmod(i, sizes.topic)
            parts[i][...] = acc[window(g * sizes.topic + (topic_at ^ s), chunk), :].astype(BF16)
        rows = window(side, half)
        for s in range(far):
            target = lax.rem(sizes.vocab_at(here_ref) + s + 1, sizes.vocab)
            halves[s][...] = logit_ref[rows, window(target, share)]

    out = pl.pallas_call(
        kernel,
        out_shape=[jax.ShapeDtypeStruct((chunk, docs), BF16)] * count
        + [jax.ShapeDtypeStruct((half, share), BF16)] * far
        + [
            jax.ShapeDtypeStruct((docs, side_width), BF16),
            jax.ShapeDtypeStruct((docs, side_width), BF16),
            jax.ShapeDtypeStruct(word_logits.shape, BF16),
            jax.ShapeDtypeStruct(log_norm.shape, F32),
        ],
        in_specs=[SMEM, HBM, HBM, HBM],
        out_specs=[VMEM] * (count + far + 4),
        scratch_shapes=[
            pltpu.VMEM(word_logits.shape, BF16),
            pltpu.VMEM((words, docs), F32),
            pltpu.SemaphoreType.DMA((2, 2 * steps)),
            pltpu.SemaphoreType.DMA,
        ],
        compiler_params=call_params(),
        cost_estimate=cost(2 * words * docs * width, 2 * (words + docs) * width, words * width),
        name="rate_partial",
    )(here, in_hbm(doc_topics), in_hbm(word_logits), in_hbm(log_norm))
    parts = [out[g * sizes.topic : (g + 1) * sizes.topic] for g in range(groups)]
    return parts, out[count : count + far], *out[count + far :]


def chunk_counts(sizes, here, word_counts, tile_doc, tile_word, docs, words, groups):
    slots, word_tile, doc_tile = word_counts.shape
    chunk = words // (groups * sizes.topic)

    def kernel(here_ref, doc_at, word_at, count_ref, *out_refs):
        for g, out_ref in enumerate(out_refs):
            first = (g * sizes.topic + sizes.topic_at(here_ref)) * chunk
            block = first // word_tile
            row = pl.multiple_of(lax.rem(first, word_tile), chunk)
            out_ref[...] = jnp.zeros_like(out_ref)
            for s in range(slots):
                @pl.when(word_at[s] == block)
                def _():
                    out_ref[:, window(doc_at[s], doc_tile)] = count_ref[s, pl.ds(row, chunk), :].astype(F32)

    return pl.pallas_call(
        kernel,
        out_shape=[jax.ShapeDtypeStruct((chunk, docs), F32)] * groups,
        in_specs=[SMEM, SMEM, SMEM, VMEM],
        out_specs=[VMEM] * groups,
        compiler_params=call_params(),
        cost_estimate=cost(words * docs, 4 * words * docs),
        name="chunk_counts",
    )(here, in_hbm(tile_doc), in_hbm(tile_word), word_counts)


def ratio_chunk(parts, counts, word_tile, after):
    def kernel(*refs):
        part_refs, count_ref, out_ref = refs[: len(parts)], refs[len(parts)], refs[-1]
        rate = part_refs[0][...].astype(F32)
        for ref in part_refs[1:]:
            rate += ref[...].astype(F32)
        out_ref[...] = (count_ref[...] / (word_tile * rate)).astype(BF16)

    return pl.pallas_call(
        kernel,
        out_shape=jax.ShapeDtypeStruct(counts.shape, BF16),
        in_specs=[VMEM] * (len(parts) + 1) + [ANY] * len(after),
        out_specs=VMEM,
        compiler_params=call_params(),
        cost_estimate=cost(10 * counts.size, 16 * counts.size),
        name="ratio_chunk",
    )(*parts, counts, *after)


def join_ratio(sizes, here, chunks, order, after):
    rows, docs = chunks[0].shape
    count = sizes.topic

    def kernel(here_ref, *refs):
        topic_at = sizes.topic_at(here_ref)
        for s, ref in zip(order, refs):
            refs[-1][window(topic_at ^ s, rows), :] = ref[...]

    return pl.pallas_call(
        kernel,
        out_shape=jax.ShapeDtypeStruct((rows * count, docs), BF16),
        in_specs=[SMEM] + [VMEM] * count + [ANY] * len(after),
        out_specs=VMEM,
        compiler_params=call_params(),
        cost_estimate=cost(0, 4 * rows * docs * count),
        name="join_ratio",
    )(here, *chunks, *after)


def stack_rows(groups):
    rows, docs = groups[0].shape

    def kernel(*refs):
        for g, ref in enumerate(refs[:-1]):
            refs[-1][g * rows : (g + 1) * rows, :] = ref[...]

    return pl.pallas_call(
        kernel,
        out_shape=jax.ShapeDtypeStruct((len(groups) * rows, docs), BF16),
        in_specs=[VMEM] * len(groups),
        out_specs=VMEM,
        compiler_params=call_params(),
        cost_estimate=cost(0, 4 * len(groups) * rows * docs),
        name="stack_rows",
    )(*groups)


def own_product(ratio, docs_held):
    words, docs = ratio.shape
    width = docs_held.shape[1]

    def kernel(ratio_ref, doc_ref, out_ref):
        out_ref[...] = jnp.dot(ratio_ref[...], doc_ref[...], preferred_element_type=F32)

    return pl.pallas_call(
        kernel,
        out_shape=jax.ShapeDtypeStruct((words, width), F32),
        in_specs=[VMEM, VMEM],
        out_specs=VMEM,
        compiler_params=call_params(),
        cost_estimate=cost(2 * words * docs * width, 2 * docs * width + 4 * words * width),
        name="own_product",
    )(ratio, docs_held)


def beta_piece(sizes, here, product, ratio, docs_held, prob_held, group, spans, after):
    words, side_width = product.shape
    docs, width = docs_held.shape[0], sum(spans)
    rows = pl.ds(group * words, words)

    def kernel(here_ref, product_ref, ratio_ref, doc_ref, prob_ref, *rest):
        side = sizes.side(here_ref)
        begin = 0
        for out_ref, span in zip(rest[len(after) :], spans):
            at = pl.ds(begin, span)
            prob_at = pl.ds(pl.multiple_of(side * side_width + begin, 128), span)
            summed = product_ref[:, at] + jnp.dot(ratio_ref[...], doc_ref[:, at], preferred_element_type=F32)
            out_ref[...] = (-prob_ref[rows, prob_at].astype(F32) * summed).astype(BF16)
            begin += span

    return pl.pallas_call(
        kernel,
        out_shape=[jax.ShapeDtypeStruct((words, span), BF16) for span in spans],
        in_specs=[SMEM] + [VMEM] * 4 + [ANY] * len(after),
        out_specs=[VMEM] * len(spans),
        compiler_params=call_params(),
        cost_estimate=cost(2 * words * docs * width, 2 * (4 * words + docs) * width),
        name="beta_piece",
    )(here, product, ratio, docs_held, prob_held, *after)


def add_pair(own, other, after=()):
    def kernel(own_ref, other_ref, *rest):
        rest[-1][...] = (own_ref[...].astype(F32) + other_ref[...].astype(F32)).astype(BF16)

    return pl.pallas_call(
        kernel,
        out_shape=jax.ShapeDtypeStruct(own.shape, BF16),
        in_specs=[VMEM, VMEM] + [ANY] * len(after),
        out_specs=VMEM,
        compiler_params=call_params(),
        cost_estimate=cost(own.size, 6 * own.size),
        name="add_pair",
    )(own, other, *after)


def hold(array, after):
    def kernel(in_ref, *rest):
        rest[-1][...] = in_ref[...]

    return pl.pallas_call(
        kernel,
        out_shape=jax.ShapeDtypeStruct(array.shape, array.dtype),
        in_specs=[VMEM] + [ANY] * len(after),
        out_specs=VMEM,
        compiler_params=call_params(),
        cost_estimate=cost(0, 4 * array.size),
        name="hold",
    )(array, *after)


def theta_grad(sizes, here, ratio, far_ratios, prob_held, far_logits, log_norm):
    words, docs = ratio.shape
    half = words // 2
    share = far_logits[0].shape[1]
    far = len(far_ratios)
    count = far + 1
    span = min(share, 512)
    blocks = share // span

    def kernel(here_ref, ratio_ref, *refs):
        far_refs, prob_ref = refs[:far], refs[far]
        logit_refs, norm_ref = refs[far + 1 : 3 * far + 1], refs[3 * far + 1]
        out_ref, done_ref, turned = refs[-3:]
        done_ref[...] = jnp.zeros_like(done_ref)
        side = sizes.side(here_ref)

        @pl.when(pl.program_id(0) == 0)
        def _():
            def put(rows, at):
                turned[:, at : at + rows.shape[0]] = (-rows.astype(F32)).T.astype(BF16)

            put(ratio_ref[...], 0)
            for l in range(far):
                for h in range(2):
                    which = side if h == 0 else 1 - side
                    put(far_refs[l][window(which, half), :], (l + 1) * words + h * half)

        prob = jnp.concatenate(
            [prob_ref[...]] + [jnp.exp(ref[...].astype(F32) - norm_ref[...]).astype(BF16) for ref in logit_refs],
            axis=0,
        )
        out_ref[...] = jnp.dot(turned[...], prob, preferred_element_type=F32)

    whole = lambda j, h: (0, 0)
    held = lambda j, h: (0, lax.rem(h[0], sizes.vocab) * blocks + j)
    column = lambda j, h: (0, j)
    return pl.pallas_call(
        kernel,
        out_shape=[jax.ShapeDtypeStruct((docs, share), F32), jax.ShapeDtypeStruct((8, 128), F32)],
        grid_spec=pltpu.PrefetchScalarGridSpec(
            num_scalar_prefetch=1,
            grid=(blocks,),
            in_specs=[pl.BlockSpec((words, docs), whole)] * count
            + [pl.BlockSpec((words, span), held)]
            + [pl.BlockSpec((half, span), column)] * (2 * far)
            + [pl.BlockSpec((1, span), held)],
            out_specs=[pl.BlockSpec((docs, span), column), pl.BlockSpec((8, 128), whole)],
            scratch_shapes=[pltpu.VMEM((docs, count * words), BF16)],
        ),
        compiler_params=call_params(),
        cost_estimate=cost(
            20 * count * words * docs * share, (40 * docs + 20 * count * words) * share, 10 * count * words * share
        ),
        name="theta_grad",
    )(here, ratio, *far_ratios, prob_held, *far_logits, log_norm)


def place_pieces(sizes, here, own, other, corners, shape):
    pieces = len(own)
    side_width = shape[1] // 2

    def kernel(here_ref, *refs):
        own_refs, other_refs, (out_ref, sems) = refs[:pieces], refs[pieces : 2 * pieces], refs[-2:]
        side = sizes.side(here_ref)
        copies = []
        for p in range(pieces):
            for h, (ref, which) in enumerate(((own_refs[p], side), (other_refs[p], 1 - side))):
                row, column = corners[p]
                columns = pl.ds(pl.multiple_of(which * side_width + column, 128), ref.shape[1])
                target = out_ref.at[pl.ds(row, ref.shape[0]), columns]
                copies.append(pltpu.make_async_copy(ref, target, sems.at[h, p]))
        for copy in copies:
            copy.start()
        for copy in copies:
            copy.wait()

    return pl.pallas_call(
        kernel,
        out_shape=jax.ShapeDtypeStruct(shape, BF16),
        in_specs=[SMEM] + [VMEM] * (2 * pieces),
        out_specs=HBM,
        scratch_shapes=[pltpu.SemaphoreType.DMA((2, pieces))],
        compiler_params=call_params(),
        cost_estimate=cost(0, 4 * shape[0] * shape[1]),
        name="place_pieces",
    )(here, *own, *other)


def on_device(sizes, doc_topics, word_logits, log_norm, tile_doc, tile_word, word_counts):
    docs, width = doc_topics.shape
    words = word_logits.shape[0]
    word_tile = word_counts.shape[1]
    here = lax.axis_index(("doc", "topic", "vocab")).astype(jnp.int32)[None]

    def shift(array, by):
        return lax.ppermute(array, "vocab", [(i, (i + by) % sizes.vocab) for i in range(sizes.vocab)])

    def swap(array, axis, bits):
        count = {"doc": sizes.doc, "topic": sizes.topic}[axis]
        return lax.ppermute(array, axis, [(i, i ^ bits) for i in range(count)])

    groups = 2 if words % (32 * sizes.topic) == 0 else 1
    parts, near_logits, docs_held, docs_sent, prob_held, norm_held = rate_partial(
        sizes, here, doc_topics, word_logits, log_norm[None, :], groups
    )
    near_logits = [shift(part, s) for s, part in enumerate(near_logits, 1)]
    sibling_docs = swap(docs_sent, "doc", 1)
    order = sorted(range(1, sizes.topic), key=lambda s: s < sizes.topic // 2)
    counts = chunk_counts(sizes, here, word_counts, tile_doc, tile_word, docs, words, groups)
    arrived = [[swap(parts[g][s], "topic", s) for s in order] for g in range(groups)]
    ratios = []
    for g in range(groups):
        own_ratio = ratio_chunk([parts[g][0]] + arrived[g], counts[g], word_tile, [sibling_docs])
        gathered = [own_ratio] + [swap(own_ratio, "topic", s) for s in order]
        after = sum(arrived[g + 1 :], []) if g < groups - 1 else near_logits
        ratios.append(join_ratio(sizes, here, gathered, [0] + order, after))
    ratio = stack_rows(ratios)
    far_ratios = [shift(ratio, s) for s in range(1, sizes.vocab)]

    side_width = width // 2
    far_bits = [1 << b for b in range(1, sizes.doc.bit_length() - 1)]
    sums, others, corners = [], [], []
    for g in range(groups):
        product = own_product(ratios[g], docs_held)
        spans = [side_width] if g < groups - 1 else [side_width // 2] * 2
        corners += [(g * words // groups, sum(spans[:i])) for i in range(len(spans))]
        pieces = beta_piece(
            sizes, here, product, swap(ratios[g], "doc", 1), sibling_docs, prob_held, g, spans, others[-1:]
        )
        for bit in far_bits[:-1]:
            pieces = [add_pair(part, swap(part, "doc", bit)) for part in pieces]
        sums += pieces
        others += [swap(part, "doc", far_bits[-1]) for part in pieces]

    far_logits = []
    for part in near_logits:
        part = hold(part, sums[-1:])
        far_logits += [part, swap(part, "doc", 1)]
    theta, theta_done = theta_grad(sizes, here, ratio, far_ratios, prob_held, far_logits, norm_held)

    sums = [
        add_pair(*pair, [theta_done] if i >= groups - 1 else []) for i, pair in enumerate(zip(sums, others))
    ]
    out = place_pieces(sizes, here, sums, [swap(part, "doc", 1) for part in sums], corners, word_logits.shape)
    return theta, out


def solution(mesh):
    placed = (
        P("doc", "topic"),
        P("vocab", "topic"),
        P("topic"),
        P(("doc", "vocab")),
        P(("doc", "vocab")),
        P(("doc", "vocab"), None, None),
    )
    return jax.shard_map(
        functools.partial(on_device, Sizes(mesh)),
        mesh=mesh,
        in_specs=placed,
        out_specs=(P("doc", ("topic", "vocab")), P("vocab", "topic")),
        check_vma=False,
    )
```

```python
import functools

import jax
import jax.numpy as jnp
from jax import lax
from jax.experimental import pallas as pl
from jax.experimental.pallas import tpu as pltpu
from jax.sharding import PartitionSpec as P

BF16 = jnp.bfloat16
F32 = jnp.float32
MIB = 1024 * 1024
ANY = pl.BlockSpec(memory_space=pl.ANY)
HBM = pl.BlockSpec(memory_space=pltpu.HBM)
VMEM = pl.BlockSpec(memory_space=pltpu.VMEM)
SMEM = pl.BlockSpec(memory_space=pltpu.SMEM)


def call_params(mib=16):
    return pltpu.CompilerParams(vmem_limit_bytes=mib * MIB)


def cost(flops, bytes_accessed, transcendentals=0):
    return pl.CostEstimate(flops=flops, bytes_accessed=bytes_accessed, transcendentals=transcendentals)


def in_hbm(array):
    return pltpu.with_memory_space_constraint(array, pltpu.HBM)


def window(index, size):
    return pl.ds(pl.multiple_of(index * size, size), size)


class Sizes:
    def __init__(self, mesh):
        self.doc, self.topic, self.vocab = (mesh.shape[axis] for axis in ("doc", "topic", "vocab"))

    def vocab_at(self, here_ref):
        return lax.rem(here_ref[0], self.vocab)

    def topic_at(self, here_ref):
        return lax.rem(lax.div(here_ref[0], self.vocab), self.topic)

    def side(self, here_ref):
        return lax.rem(lax.div(here_ref[0], self.vocab * self.topic), 2)


def rate_partial(sizes, here, doc_topics, word_logits, log_norm):
    docs, width = doc_topics.shape
    words = word_logits.shape[0]
    side_width = width // 2
    span = min(side_width, 1024)
    steps = side_width // span
    count, far = sizes.topic, sizes.vocab - 1
    chunk, half, share = words // count, words // 2, width // sizes.vocab

    def kernel(here_ref, doc_in, logit_in, norm_in, *rest):
        parts, halves = rest[:count], rest[count : count + far]
        own_ref, sibling_ref, prob_ref, norm_ref, logit_ref, acc, sems, norm_sem = rest[count + far :]
        side = sizes.side(here_ref)
        norm_copy = pltpu.make_async_copy(norm_in, norm_ref, norm_sem)
        norm_copy.start()
        blocks = []
        for which, doc_ref in ((1 - side, sibling_ref), (side, own_ref)):
            for j in range(steps):
                at = window(which * steps + j, span)
                i = len(blocks)
                logit_copy = pltpu.make_async_copy(logit_in.at[:, at], logit_ref.at[:, at], sems.at[0, i])
                held = doc_ref.at[:, pl.ds(j * span, span)]
                doc_copy = pltpu.make_async_copy(doc_in.at[:, at], held, sems.at[1, i])
                blocks.append((at, logit_copy, doc_copy, held))
        for _, logit_copy, doc_copy, _ in blocks:
            logit_copy.start()
            doc_copy.start()
        norm_copy.wait()
        for i, (at, logit_copy, doc_copy, held) in enumerate(blocks):
            logit_copy.wait()
            prob = jnp.exp(logit_ref[:, at].astype(F32) - norm_ref[:, at]).astype(BF16)
            prob_ref[:, at] = prob
            doc_copy.wait()
            part = lax.dot_general(
                prob, held[...], (((1,), (1,)), ((), ())), preferred_element_type=F32
            )
            if i == 0:
                acc[...] = part
            else:
                acc[...] += part
        topic_at = sizes.topic_at(here_ref)
        for s in range(count):
            parts[s][...] = acc[window(topic_at ^ s, chunk), :].astype(BF16)
        rows = window(side, half)
        for s in range(far):
            target = lax.rem(sizes.vocab_at(here_ref) + s + 1, sizes.vocab)
            halves[s][...] = logit_ref[rows, window(target, share)]

    out = pl.pallas_call(
        kernel,
        out_shape=[jax.ShapeDtypeStruct((chunk, docs), BF16)] * count
        + [jax.ShapeDtypeStruct((half, share), BF16)] * far
        + [
            jax.ShapeDtypeStruct((docs, side_width), BF16),
            jax.ShapeDtypeStruct((docs, side_width), BF16),
            jax.ShapeDtypeStruct(word_logits.shape, BF16),
            jax.ShapeDtypeStruct(log_norm.shape, F32),
        ],
        in_specs=[SMEM, HBM, HBM, HBM],
        out_specs=[VMEM] * (count + far + 4),
        scratch_shapes=[
            pltpu.VMEM(word_logits.shape, BF16),
            pltpu.VMEM((words, docs), F32),
            pltpu.SemaphoreType.DMA((2, 2 * steps)),
            pltpu.SemaphoreType.DMA,
        ],
        compiler_params=call_params(),
        cost_estimate=cost(2 * words * docs * width, 2 * (words + docs) * width, words * width),
        name="rate_partial",
    )(here, in_hbm(doc_topics), in_hbm(word_logits), in_hbm(log_norm))
    return out[:count], out[count : count + far], *out[count + far :]


def chunk_counts(sizes, here, word_counts, tile_doc, tile_word, docs, words):
    slots, word_tile, doc_tile = word_counts.shape
    chunk = words // sizes.topic

    def kernel(here_ref, doc_at, word_at, count_ref, out_ref):
        first = sizes.topic_at(here_ref) * chunk
        block = first // word_tile
        row = pl.multiple_of(lax.rem(first, word_tile), chunk)
        out_ref[...] = jnp.zeros_like(out_ref)
        for s in range(slots):
            @pl.when(word_at[s] == block)
            def _():
                out_ref[:, window(doc_at[s], doc_tile)] = count_ref[s, pl.ds(row, chunk), :].astype(F32)

    return pl.pallas_call(
        kernel,
        out_shape=jax.ShapeDtypeStruct((chunk, docs), F32),
        in_specs=[SMEM, SMEM, SMEM, VMEM],
        out_specs=VMEM,
        compiler_params=call_params(),
        cost_estimate=cost(words * docs, 4 * words * docs),
        name="chunk_counts",
    )(here, in_hbm(tile_doc), in_hbm(tile_word), word_counts)


def ratio_chunk(parts, counts, word_tile):
    def kernel(*refs):
        part_refs, count_ref, out_ref = refs[:-2], refs[-2], refs[-1]
        rate = part_refs[0][...].astype(F32)
        for ref in part_refs[1:]:
            rate += ref[...].astype(F32)
        out_ref[...] = (count_ref[...] / (word_tile * rate)).astype(BF16)

    return pl.pallas_call(
        kernel,
        out_shape=jax.ShapeDtypeStruct(counts.shape, BF16),
        in_specs=[VMEM] * (len(parts) + 1),
        out_specs=VMEM,
        compiler_params=call_params(),
        cost_estimate=cost(10 * counts.size, 16 * counts.size),
        name="ratio_chunk",
    )(*parts, counts)


def join_ratio(sizes, here, chunks, order, after):
    rows, docs = chunks[0].shape
    count = sizes.topic

    def kernel(here_ref, *refs):
        topic_at = sizes.topic_at(here_ref)
        for s, ref in zip(order, refs):
            refs[-1][window(topic_at ^ s, rows), :] = ref[...]

    return pl.pallas_call(
        kernel,
        out_shape=jax.ShapeDtypeStruct((rows * count, docs), BF16),
        in_specs=[SMEM] + [VMEM] * count + [ANY] * len(after),
        out_specs=VMEM,
        compiler_params=call_params(),
        cost_estimate=cost(0, 4 * rows * docs * count),
        name="join_ratio",
    )(here, *chunks, *after)


def own_product(ratio, docs_held):
    words, docs = ratio.shape
    width = docs_held.shape[1]

    def kernel(ratio_ref, doc_ref, out_ref):
        out_ref[...] = jnp.dot(ratio_ref[...], doc_ref[...], preferred_element_type=F32)

    return pl.pallas_call(
        kernel,
        out_shape=jax.ShapeDtypeStruct((words, width), F32),
        in_specs=[VMEM, VMEM],
        out_specs=VMEM,
        compiler_params=call_params(),
        cost_estimate=cost(2 * words * docs * width, 2 * docs * width + 4 * words * width),
        name="own_product",
    )(ratio, docs_held)


def beta_pieces(sizes, here, product, ratio, docs_held, prob_held, flips, after):
    words, side_width = product.shape
    docs = docs_held.shape[0]
    rows = words // len(flips)

    def kernel(here_ref, product_ref, ratio_ref, doc_ref, prob_ref, *rest):
        columns = window(sizes.side(here_ref), side_width)
        topic_at = sizes.topic_at(here_ref)
        summed = product_ref[...] + jnp.dot(ratio_ref[...], doc_ref[...], preferred_element_type=F32)
        for i, (flip, out_ref) in enumerate(zip(flips, rest[len(after) :])):
            prob = prob_ref[window(topic_at ^ flip, rows), columns].astype(F32)
            out_ref[...] = (-prob * summed[i * rows : (i + 1) * rows, :]).astype(BF16)

    return pl.pallas_call(
        kernel,
        out_shape=[jax.ShapeDtypeStruct((rows, side_width), BF16)] * len(flips),
        in_specs=[SMEM] + [VMEM] * 4 + [ANY] * len(after),
        out_specs=[VMEM] * len(flips),
        compiler_params=call_params(),
        cost_estimate=cost(2 * words * docs * side_width, 2 * (4 * words + docs) * side_width),
        name="beta_pieces",
    )(here, product, ratio, docs_held, prob_held, *after)


def stack_rows(parts, after):
    rows, docs = parts[0].shape

    def kernel(*refs):
        for i, ref in enumerate(refs[: len(parts)]):
            refs[-1][i * rows : (i + 1) * rows, :] = ref[...]

    return pl.pallas_call(
        kernel,
        out_shape=jax.ShapeDtypeStruct((len(parts) * rows, docs), BF16),
        in_specs=[VMEM] * len(parts) + [ANY] * len(after),
        out_specs=VMEM,
        compiler_params=call_params(),
        cost_estimate=cost(0, 4 * len(parts) * rows * docs),
        name="stack_rows",
    )(*parts, *after)


def add_pair(own, other, after=()):
    def kernel(own_ref, other_ref, *rest):
        rest[-1][...] = (own_ref[...].astype(F32) + other_ref[...].astype(F32)).astype(BF16)

    return pl.pallas_call(
        kernel,
        out_shape=jax.ShapeDtypeStruct(own.shape, BF16),
        in_specs=[VMEM, VMEM] + [ANY] * len(after),
        out_specs=VMEM,
        compiler_params=call_params(),
        cost_estimate=cost(own.size, 6 * own.size),
        name="add_pair",
    )(own, other, *after)


def hold(array, after):
    def kernel(in_ref, *rest):
        rest[-1][...] = in_ref[...]

    return pl.pallas_call(
        kernel,
        out_shape=jax.ShapeDtypeStruct(array.shape, array.dtype),
        in_specs=[VMEM] + [ANY] * len(after),
        out_specs=VMEM,
        compiler_params=call_params(),
        cost_estimate=cost(0, 4 * array.size),
        name="hold",
    )(array, *after)


def theta_grad(sizes, here, ratio, far_ratios, prob_held, far_logits, log_norm):
    words, docs = ratio.shape
    half = words // 2
    share = far_logits[0].shape[1]
    far = len(far_ratios)
    count = far + 1
    span = min(share, 512)
    blocks = share // span

    def kernel(here_ref, ratio_ref, *refs):
        far_refs, prob_ref = refs[:far], refs[far]
        logit_refs, norm_ref = refs[far + 1 : 3 * far + 1], refs[3 * far + 1]
        out_ref, done_ref, turned = refs[-3:]
        done_ref[...] = jnp.zeros_like(done_ref)
        side = sizes.side(here_ref)

        @pl.when(pl.program_id(0) == 0)
        def _():
            def put(rows, at):
                turned[:, at : at + rows.shape[0]] = (-rows.astype(F32)).T.astype(BF16)

            put(ratio_ref[...], 0)
            for l in range(far):
                for h in range(2):
                    which = side if h == 0 else 1 - side
                    put(far_refs[l][window(which, half), :], (l + 1) * words + h * half)

        prob = jnp.concatenate(
            [prob_ref[...]] + [jnp.exp(ref[...].astype(F32) - norm_ref[...]).astype(BF16) for ref in logit_refs],
            axis=0,
        )
        out_ref[...] = jnp.dot(turned[...], prob, preferred_element_type=F32)

    whole = lambda j, h: (0, 0)
    held = lambda j, h: (0, lax.rem(h[0], sizes.vocab) * blocks + j)
    column = lambda j, h: (0, j)
    return pl.pallas_call(
        kernel,
        out_shape=[jax.ShapeDtypeStruct((docs, share), F32), jax.ShapeDtypeStruct((8, 128), F32)],
        grid_spec=pltpu.PrefetchScalarGridSpec(
            num_scalar_prefetch=1,
            grid=(blocks,),
            in_specs=[pl.BlockSpec((words, docs), whole)] * count
            + [pl.BlockSpec((words, span), held)]
            + [pl.BlockSpec((half, span), column)] * (2 * far)
            + [pl.BlockSpec((1, span), held)],
            out_specs=[pl.BlockSpec((docs, span), column), pl.BlockSpec((8, 128), whole)],
            scratch_shapes=[pltpu.VMEM((docs, count * words), BF16)],
        ),
        compiler_params=call_params(),
        cost_estimate=cost(
            20 * count * words * docs * share, (40 * docs + 20 * count * words) * share, 10 * count * words * share
        ),
        name="theta_grad",
    )(here, ratio, *far_ratios, prob_held, *far_logits, log_norm)


def place_pieces(sizes, here, own, other, flips, shape):
    pieces = len(own)
    side_width = shape[1] // 2

    def kernel(here_ref, *refs):
        own_refs, other_refs, (out_ref, sems) = refs[:pieces], refs[pieces : 2 * pieces], refs[-2:]
        side, topic_at = sizes.side(here_ref), sizes.topic_at(here_ref)
        copies = []
        for p, flip in enumerate(flips):
            for h, (ref, which) in enumerate(((own_refs[p], side), (other_refs[p], 1 - side))):
                target = out_ref.at[window(topic_at ^ flip, ref.shape[0]), window(which, side_width)]
                copies.append(pltpu.make_async_copy(ref, target, sems.at[h, p]))
        for copy in copies:
            copy.start()
        for copy in copies:
            copy.wait()

    return pl.pallas_call(
        kernel,
        out_shape=jax.ShapeDtypeStruct(shape, BF16),
        in_specs=[SMEM] + [VMEM] * (2 * pieces),
        out_specs=HBM,
        scratch_shapes=[pltpu.SemaphoreType.DMA((2, pieces))],
        compiler_params=call_params(),
        cost_estimate=cost(0, 4 * shape[0] * shape[1]),
        name="place_pieces",
    )(here, *own, *other)


def on_device(sizes, doc_topics, word_logits, log_norm, tile_doc, tile_word, word_counts):
    docs, width = doc_topics.shape
    words = word_logits.shape[0]
    word_tile = word_counts.shape[1]
    here = lax.axis_index(("doc", "topic", "vocab")).astype(jnp.int32)[None]

    def shift(array, by):
        return lax.ppermute(array, "vocab", [(i, (i + by) % sizes.vocab) for i in range(sizes.vocab)])

    def swap(array, axis, bits):
        count = {"doc": sizes.doc, "topic": sizes.topic}[axis]
        return lax.ppermute(array, axis, [(i, i ^ bits) for i in range(count)])

    parts, near_logits, docs_held, docs_sent, prob_held, norm_held = rate_partial(
        sizes, here, doc_topics, word_logits, log_norm[None, :]
    )
    near_logits = [shift(part, s) for s, part in enumerate(near_logits, 1)]
    sibling_docs = swap(docs_sent, "doc", 1)
    order = sorted(range(1, sizes.topic), key=lambda s: s < sizes.topic // 2)
    arrived = [swap(parts[s], "topic", s) for s in order]
    counts = chunk_counts(sizes, here, word_counts, tile_doc, tile_word, docs, words)
    own_ratio = ratio_chunk([parts[0]] + arrived, counts, word_tile)
    gathered = [swap(own_ratio, "topic", s) for s in order]
    far_bits = [1 << b for b in range(1, sizes.doc.bit_length() - 1)]

    def beta(ratio, flips, after):
        pieces = beta_pieces(
            sizes, here, own_product(ratio, docs_held), swap(ratio, "doc", 1), sibling_docs, prob_held, flips, after
        )
        for bit in far_bits[:-1]:
            pieces = [add_pair(part, swap(part, "doc", bit)) for part in pieces]
        return [(part, swap(part, "doc", far_bits[-1])) for part in pieces]

    own_pair = beta(own_ratio, [0], [])
    pairs = own_pair + beta(stack_rows(gathered, near_logits), order, [own_pair[0][1]])
    ratio = join_ratio(sizes, here, [own_ratio] + gathered, [0] + order, [pairs[1][0]])
    far_ratios = [shift(ratio, s) for s in range(1, sizes.vocab)]

    far_logits = []
    for part in near_logits:
        part = hold(part, [pairs[-1][0]])
        far_logits += [part, swap(part, "doc", 1)]
    theta, theta_done = theta_grad(sizes, here, ratio, far_ratios, prob_held, far_logits, norm_held)

    sums = [add_pair(*pair, [theta_done] if p else []) for p, pair in enumerate(pairs)]
    out = place_pieces(sizes, here, sums, [swap(part, "doc", 1) for part in sums], [0] + order, word_logits.shape)
    return theta, out


def solution(mesh):
    placed = (
        P("doc", "topic"),
        P("vocab", "topic"),
        P("topic"),
        P(("doc", "vocab")),
        P(("doc", "vocab")),
        P(("doc", "vocab"), None, None),
    )
    return jax.shard_map(
        functools.partial(on_device, Sizes(mesh)),
        mesh=mesh,
        in_specs=placed,
        out_specs=(P("doc", ("topic", "vocab")), P("vocab", "topic")),
        check_vma=False,
    )
```

```python
import functools

import jax
import jax.numpy as jnp
from jax import lax
from jax.experimental import pallas as pl
from jax.experimental.pallas import tpu as pltpu
from jax.sharding import PartitionSpec as P

BF16 = jnp.bfloat16
F32 = jnp.float32
MIB = 1024 * 1024
ANY = pl.BlockSpec(memory_space=pl.ANY)
HBM = pl.BlockSpec(memory_space=pltpu.HBM)
VMEM = pl.BlockSpec(memory_space=pltpu.VMEM)
SMEM = pl.BlockSpec(memory_space=pltpu.SMEM)


def call_params(mib=16):
    return pltpu.CompilerParams(vmem_limit_bytes=mib * MIB)


def cost(flops, bytes_accessed, transcendentals=0):
    return pl.CostEstimate(flops=flops, bytes_accessed=bytes_accessed, transcendentals=transcendentals)


def in_hbm(array):
    return pltpu.with_memory_space_constraint(array, pltpu.HBM)


def window(index, size):
    return pl.ds(pl.multiple_of(index * size, size), size)


class Sizes:
    def __init__(self, mesh):
        self.doc, self.topic, self.vocab = (mesh.shape[axis] for axis in ("doc", "topic", "vocab"))

    def vocab_at(self, here_ref):
        return lax.rem(here_ref[0], self.vocab)

    def topic_at(self, here_ref):
        return lax.rem(lax.div(here_ref[0], self.vocab), self.topic)

    def side(self, here_ref):
        return lax.rem(lax.div(here_ref[0], self.vocab * self.topic), 2)


def rate_partial(sizes, here, doc_topics, word_logits, log_norm):
    docs, width = doc_topics.shape
    words = word_logits.shape[0]
    side_width = width // 2
    span = min(side_width, 512)
    steps = side_width // span
    count, far = sizes.topic, sizes.vocab - 1
    chunk, half, share = words // count, words // 2, width // sizes.vocab

    def kernel(here_ref, doc_in, logit_in, norm_in, *rest):
        parts, halves = rest[:count], rest[count : count + far]
        own_ref, sibling_ref, prob_ref, norm_ref, logit_ref, acc, sems, norm_sem = rest[count + far :]
        side = sizes.side(here_ref)
        norm_copy = pltpu.make_async_copy(norm_in, norm_ref, norm_sem)
        blocks = []
        for which, doc_ref in ((1 - side, sibling_ref), (side, own_ref)):
            for j in range(steps):
                at = window(which * steps + j, span)
                i = len(blocks)
                logit_copy = pltpu.make_async_copy(logit_in.at[:, at], logit_ref.at[:, at], sems.at[0, i])
                held = doc_ref.at[:, pl.ds(j * span, span)]
                doc_copy = pltpu.make_async_copy(doc_in.at[:, at], held, sems.at[1, i])
                blocks.append((at, logit_copy, doc_copy, held))
        for i, (_, logit_copy, doc_copy, _) in enumerate(blocks):
            logit_copy.start()
            if i == 0:
                norm_copy.start()
            doc_copy.start()
        norm_copy.wait()
        for i, (at, logit_copy, doc_copy, held) in enumerate(blocks):
            logit_copy.wait()
            prob = jnp.exp(logit_ref[:, at].astype(F32) - norm_ref[:, at]).astype(BF16)
            prob_ref[:, at] = prob
            doc_copy.wait()
            part = lax.dot_general(
                prob, held[...], (((1,), (1,)), ((), ())), preferred_element_type=F32
            )
            if i == 0:
                acc[...] = part
            else:
                acc[...] += part
        topic_at = sizes.topic_at(here_ref)
        for s in range(count):
            parts[s][...] = acc[window(topic_at ^ s, chunk), :].astype(BF16)
        rows = window(side, half)
        for s in range(far):
            target = lax.rem(sizes.vocab_at(here_ref) + s + 1, sizes.vocab)
            halves[s][...] = logit_ref[rows, window(target, share)]

    out = pl.pallas_call(
        kernel,
        out_shape=[jax.ShapeDtypeStruct((chunk, docs), BF16)] * count
        + [jax.ShapeDtypeStruct((half, share), BF16)] * far
        + [
            jax.ShapeDtypeStruct((docs, side_width), BF16),
            jax.ShapeDtypeStruct((docs, side_width), BF16),
            jax.ShapeDtypeStruct(word_logits.shape, BF16),
            jax.ShapeDtypeStruct(log_norm.shape, F32),
        ],
        in_specs=[SMEM, HBM, HBM, HBM],
        out_specs=[VMEM] * (count + far + 4),
        scratch_shapes=[
            pltpu.VMEM(word_logits.shape, BF16),
            pltpu.VMEM((words, docs), F32),
            pltpu.SemaphoreType.DMA((2, 2 * steps)),
            pltpu.SemaphoreType.DMA,
        ],
        compiler_params=call_params(),
        cost_estimate=cost(2 * words * docs * width, 2 * (words + docs) * width, words * width),
        name="rate_partial",
    )(here, in_hbm(doc_topics), in_hbm(word_logits), in_hbm(log_norm))
    return out[:count], out[count : count + far], *out[count + far :]


def chunk_counts(sizes, here, word_counts, tile_doc, tile_word, docs, words):
    slots, word_tile, doc_tile = word_counts.shape
    chunk = words // sizes.topic

    def kernel(here_ref, doc_at, word_at, count_ref, out_ref):
        first = sizes.topic_at(here_ref) * chunk
        block = first // word_tile
        row = pl.multiple_of(lax.rem(first, word_tile), chunk)
        out_ref[...] = jnp.zeros_like(out_ref)
        for s in range(slots):
            @pl.when(word_at[s] == block)
            def _():
                out_ref[:, window(doc_at[s], doc_tile)] = count_ref[s, pl.ds(row, chunk), :].astype(F32)

    return pl.pallas_call(
        kernel,
        out_shape=jax.ShapeDtypeStruct((chunk, docs), F32),
        in_specs=[SMEM, SMEM, SMEM, VMEM],
        out_specs=VMEM,
        compiler_params=call_params(),
        cost_estimate=cost(words * docs, 4 * words * docs),
        name="chunk_counts",
    )(here, in_hbm(tile_doc), in_hbm(tile_word), word_counts)


def ratio_chunk(parts, counts, word_tile):
    def kernel(*refs):
        part_refs, count_ref, out_ref = refs[:-2], refs[-2], refs[-1]
        rate = part_refs[0][...].astype(F32)
        for ref in part_refs[1:]:
            rate += ref[...].astype(F32)
        out_ref[...] = (count_ref[...] / (word_tile * rate)).astype(BF16)

    return pl.pallas_call(
        kernel,
        out_shape=jax.ShapeDtypeStruct(counts.shape, BF16),
        in_specs=[VMEM] * (len(parts) + 1),
        out_specs=VMEM,
        compiler_params=call_params(),
        cost_estimate=cost(10 * counts.size, 16 * counts.size),
        name="ratio_chunk",
    )(*parts, counts)


def join_ratio(sizes, here, chunks, order, after):
    rows, docs = chunks[0].shape
    count = sizes.topic

    def kernel(here_ref, *refs):
        topic_at = sizes.topic_at(here_ref)
        for s, ref in zip(order, refs):
            refs[-1][window(topic_at ^ s, rows), :] = ref[...]

    return pl.pallas_call(
        kernel,
        out_shape=jax.ShapeDtypeStruct((rows * count, docs), BF16),
        in_specs=[SMEM] + [VMEM] * count + [ANY] * len(after),
        out_specs=VMEM,
        compiler_params=call_params(),
        cost_estimate=cost(0, 4 * rows * docs * count),
        name="join_ratio",
    )(here, *chunks, *after)


def own_product(ratio, docs_held):
    words, docs = ratio.shape
    width = docs_held.shape[1]

    def kernel(ratio_ref, doc_ref, out_ref):
        out_ref[...] = jnp.dot(ratio_ref[...], doc_ref[...], preferred_element_type=F32)

    return pl.pallas_call(
        kernel,
        out_shape=jax.ShapeDtypeStruct((words, width), F32),
        in_specs=[VMEM, VMEM],
        out_specs=VMEM,
        compiler_params=call_params(),
        cost_estimate=cost(2 * words * docs * width, 2 * docs * width + 4 * words * width),
        name="own_product",
    )(ratio, docs_held)


def beta_piece(sizes, here, product, ratio, docs_held, prob_held, flips, chosen):
    side_width = product.shape[1]
    docs = docs_held.shape[0]
    rows = product.shape[0] // len(flips)
    words = rows * len(chosen)

    def kernel(here_ref, product_ref, ratio_ref, doc_ref, prob_ref, out_ref):
        columns = window(sizes.side(here_ref), side_width)
        topic_at = sizes.topic_at(here_ref)
        at = pl.ds(chosen[0] * rows, words)
        summed = product_ref[at, :] + jnp.dot(ratio_ref[at, :], doc_ref[...], preferred_element_type=F32)
        for i, c in enumerate(chosen):
            at = pl.ds(i * rows, rows)
            prob = prob_ref[window(topic_at ^ flips[c], rows), columns].astype(F32)
            out_ref[at, :] = (-prob * summed[i * rows : (i + 1) * rows, :]).astype(BF16)

    return pl.pallas_call(
        kernel,
        out_shape=jax.ShapeDtypeStruct((words, side_width), BF16),
        in_specs=[SMEM] + [VMEM] * 4,
        out_specs=VMEM,
        compiler_params=call_params(),
        cost_estimate=cost(2 * words * docs * side_width, 2 * (4 * words + docs) * side_width),
        name="beta_piece",
    )(here, product, ratio, docs_held, prob_held)


def stack_rows(parts, after):
    rows, docs = parts[0].shape

    def kernel(*refs):
        for i, ref in enumerate(refs[: len(parts)]):
            refs[-1][i * rows : (i + 1) * rows, :] = ref[...]

    return pl.pallas_call(
        kernel,
        out_shape=jax.ShapeDtypeStruct((len(parts) * rows, docs), BF16),
        in_specs=[VMEM] * len(parts) + [ANY] * len(after),
        out_specs=VMEM,
        compiler_params=call_params(),
        cost_estimate=cost(0, 4 * len(parts) * rows * docs),
        name="stack_rows",
    )(*parts, *after)


def add_pair(own, other, after=()):
    def kernel(own_ref, other_ref, *rest):
        rest[-1][...] = (own_ref[...].astype(F32) + other_ref[...].astype(F32)).astype(BF16)

    return pl.pallas_call(
        kernel,
        out_shape=jax.ShapeDtypeStruct(own.shape, BF16),
        in_specs=[VMEM, VMEM] + [ANY] * len(after),
        out_specs=VMEM,
        compiler_params=call_params(),
        cost_estimate=cost(own.size, 6 * own.size),
        name="add_pair",
    )(own, other, *after)


def hold(array, after):
    def kernel(in_ref, *rest):
        rest[-1][...] = in_ref[...]

    return pl.pallas_call(
        kernel,
        out_shape=jax.ShapeDtypeStruct(array.shape, array.dtype),
        in_specs=[VMEM] + [ANY] * len(after),
        out_specs=VMEM,
        compiler_params=call_params(),
        cost_estimate=cost(0, 4 * array.size),
        name="hold",
    )(array, *after)


def theta_grad(sizes, here, ratio, far_ratios, prob_held, far_logits, log_norm):
    words, docs = ratio.shape
    half = words // 2
    share = far_logits[0].shape[1]
    far = len(far_ratios)
    count = far + 1
    span = min(share, 512)
    blocks = share // span

    def kernel(here_ref, ratio_ref, *refs):
        far_refs, prob_ref = refs[:far], refs[far]
        logit_refs, norm_ref = refs[far + 1 : 3 * far + 1], refs[3 * far + 1]
        out_ref, done_ref, turned = refs[-3:]
        done_ref[...] = jnp.zeros_like(done_ref)
        side = sizes.side(here_ref)

        @pl.when(pl.program_id(0) == 0)
        def _():
            def put(rows, at):
                turned[:, at : at + rows.shape[0]] = (-rows.astype(F32)).T.astype(BF16)

            put(ratio_ref[...], 0)
            for l in range(far):
                for h in range(2):
                    which = side if h == 0 else 1 - side
                    put(far_refs[l][window(which, half), :], (l + 1) * words + h * half)

        prob = jnp.concatenate(
            [prob_ref[...]] + [jnp.exp(ref[...].astype(F32) - norm_ref[...]).astype(BF16) for ref in logit_refs],
            axis=0,
        )
        out_ref[...] = jnp.dot(turned[...], prob, preferred_element_type=F32)

    whole = lambda j, h: (0, 0)
    held = lambda j, h: (0, lax.rem(h[0], sizes.vocab) * blocks + j)
    column = lambda j, h: (0, j)
    return pl.pallas_call(
        kernel,
        out_shape=[jax.ShapeDtypeStruct((docs, share), F32), jax.ShapeDtypeStruct((8, 128), F32)],
        grid_spec=pltpu.PrefetchScalarGridSpec(
            num_scalar_prefetch=1,
            grid=(blocks,),
            in_specs=[pl.BlockSpec((words, docs), whole)] * count
            + [pl.BlockSpec((words, span), held)]
            + [pl.BlockSpec((half, span), column)] * (2 * far)
            + [pl.BlockSpec((1, span), held)],
            out_specs=[pl.BlockSpec((docs, span), column), pl.BlockSpec((8, 128), whole)],
            scratch_shapes=[pltpu.VMEM((docs, count * words), BF16)],
        ),
        compiler_params=call_params(),
        cost_estimate=cost(1, 1),
        name="theta_grad",
    )(here, ratio, *far_ratios, prob_held, *far_logits, log_norm)


def place_pieces(sizes, here, own, other, flips, shape):
    pieces = len(own)
    side_width = shape[1] // 2

    def kernel(here_ref, *refs):
        own_refs, other_refs, (out_ref, sems) = refs[:pieces], refs[pieces : 2 * pieces], refs[-2:]
        side, topic_at = sizes.side(here_ref), sizes.topic_at(here_ref)
        copies = []
        for p in range(pieces):
            rows = own_refs[p].shape[0] // len(flips[p])
            for h, (ref, which) in enumerate(((own_refs[p], side), (other_refs[p], 1 - side))):
                for i, flip in enumerate(flips[p]):
                    part = ref.at[pl.ds(i * rows, rows), :]
                    target = out_ref.at[window(topic_at ^ flip, rows), window(which, side_width)]
                    copies.append(pltpu.make_async_copy(part, target, sems.at[len(copies)]))
        for copy in copies:
            copy.start()
        for copy in copies:
            copy.wait()

    return pl.pallas_call(
        kernel,
        out_shape=jax.ShapeDtypeStruct(shape, BF16),
        in_specs=[SMEM] + [VMEM] * (2 * pieces),
        out_specs=HBM,
        scratch_shapes=[pltpu.SemaphoreType.DMA((2 * sum(map(len, flips)),))],
        compiler_params=call_params(),
        cost_estimate=cost(0, 4 * shape[0] * shape[1]),
        name="place_pieces",
    )(here, *own, *other)


def on_device(sizes, doc_topics, word_logits, log_norm, tile_doc, tile_word, word_counts):
    docs, width = doc_topics.shape
    words = word_logits.shape[0]
    word_tile = word_counts.shape[1]
    here = lax.axis_index(("doc", "topic", "vocab")).astype(jnp.int32)[None]

    def shift(array, by):
        return lax.ppermute(array, "vocab", [(i, (i + by) % sizes.vocab) for i in range(sizes.vocab)])

    def swap(array, axis, bits):
        count = {"doc": sizes.doc, "topic": sizes.topic}[axis]
        return lax.ppermute(array, axis, [(i, i ^ bits) for i in range(count)])

    parts, near_logits, docs_held, docs_sent, prob_held, norm_held = rate_partial(
        sizes, here, doc_topics, word_logits, log_norm[None, :]
    )
    near_logits = [shift(part, s) for s, part in enumerate(near_logits, 1)]
    sibling_docs = swap(docs_sent, "doc", 1)
    order = sorted(range(1, sizes.topic), key=lambda s: s < sizes.topic // 2)
    arrived = [swap(parts[s], "topic", s) for s in order]
    counts = chunk_counts(sizes, here, word_counts, tile_doc, tile_word, docs, words)
    own_ratio = ratio_chunk([parts[0]] + arrived, counts, word_tile)
    gathered = [swap(own_ratio, "topic", s) for s in order]
    far_bits = [1 << b for b in range(1, sizes.doc.bit_length() - 1)]

    def beta(ratio, flips, groups):
        product, sibling_ratio = own_product(ratio, docs_held), swap(ratio, "doc", 1)
        pieces = [
            beta_piece(sizes, here, product, sibling_ratio, sibling_docs, prob_held, flips, chosen) for chosen in groups
        ]
        for bit in far_bits[:-1]:
            pieces = [add_pair(part, swap(part, "doc", bit)) for part in pieces]
        return [(part, swap(part, "doc", far_bits[-1])) for part in pieces]

    first = add_pair(*beta(own_ratio, [0], [[0]])[0])
    last = len(order) - 1
    groups = [list(range(last)), [last]] if last else [[0]]
    pairs = beta(stack_rows(gathered, near_logits), order, groups)

    ratio = join_ratio(sizes, here, [own_ratio] + gathered, [0] + order, [first])
    far_ratios = [shift(ratio, s) for s in range(1, sizes.vocab)]
    far_logits = []
    for part in near_logits:
        part = hold(part, [pairs[0][0]])
        far_logits += [part, swap(part, "doc", 1)]
    theta, theta_done = theta_grad(sizes, here, ratio, far_ratios, prob_held, far_logits, norm_held)

    sums = [first] + [add_pair(*pair, [theta_done]) for pair in pairs]
    flips = [[0]] + [[order[c] for c in chosen] for chosen in groups]
    out = place_pieces(sizes, here, sums, [swap(part, "doc", 1) for part in sums], flips, word_logits.shape)
    return theta, out


def solution(mesh):
    placed = (
        P("doc", "topic"),
        P("vocab", "topic"),
        P("topic"),
        P(("doc", "vocab")),
        P(("doc", "vocab")),
        P(("doc", "vocab"), None, None),
    )
    return jax.shard_map(
        functools.partial(on_device, Sizes(mesh)),
        mesh=mesh,
        in_specs=placed,
        out_specs=(P("doc", ("topic", "vocab")), P("vocab", "topic")),
        check_vma=False,
    )
```

```python
import functools

import jax
import jax.numpy as jnp
from jax import lax
from jax.experimental import pallas as pl
from jax.experimental.pallas import tpu as pltpu
from jax.sharding import PartitionSpec as P

BF16 = jnp.bfloat16
F32 = jnp.float32
MIB = 1024 * 1024
ANY = pl.BlockSpec(memory_space=pl.ANY)
HBM = pl.BlockSpec(memory_space=pltpu.HBM)
VMEM = pl.BlockSpec(memory_space=pltpu.VMEM)
SMEM = pl.BlockSpec(memory_space=pltpu.SMEM)


def call_params(mib=16):
    return pltpu.CompilerParams(vmem_limit_bytes=mib * MIB)


def cost(flops, bytes_accessed, transcendentals=0):
    return pl.CostEstimate(flops=flops, bytes_accessed=bytes_accessed, transcendentals=transcendentals)


def in_hbm(array):
    return pltpu.with_memory_space_constraint(array, pltpu.HBM)


def window(index, size):
    return pl.ds(pl.multiple_of(index * size, size), size)


class Sizes:
    def __init__(self, mesh):
        self.doc, self.topic, self.vocab = (mesh.shape[axis] for axis in ("doc", "topic", "vocab"))

    def vocab_at(self, here_ref):
        return lax.rem(here_ref[0], self.vocab)

    def topic_at(self, here_ref):
        return lax.rem(lax.div(here_ref[0], self.vocab), self.topic)

    def side(self, here_ref):
        return lax.rem(lax.div(here_ref[0], self.vocab * self.topic), 2)


def rate_partial(sizes, here, doc_topics, word_logits, log_norm):
    docs, width = doc_topics.shape
    words = word_logits.shape[0]
    side_width = width // 2
    span = min(side_width, 1024)
    steps = side_width // span
    count, far = sizes.topic, sizes.vocab - 1
    chunk, half, share = words // count, words // 2, width // sizes.vocab

    def kernel(here_ref, doc_in, logit_in, norm_in, *rest):
        parts, halves = rest[:count], rest[count : count + far]
        own_ref, sibling_ref, prob_ref, norm_ref, logit_ref, acc, sems, norm_sem = rest[count + far :]
        side = sizes.side(here_ref)
        norm_copy = pltpu.make_async_copy(norm_in, norm_ref, norm_sem)
        norm_copy.start()
        blocks = []
        for which, doc_ref in ((1 - side, sibling_ref), (side, own_ref)):
            for j in range(steps):
                at = window(which * steps + j, span)
                i = len(blocks)
                logit_copy = pltpu.make_async_copy(logit_in.at[:, at], logit_ref.at[:, at], sems.at[0, i])
                held = doc_ref.at[:, pl.ds(j * span, span)]
                doc_copy = pltpu.make_async_copy(doc_in.at[:, at], held, sems.at[1, i])
                blocks.append((at, logit_copy, doc_copy, held))
        for _, logit_copy, doc_copy, _ in blocks:
            logit_copy.start()
            doc_copy.start()
        norm_copy.wait()
        for i, (at, logit_copy, doc_copy, held) in enumerate(blocks):
            logit_copy.wait()
            prob = jnp.exp(logit_ref[:, at].astype(F32) - norm_ref[:, at]).astype(BF16)
            prob_ref[:, at] = prob
            doc_copy.wait()
            part = lax.dot_general(
                prob, held[...], (((1,), (1,)), ((), ())), preferred_element_type=F32
            )
            if i == 0:
                acc[...] = part
            else:
                acc[...] += part
        topic_at = sizes.topic_at(here_ref)
        for s in range(count):
            parts[s][...] = acc[window(topic_at ^ s, chunk), :].astype(BF16)
        rows = window(side, half)
        for s in range(far):
            target = lax.rem(sizes.vocab_at(here_ref) + s + 1, sizes.vocab)
            halves[s][...] = logit_ref[rows, window(target, share)]

    out = pl.pallas_call(
        kernel,
        out_shape=[jax.ShapeDtypeStruct((chunk, docs), BF16)] * count
        + [jax.ShapeDtypeStruct((half, share), BF16)] * far
        + [
            jax.ShapeDtypeStruct((docs, side_width), BF16),
            jax.ShapeDtypeStruct((docs, side_width), BF16),
            jax.ShapeDtypeStruct(word_logits.shape, BF16),
            jax.ShapeDtypeStruct(log_norm.shape, F32),
        ],
        in_specs=[SMEM, HBM, HBM, HBM],
        out_specs=[VMEM] * (count + far + 4),
        scratch_shapes=[
            pltpu.VMEM(word_logits.shape, BF16),
            pltpu.VMEM((words, docs), F32),
            pltpu.SemaphoreType.DMA((2, 2 * steps)),
            pltpu.SemaphoreType.DMA,
        ],
        compiler_params=call_params(),
        cost_estimate=cost(2 * words * docs * width, 2 * (words + docs) * width, words * width),
        name="rate_partial",
    )(here, in_hbm(doc_topics), in_hbm(word_logits), in_hbm(log_norm))
    return out[:count], out[count : count + far], *out[count + far :]


def chunk_counts(sizes, here, word_counts, tile_doc, tile_word, docs, words):
    slots, word_tile, doc_tile = word_counts.shape
    chunk = words // sizes.topic

    def kernel(here_ref, doc_at, word_at, count_ref, out_ref):
        first = sizes.topic_at(here_ref) * chunk
        block = first // word_tile
        row = pl.multiple_of(lax.rem(first, word_tile), chunk)
        out_ref[...] = jnp.zeros_like(out_ref)
        for s in range(slots):
            @pl.when(word_at[s] == block)
            def _():
                out_ref[:, window(doc_at[s], doc_tile)] = count_ref[s, pl.ds(row, chunk), :].astype(F32)

    return pl.pallas_call(
        kernel,
        out_shape=jax.ShapeDtypeStruct((chunk, docs), F32),
        in_specs=[SMEM, SMEM, SMEM, VMEM],
        out_specs=VMEM,
        compiler_params=call_params(),
        cost_estimate=cost(words * docs, 4 * words * docs),
        name="chunk_counts",
    )(here, in_hbm(tile_doc), in_hbm(tile_word), word_counts)


def ratio_chunk(parts, counts, word_tile):
    def kernel(*refs):
        part_refs, count_ref, out_ref = refs[:-2], refs[-2], refs[-1]
        rate = part_refs[0][...].astype(F32)
        for ref in part_refs[1:]:
            rate += ref[...].astype(F32)
        out_ref[...] = (count_ref[...] / (word_tile * rate)).astype(BF16)

    return pl.pallas_call(
        kernel,
        out_shape=jax.ShapeDtypeStruct(counts.shape, BF16),
        in_specs=[VMEM] * (len(parts) + 1),
        out_specs=VMEM,
        compiler_params=call_params(),
        cost_estimate=cost(10 * counts.size, 16 * counts.size),
        name="ratio_chunk",
    )(*parts, counts)


def join_ratio(sizes, here, chunks, order, after):
    rows, docs = chunks[0].shape
    count = sizes.topic

    def kernel(here_ref, *refs):
        topic_at = sizes.topic_at(here_ref)
        for s, ref in zip(order, refs):
            refs[-1][window(topic_at ^ s, rows), :] = ref[...]

    return pl.pallas_call(
        kernel,
        out_shape=jax.ShapeDtypeStruct((rows * count, docs), BF16),
        in_specs=[SMEM] + [VMEM] * count + [ANY] * len(after),
        out_specs=VMEM,
        compiler_params=call_params(),
        cost_estimate=cost(0, 4 * rows * docs * count),
        name="join_ratio",
    )(here, *chunks, *after)


def own_product(ratio, docs_held):
    words, docs = ratio.shape
    width = docs_held.shape[1]

    def kernel(ratio_ref, doc_ref, out_ref):
        out_ref[...] = jnp.dot(ratio_ref[...], doc_ref[...], preferred_element_type=F32)

    return pl.pallas_call(
        kernel,
        out_shape=jax.ShapeDtypeStruct((words, width), F32),
        in_specs=[VMEM, VMEM],
        out_specs=VMEM,
        compiler_params=call_params(),
        cost_estimate=cost(2 * words * docs * width, 2 * docs * width + 4 * words * width),
        name="own_product",
    )(ratio, docs_held)


def beta_pieces(sizes, here, product, ratio, docs_held, prob_held, flips, after):
    words, side_width = product.shape
    docs = docs_held.shape[0]
    rows = words // sum(map(len, flips))

    def kernel(here_ref, product_ref, ratio_ref, doc_ref, prob_ref, *rest):
        columns = window(sizes.side(here_ref), side_width)
        topic_at = sizes.topic_at(here_ref)
        summed = product_ref[...] + jnp.dot(ratio_ref[...], doc_ref[...], preferred_element_type=F32)
        chunk = 0
        for piece, out_ref in zip(flips, rest[len(after) :]):
            for i, flip in enumerate(piece):
                prob = prob_ref[window(topic_at ^ flip, rows), columns].astype(F32)
                out_ref[i * rows : (i + 1) * rows, :] = (
                    -prob * summed[chunk * rows : (chunk + 1) * rows, :]
                ).astype(BF16)
                chunk += 1

    return pl.pallas_call(
        kernel,
        out_shape=[jax.ShapeDtypeStruct((rows * len(piece), side_width), BF16) for piece in flips],
        in_specs=[SMEM] + [VMEM] * 4 + [ANY] * len(after),
        out_specs=[VMEM] * len(flips),
        compiler_params=call_params(),
        cost_estimate=cost(2 * words * docs * side_width, 2 * (4 * words + docs) * side_width),
        name="beta_pieces",
    )(here, product, ratio, docs_held, prob_held, *after)


def stack_rows(parts, after):
    rows, docs = parts[0].shape

    def kernel(*refs):
        for i, ref in enumerate(refs[: len(parts)]):
            refs[-1][i * rows : (i + 1) * rows, :] = ref[...]

    return pl.pallas_call(
        kernel,
        out_shape=jax.ShapeDtypeStruct((len(parts) * rows, docs), BF16),
        in_specs=[VMEM] * len(parts) + [ANY] * len(after),
        out_specs=VMEM,
        compiler_params=call_params(),
        cost_estimate=cost(0, 4 * len(parts) * rows * docs),
        name="stack_rows",
    )(*parts, *after)


def add_pair(own, other, after=()):
    def kernel(own_ref, other_ref, *rest):
        rest[-1][...] = (own_ref[...].astype(F32) + other_ref[...].astype(F32)).astype(BF16)

    return pl.pallas_call(
        kernel,
        out_shape=jax.ShapeDtypeStruct(own.shape, BF16),
        in_specs=[VMEM, VMEM] + [ANY] * len(after),
        out_specs=VMEM,
        compiler_params=call_params(),
        cost_estimate=cost(own.size, 6 * own.size),
        name="add_pair",
    )(own, other, *after)


def hold(array, after):
    def kernel(in_ref, *rest):
        rest[-1][...] = in_ref[...]

    return pl.pallas_call(
        kernel,
        out_shape=jax.ShapeDtypeStruct(array.shape, array.dtype),
        in_specs=[VMEM] + [ANY] * len(after),
        out_specs=VMEM,
        compiler_params=call_params(),
        cost_estimate=cost(0, 4 * array.size),
        name="hold",
    )(array, *after)


def theta_grad(sizes, here, ratio, far_ratios, prob_held, far_logits, log_norm):
    words, docs = ratio.shape
    half = words // 2
    share = far_logits[0].shape[1]
    far = len(far_ratios)
    count = far + 1
    span = min(share, 512)
    blocks = share // span

    def kernel(here_ref, ratio_ref, *refs):
        far_refs, prob_ref = refs[:far], refs[far]
        logit_refs, norm_ref = refs[far + 1 : 3 * far + 1], refs[3 * far + 1]
        out_ref, done_ref, turned = refs[-3:]
        done_ref[...] = jnp.zeros_like(done_ref)
        side = sizes.side(here_ref)

        @pl.when(pl.program_id(0) == 0)
        def _():
            def put(rows, at):
                turned[:, at : at + rows.shape[0]] = (-rows.astype(F32)).T.astype(BF16)

            put(ratio_ref[...], 0)
            for l in range(far):
                for h in range(2):
                    which = side if h == 0 else 1 - side
                    put(far_refs[l][window(which, half), :], (l + 1) * words + h * half)

        prob = jnp.concatenate(
            [prob_ref[...]] + [jnp.exp(ref[...].astype(F32) - norm_ref[...]).astype(BF16) for ref in logit_refs],
            axis=0,
        )
        out_ref[...] = jnp.dot(turned[...], prob, preferred_element_type=F32)

    whole = lambda j, h: (0, 0)
    held = lambda j, h: (0, lax.rem(h[0], sizes.vocab) * blocks + j)
    column = lambda j, h: (0, j)
    return pl.pallas_call(
        kernel,
        out_shape=[jax.ShapeDtypeStruct((docs, share), F32), jax.ShapeDtypeStruct((8, 128), F32)],
        grid_spec=pltpu.PrefetchScalarGridSpec(
            num_scalar_prefetch=1,
            grid=(blocks,),
            in_specs=[pl.BlockSpec((words, docs), whole)] * count
            + [pl.BlockSpec((words, span), held)]
            + [pl.BlockSpec((half, span), column)] * (2 * far)
            + [pl.BlockSpec((1, span), held)],
            out_specs=[pl.BlockSpec((docs, span), column), pl.BlockSpec((8, 128), whole)],
            scratch_shapes=[pltpu.VMEM((docs, count * words), BF16)],
        ),
        compiler_params=call_params(),
        cost_estimate=cost(1, 1),
        name="theta_grad",
    )(here, ratio, *far_ratios, prob_held, *far_logits, log_norm)


def place_pieces(sizes, here, own, other, flips, shape):
    pieces = len(own)
    side_width = shape[1] // 2

    def kernel(here_ref, *refs):
        own_refs, other_refs, (out_ref, sems) = refs[:pieces], refs[pieces : 2 * pieces], refs[-2:]
        side, topic_at = sizes.side(here_ref), sizes.topic_at(here_ref)
        copies = []
        for p in range(pieces):
            rows = own_refs[p].shape[0] // len(flips[p])
            for h, (ref, which) in enumerate(((own_refs[p], side), (other_refs[p], 1 - side))):
                for i, flip in enumerate(flips[p]):
                    part = ref.at[pl.ds(i * rows, rows), :]
                    target = out_ref.at[window(topic_at ^ flip, rows), window(which, side_width)]
                    copies.append(pltpu.make_async_copy(part, target, sems.at[len(copies)]))
        for copy in copies:
            copy.start()
        for copy in copies:
            copy.wait()

    return pl.pallas_call(
        kernel,
        out_shape=jax.ShapeDtypeStruct(shape, BF16),
        in_specs=[SMEM] + [VMEM] * (2 * pieces),
        out_specs=HBM,
        scratch_shapes=[pltpu.SemaphoreType.DMA((2 * sum(map(len, flips)),))],
        compiler_params=call_params(),
        cost_estimate=cost(0, 4 * shape[0] * shape[1]),
        name="place_pieces",
    )(here, *own, *other)


def on_device(sizes, doc_topics, word_logits, log_norm, tile_doc, tile_word, word_counts):
    docs, width = doc_topics.shape
    words = word_logits.shape[0]
    word_tile = word_counts.shape[1]
    here = lax.axis_index(("doc", "topic", "vocab")).astype(jnp.int32)[None]

    def shift(array, by):
        return lax.ppermute(array, "vocab", [(i, (i + by) % sizes.vocab) for i in range(sizes.vocab)])

    def swap(array, axis, bits):
        count = {"doc": sizes.doc, "topic": sizes.topic}[axis]
        return lax.ppermute(array, axis, [(i, i ^ bits) for i in range(count)])

    parts, near_logits, docs_held, docs_sent, prob_held, norm_held = rate_partial(
        sizes, here, doc_topics, word_logits, log_norm[None, :]
    )
    sibling_docs = swap(docs_sent, "doc", 1)
    order = sorted(range(1, sizes.topic), key=lambda s: s < sizes.topic // 2)
    arrived = [swap(parts[s], "topic", s) for s in order]
    counts = chunk_counts(sizes, here, word_counts, tile_doc, tile_word, docs, words)
    own_ratio = ratio_chunk([parts[0]] + arrived, counts, word_tile)
    gathered = [swap(own_ratio, "topic", s) for s in order]
    near_logits = [shift(hold(part, gathered[:1]), s) for s, part in enumerate(near_logits, 1)]
    far_bits = [1 << b for b in range(1, sizes.doc.bit_length() - 1)]

    def beta(ratio, flips, after):
        pieces = beta_pieces(
            sizes, here, own_product(ratio, docs_held), swap(ratio, "doc", 1), sibling_docs, prob_held, flips, after
        )
        for bit in far_bits[:-1]:
            pieces = [add_pair(part, swap(part, "doc", bit)) for part in pieces]
        return [(part, swap(part, "doc", far_bits[-1])) for part in pieces]

    flips = [[0], order]
    pairs = beta(own_ratio, flips[:1], [])
    pairs += beta(stack_rows(gathered, []), flips[1:], [pairs[0][1]])

    ratio = join_ratio(sizes, here, [own_ratio] + gathered, [0] + order, [pairs[1][0]])
    far_ratios = [shift(ratio, s) for s in range(1, sizes.vocab)]
    far_logits = []
    for part in near_logits:
        part = hold(part, [pairs[1][0]])
        far_logits += [part, swap(part, "doc", 1)]
    theta, theta_done = theta_grad(sizes, here, ratio, far_ratios, prob_held, far_logits, norm_held)

    sums = [add_pair(*pair, [theta_done] if p else []) for p, pair in enumerate(pairs)]
    out = place_pieces(sizes, here, sums, [swap(part, "doc", 1) for part in sums], flips, word_logits.shape)
    return theta, out


def solution(mesh):
    placed = (
        P("doc", "topic"),
        P("vocab", "topic"),
        P("topic"),
        P(("doc", "vocab")),
        P(("doc", "vocab")),
        P(("doc", "vocab"), None, None),
    )
    return jax.shard_map(
        functools.partial(on_device, Sizes(mesh)),
        mesh=mesh,
        in_specs=placed,
        out_specs=(P("doc", ("topic", "vocab")), P("vocab", "topic")),
        check_vma=False,
    )
```

```python
import functools

import jax
import jax.numpy as jnp
from jax import lax
from jax.experimental import pallas as pl
from jax.experimental.pallas import tpu as pltpu
from jax.sharding import PartitionSpec as P

BF16 = jnp.bfloat16
F32 = jnp.float32
MIB = 1024 * 1024
HOLD_COST = 5 * 10**8
TURN_COST = 4 * 10**9
ANY = pl.BlockSpec(memory_space=pl.ANY)
HBM = pl.BlockSpec(memory_space=pltpu.HBM)
VMEM = pl.BlockSpec(memory_space=pltpu.VMEM)
SMEM = pl.BlockSpec(memory_space=pltpu.SMEM)


def call_params(mib=16):
    return pltpu.CompilerParams(vmem_limit_bytes=mib * MIB)


def cost(flops, bytes_accessed, transcendentals=0):
    return pl.CostEstimate(flops=flops, bytes_accessed=bytes_accessed, transcendentals=transcendentals)


def in_hbm(array):
    return pltpu.with_memory_space_constraint(array, pltpu.HBM)


def window(index, size):
    return pl.ds(pl.multiple_of(index * size, size), size)


class Sizes:
    def __init__(self, mesh):
        self.doc, self.topic, self.vocab = (mesh.shape[axis] for axis in ("doc", "topic", "vocab"))

    def vocab_at(self, here_ref):
        return lax.rem(here_ref[0], self.vocab)

    def topic_at(self, here_ref):
        return lax.rem(lax.div(here_ref[0], self.vocab), self.topic)

    def side(self, here_ref):
        return lax.rem(lax.div(here_ref[0], self.vocab * self.topic), 2)


def rate_partial(sizes, here, doc_topics, word_logits, log_norm):
    docs, width = doc_topics.shape
    words = word_logits.shape[0]
    side_width = width // 2
    span = min(side_width, 1024)
    steps = side_width // span
    count, far = sizes.topic, sizes.vocab - 1
    chunk, half, share = words // count, words // 2, width // sizes.vocab

    def kernel(here_ref, doc_in, logit_in, norm_in, *rest):
        parts, halves = rest[:count], rest[count : count + far]
        own_ref, sibling_ref, prob_ref, norm_ref, logit_ref, acc, sems, norm_sem = rest[count + far :]
        side = sizes.side(here_ref)
        norm_copy = pltpu.make_async_copy(norm_in, norm_ref, norm_sem)
        norm_copy.start()
        blocks = []
        for which, doc_ref in ((1 - side, sibling_ref), (side, own_ref)):
            for j in range(steps):
                at = window(which * steps + j, span)
                i = len(blocks)
                logit_copy = pltpu.make_async_copy(logit_in.at[:, at], logit_ref.at[:, at], sems.at[0, i])
                held = doc_ref.at[:, pl.ds(j * span, span)]
                doc_copy = pltpu.make_async_copy(doc_in.at[:, at], held, sems.at[1, i])
                blocks.append((at, logit_copy, doc_copy, held))
        for _, logit_copy, doc_copy, _ in blocks:
            logit_copy.start()
            doc_copy.start()
        norm_copy.wait()
        for i, (at, logit_copy, doc_copy, held) in enumerate(blocks):
            logit_copy.wait()
            prob = jnp.exp(logit_ref[:, at].astype(F32) - norm_ref[:, at]).astype(BF16)
            prob_ref[:, at] = prob
            doc_copy.wait()
            part = lax.dot_general(
                prob, held[...], (((1,), (1,)), ((), ())), preferred_element_type=F32
            )
            if i == 0:
                acc[...] = part
            else:
                acc[...] += part
        topic_at = sizes.topic_at(here_ref)
        for s in range(count):
            parts[s][...] = acc[window(topic_at ^ s, chunk), :].astype(BF16)
        rows = window(side, half)
        for s in range(far):
            target = lax.rem(sizes.vocab_at(here_ref) + s + 1, sizes.vocab)
            halves[s][...] = logit_ref[rows, window(target, share)]

    out = pl.pallas_call(
        kernel,
        out_shape=[jax.ShapeDtypeStruct((chunk, docs), BF16)] * count
        + [jax.ShapeDtypeStruct((half, share), BF16)] * far
        + [
            jax.ShapeDtypeStruct((docs, side_width), BF16),
            jax.ShapeDtypeStruct((docs, side_width), BF16),
            jax.ShapeDtypeStruct(word_logits.shape, BF16),
            jax.ShapeDtypeStruct(log_norm.shape, F32),
        ],
        in_specs=[SMEM, HBM, HBM, HBM],
        out_specs=[VMEM] * (count + far + 4),
        scratch_shapes=[
            pltpu.VMEM(word_logits.shape, BF16),
            pltpu.VMEM((words, docs), F32),
            pltpu.SemaphoreType.DMA((2, 2 * steps)),
            pltpu.SemaphoreType.DMA,
        ],
        compiler_params=call_params(),
        cost_estimate=cost(2 * words * docs * width, 2 * (words + docs) * width, words * width),
        name="rate_partial",
    )(here, in_hbm(doc_topics), in_hbm(word_logits), in_hbm(log_norm))
    return out[:count], out[count : count + far], *out[count + far :]


def chunk_counts(sizes, here, word_counts, tile_doc, tile_word, docs, words):
    slots, word_tile, doc_tile = word_counts.shape
    chunk = words // sizes.topic

    def kernel(here_ref, doc_at, word_at, count_ref, out_ref):
        first = sizes.topic_at(here_ref) * chunk
        block = first // word_tile
        row = pl.multiple_of(lax.rem(first, word_tile), chunk)
        out_ref[...] = jnp.zeros_like(out_ref)
        for s in range(slots):
            @pl.when(word_at[s] == block)
            def _():
                out_ref[:, window(doc_at[s], doc_tile)] = count_ref[s, pl.ds(row, chunk), :].astype(F32)

    return pl.pallas_call(
        kernel,
        out_shape=jax.ShapeDtypeStruct((chunk, docs), F32),
        in_specs=[SMEM, SMEM, SMEM, VMEM],
        out_specs=VMEM,
        compiler_params=call_params(),
        cost_estimate=cost(words * docs, 4 * words * docs),
        name="chunk_counts",
    )(here, in_hbm(tile_doc), in_hbm(tile_word), word_counts)


def ratio_chunk(parts, counts, word_tile):
    def kernel(*refs):
        part_refs, count_ref, out_ref = refs[:-2], refs[-2], refs[-1]
        rate = part_refs[0][...].astype(F32)
        for ref in part_refs[1:]:
            rate += ref[...].astype(F32)
        out_ref[...] = (count_ref[...] / (word_tile * rate)).astype(BF16)

    return pl.pallas_call(
        kernel,
        out_shape=jax.ShapeDtypeStruct(counts.shape, BF16),
        in_specs=[VMEM] * (len(parts) + 1),
        out_specs=VMEM,
        compiler_params=call_params(),
        cost_estimate=cost(10 * counts.size, 16 * counts.size),
        name="ratio_chunk",
    )(*parts, counts)


def join_ratio(sizes, here, chunks, order, after):
    rows, docs = chunks[0].shape
    count = sizes.topic

    def kernel(here_ref, *refs):
        topic_at = sizes.topic_at(here_ref)
        for s, ref in zip(order, refs):
            refs[-1][window(topic_at ^ s, rows), :] = ref[...]

    return pl.pallas_call(
        kernel,
        out_shape=jax.ShapeDtypeStruct((rows * count, docs), BF16),
        in_specs=[SMEM] + [VMEM] * count + [ANY] * len(after),
        out_specs=VMEM,
        compiler_params=call_params(),
        cost_estimate=cost(0, 4 * rows * docs * count),
        name="join_ratio",
    )(here, *chunks, *after)


def own_product(ratio, docs_held):
    words, docs = ratio.shape
    width = docs_held.shape[1]

    def kernel(ratio_ref, doc_ref, out_ref):
        out_ref[...] = jnp.dot(ratio_ref[...], doc_ref[...], preferred_element_type=F32)

    return pl.pallas_call(
        kernel,
        out_shape=jax.ShapeDtypeStruct((words, width), F32),
        in_specs=[VMEM, VMEM],
        out_specs=VMEM,
        compiler_params=call_params(),
        cost_estimate=cost(2 * words * docs * width, 2 * docs * width + 4 * words * width),
        name="own_product",
    )(ratio, docs_held)


def beta_piece(sizes, here, product, ratio, docs_held, prob_held, flips):
    words, side_width = product.shape
    docs = docs_held.shape[0]
    rows = words // len(flips)

    def kernel(here_ref, product_ref, ratio_ref, doc_ref, prob_ref, out_ref):
        columns = window(sizes.side(here_ref), side_width)
        topic_at = sizes.topic_at(here_ref)
        summed = product_ref[...] + jnp.dot(ratio_ref[...], doc_ref[...], preferred_element_type=F32)
        for i, flip in enumerate(flips):
            at = slice(i * rows, (i + 1) * rows)
            prob = prob_ref[window(topic_at ^ flip, rows), columns].astype(F32)
            out_ref[at, :] = (-prob * summed[at, :]).astype(BF16)

    return pl.pallas_call(
        kernel,
        out_shape=jax.ShapeDtypeStruct((words, side_width), BF16),
        in_specs=[SMEM] + [VMEM] * 4,
        out_specs=VMEM,
        compiler_params=call_params(),
        cost_estimate=cost(1, 1) if len(flips) > 1 else cost(2 * words * docs * side_width, 2 * (4 * words + docs) * side_width),
        name="beta_piece",
    )(here, product, ratio, docs_held, prob_held)


def stack_rows(parts, after):
    rows, docs = parts[0].shape

    def kernel(*refs):
        for i, ref in enumerate(refs[: len(parts)]):
            refs[-1][i * rows : (i + 1) * rows, :] = ref[...]

    return pl.pallas_call(
        kernel,
        out_shape=jax.ShapeDtypeStruct((len(parts) * rows, docs), BF16),
        in_specs=[VMEM] * len(parts) + [ANY] * len(after),
        out_specs=VMEM,
        compiler_params=call_params(),
        cost_estimate=cost(0, 4 * len(parts) * rows * docs),
        name="stack_rows",
    )(*parts, *after)


def add_pair(own, other, after=()):
    def kernel(own_ref, other_ref, *rest):
        rest[-1][...] = (own_ref[...].astype(F32) + other_ref[...].astype(F32)).astype(BF16)

    return pl.pallas_call(
        kernel,
        out_shape=jax.ShapeDtypeStruct(own.shape, BF16),
        in_specs=[VMEM, VMEM] + [ANY] * len(after),
        out_specs=VMEM,
        compiler_params=call_params(),
        cost_estimate=cost(own.size, 6 * own.size),
        name="add_pair",
    )(own, other, *after)


def hold(array, after, flops=1):
    def kernel(in_ref, *rest):
        rest[-1][...] = in_ref[...]

    return pl.pallas_call(
        kernel,
        out_shape=jax.ShapeDtypeStruct(array.shape, array.dtype),
        in_specs=[VMEM] + [ANY] * len(after),
        out_specs=VMEM,
        compiler_params=call_params(),
        cost_estimate=cost(flops, 4 * array.size),
        name="hold",
    )(array, *after)


def turn_ratios(sizes, here, ratio, far_ratios):
    words, docs = ratio.shape
    half = words // 2
    count = 1 + len(far_ratios)

    def kernel(here_ref, *refs):
        side = sizes.side(here_ref)
        for l, (ref, out_ref) in enumerate(zip(refs[:count], refs[count:])):
            for h, which in enumerate((side, 1 - side) if l else (0, 1)):
                rows = ref[window(which, half), :].astype(F32)
                out_ref[:, h * half : (h + 1) * half] = (-rows).T.astype(BF16)

    return pl.pallas_call(
        kernel,
        out_shape=[jax.ShapeDtypeStruct((docs, words), BF16)] * count,
        in_specs=[SMEM] + [VMEM] * count,
        out_specs=[VMEM] * count,
        compiler_params=call_params(),
        cost_estimate=cost(TURN_COST, 1),
        name="turn_ratios",
    )(here, ratio, *far_ratios)


def theta_grad(sizes, here, turned, prob_held, far_logits, log_norm):
    docs, words = turned[0].shape
    half = words // 2
    share = far_logits[0].shape[1]
    count = len(turned)
    span = min(share, 512)
    blocks = share // span

    def kernel(here_ref, *refs):
        turned_refs, prob_ref = refs[:count], refs[count]
        logit_refs, norm_ref = refs[count + 1 : 3 * count - 1], refs[3 * count - 1]
        out_ref, done_ref = refs[-2:]
        done_ref[...] = jnp.zeros_like(done_ref)
        summed = jnp.dot(turned_refs[0][...], prob_ref[...], preferred_element_type=F32)
        for l in range(count - 1):
            pair = logit_refs[2 * l : 2 * l + 2]
            prob = jnp.concatenate([jnp.exp(ref[...].astype(F32) - norm_ref[...]).astype(BF16) for ref in pair], axis=0)
            summed += jnp.dot(turned_refs[l + 1][...], prob, preferred_element_type=F32)
        out_ref[...] = summed

    whole = lambda j, h: (0, 0)
    held = lambda j, h: (0, lax.rem(h[0], sizes.vocab) * blocks + j)
    column = lambda j, h: (0, j)
    return pl.pallas_call(
        kernel,
        out_shape=[jax.ShapeDtypeStruct((docs, share), F32), jax.ShapeDtypeStruct((8, 128), F32)],
        grid_spec=pltpu.PrefetchScalarGridSpec(
            num_scalar_prefetch=1,
            grid=(blocks,),
            in_specs=[pl.BlockSpec((docs, words), whole)] * count
            + [pl.BlockSpec((words, span), held)]
            + [pl.BlockSpec((half, span), column)] * (2 * count - 2)
            + [pl.BlockSpec((1, span), held)],
            out_specs=[pl.BlockSpec((docs, span), column), pl.BlockSpec((8, 128), whole)],
        ),
        compiler_params=call_params(16),
        cost_estimate=cost(1, 1),
        name="theta_grad",
    )(here, *turned, prob_held, *far_logits, log_norm)


def place_pieces(sizes, here, own, other, flips, shape):
    pieces = len(own)
    side_width = shape[1] // 2

    def kernel(here_ref, *refs):
        own_refs, other_refs, (out_ref, sems) = refs[:pieces], refs[pieces : 2 * pieces], refs[-2:]
        side, topic_at = sizes.side(here_ref), sizes.topic_at(here_ref)
        copies = []
        for p in range(pieces):
            rows = own_refs[p].shape[0] // len(flips[p])
            for h, (ref, which) in enumerate(((own_refs[p], side), (other_refs[p], 1 - side))):
                for i, flip in enumerate(flips[p]):
                    part = ref.at[pl.ds(i * rows, rows), :]
                    target = out_ref.at[window(topic_at ^ flip, rows), window(which, side_width)]
                    copies.append(pltpu.make_async_copy(part, target, sems.at[len(copies)]))
        for copy in copies:
            copy.start()
        for copy in copies:
            copy.wait()

    return pl.pallas_call(
        kernel,
        out_shape=jax.ShapeDtypeStruct(shape, BF16),
        in_specs=[SMEM] + [VMEM] * (2 * pieces),
        out_specs=HBM,
        scratch_shapes=[pltpu.SemaphoreType.DMA((2 * sum(map(len, flips)),))],
        compiler_params=call_params(),
        cost_estimate=cost(0, 4 * shape[0] * shape[1]),
        name="place_pieces",
    )(here, *own, *other)


def on_device(sizes, doc_topics, word_logits, log_norm, tile_doc, tile_word, word_counts):
    docs, width = doc_topics.shape
    words = word_logits.shape[0]
    word_tile = word_counts.shape[1]
    here = lax.axis_index(("doc", "topic", "vocab")).astype(jnp.int32)[None]

    def shift(array, by):
        return lax.ppermute(array, "vocab", [(i, (i + by) % sizes.vocab) for i in range(sizes.vocab)])

    def swap(array, axis, bits):
        count = {"doc": sizes.doc, "topic": sizes.topic}[axis]
        return lax.ppermute(array, axis, [(i, i ^ bits) for i in range(count)])

    parts, near_logits, docs_held, docs_sent, prob_held, norm_held = rate_partial(
        sizes, here, doc_topics, word_logits, log_norm[None, :]
    )
    sibling_docs = swap(docs_sent, "doc", 1)
    order = sorted(range(1, sizes.topic), key=lambda s: s < sizes.topic // 2)
    arrived = [swap(parts[s], "topic", s) for s in order]
    counts = chunk_counts(sizes, here, word_counts, tile_doc, tile_word, docs, words)
    own_ratio = ratio_chunk([parts[0]] + arrived, counts, word_tile)
    gathered = [swap(own_ratio, "topic", s) for s in order]
    far_bits = [1 << b for b in range(1, sizes.doc.bit_length() - 1)]

    def beta(ratio, flips, after):
        part = beta_piece(sizes, here, own_product(ratio, docs_held), swap(ratio, "doc", 1), sibling_docs, prob_held, flips)
        for bit in far_bits[:-1]:
            part = add_pair(part, swap(part, "doc", bit))
        return part, swap(hold(part, after, HOLD_COST) if after else part, "doc", far_bits[-1])

    flips = [[0], order]
    pairs = [beta(own_ratio, flips[0], [])]
    near_logits = [shift(hold(part, gathered[:1]), s) for s, part in enumerate(near_logits, 1)]
    pairs.append(beta(stack_rows(gathered, []), flips[1], [pairs[0][1]]))

    ratio = join_ratio(sizes, here, [own_ratio] + gathered, [0] + order, [pairs[1][0]])
    far_ratios = [shift(ratio, s) for s in range(1, sizes.vocab)]
    far_logits = []
    for part in near_logits:
        part = hold(part, [pairs[1][0]])
        far_logits += [part, swap(part, "doc", 1)]
    turned = turn_ratios(sizes, here, ratio, far_ratios)
    theta, theta_done = theta_grad(sizes, here, turned, prob_held, far_logits, norm_held)

    sums = [add_pair(*pair, [theta_done] if p else []) for p, pair in enumerate(pairs)]
    out = place_pieces(sizes, here, sums, [swap(part, "doc", 1) for part in sums], flips, word_logits.shape)
    return theta, out


def solution(mesh):
    placed = (
        P("doc", "topic"),
        P("vocab", "topic"),
        P("topic"),
        P(("doc", "vocab")),
        P(("doc", "vocab")),
        P(("doc", "vocab"), None, None),
    )
    return jax.shard_map(
        functools.partial(on_device, Sizes(mesh)),
        mesh=mesh,
        in_specs=placed,
        out_specs=(P("doc", ("topic", "vocab")), P("vocab", "topic")),
        check_vma=False,
    )
```

```python
import functools

import jax
import jax.numpy as jnp
from jax import lax
from jax.experimental import pallas as pl
from jax.experimental.pallas import tpu as pltpu
from jax.sharding import PartitionSpec as P

BF16 = jnp.bfloat16
F32 = jnp.float32
MIB = 1024 * 1024
HOLD_COST = 15 * 10**7
TURN_COST = 10**9
ANY = pl.BlockSpec(memory_space=pl.ANY)
HBM = pl.BlockSpec(memory_space=pltpu.HBM)
VMEM = pl.BlockSpec(memory_space=pltpu.VMEM)
SMEM = pl.BlockSpec(memory_space=pltpu.SMEM)


def call_params(mib=16):
    return pltpu.CompilerParams(vmem_limit_bytes=mib * MIB)


def cost(flops, bytes_accessed, transcendentals=0):
    return pl.CostEstimate(flops=flops, bytes_accessed=bytes_accessed, transcendentals=transcendentals)


def in_hbm(array):
    return pltpu.with_memory_space_constraint(array, pltpu.HBM)


def window(index, size):
    return pl.ds(pl.multiple_of(index * size, size), size)


class Sizes:
    def __init__(self, mesh):
        self.doc, self.topic, self.vocab = (mesh.shape[axis] for axis in ("doc", "topic", "vocab"))

    def vocab_at(self, here_ref):
        return lax.rem(here_ref[0], self.vocab)

    def topic_at(self, here_ref):
        return lax.rem(lax.div(here_ref[0], self.vocab), self.topic)

    def side(self, here_ref):
        return lax.rem(lax.div(here_ref[0], self.vocab * self.topic), 2)


def rate_partial(sizes, here, doc_topics, word_logits, log_norm):
    docs, width = doc_topics.shape
    words = word_logits.shape[0]
    side_width = width // 2
    span = min(side_width, 1024)
    steps = side_width // span
    count, far = sizes.topic, sizes.vocab - 1
    chunk, half, share = words // count, words // 2, width // sizes.vocab

    def kernel(here_ref, doc_in, logit_in, norm_in, *rest):
        parts, halves = rest[:count], rest[count : count + far]
        own_ref, sibling_ref, prob_ref, norm_ref, logit_ref, acc, sems, norm_sem = rest[count + far :]
        side = sizes.side(here_ref)
        norm_copy = pltpu.make_async_copy(norm_in, norm_ref, norm_sem)
        norm_copy.start()
        blocks = []
        for which, doc_ref in ((1 - side, sibling_ref), (side, own_ref)):
            for j in range(steps):
                at = window(which * steps + j, span)
                i = len(blocks)
                logit_copy = pltpu.make_async_copy(logit_in.at[:, at], logit_ref.at[:, at], sems.at[0, i])
                held = doc_ref.at[:, pl.ds(j * span, span)]
                doc_copy = pltpu.make_async_copy(doc_in.at[:, at], held, sems.at[1, i])
                blocks.append((at, logit_copy, doc_copy, held))
        for _, logit_copy, doc_copy, _ in blocks:
            logit_copy.start()
            doc_copy.start()
        norm_copy.wait()
        for i, (at, logit_copy, doc_copy, held) in enumerate(blocks):
            logit_copy.wait()
            prob = jnp.exp(logit_ref[:, at].astype(F32) - norm_ref[:, at]).astype(BF16)
            prob_ref[:, at] = prob
            doc_copy.wait()
            part = lax.dot_general(
                prob, held[...], (((1,), (1,)), ((), ())), preferred_element_type=F32
            )
            if i == 0:
                acc[...] = part
            else:
                acc[...] += part
        topic_at = sizes.topic_at(here_ref)
        for s in range(count):
            parts[s][...] = acc[window(topic_at ^ s, chunk), :].astype(BF16)
        rows = window(side, half)
        for s in range(far):
            target = lax.rem(sizes.vocab_at(here_ref) + s + 1, sizes.vocab)
            halves[s][...] = logit_ref[rows, window(target, share)]

    out = pl.pallas_call(
        kernel,
        out_shape=[jax.ShapeDtypeStruct((chunk, docs), BF16)] * count
        + [jax.ShapeDtypeStruct((half, share), BF16)] * far
        + [
            jax.ShapeDtypeStruct((docs, side_width), BF16),
            jax.ShapeDtypeStruct((docs, side_width), BF16),
            jax.ShapeDtypeStruct(word_logits.shape, BF16),
            jax.ShapeDtypeStruct(log_norm.shape, F32),
        ],
        in_specs=[SMEM, HBM, HBM, HBM],
        out_specs=[VMEM] * (count + far + 4),
        scratch_shapes=[
            pltpu.VMEM(word_logits.shape, BF16),
            pltpu.VMEM((words, docs), F32),
            pltpu.SemaphoreType.DMA((2, 2 * steps)),
            pltpu.SemaphoreType.DMA,
        ],
        compiler_params=call_params(),
        cost_estimate=cost(2 * words * docs * width, 2 * (words + docs) * width, words * width),
        name="rate_partial",
    )(here, in_hbm(doc_topics), in_hbm(word_logits), in_hbm(log_norm))
    return out[:count], out[count : count + far], *out[count + far :]


def chunk_counts(sizes, here, word_counts, tile_doc, tile_word, docs, words):
    slots, word_tile, doc_tile = word_counts.shape
    chunk = words // sizes.topic

    def kernel(here_ref, doc_at, word_at, count_ref, out_ref):
        first = sizes.topic_at(here_ref) * chunk
        block = first // word_tile
        row = pl.multiple_of(lax.rem(first, word_tile), chunk)
        out_ref[...] = jnp.zeros_like(out_ref)
        for s in range(slots):
            @pl.when(word_at[s] == block)
            def _():
                out_ref[:, window(doc_at[s], doc_tile)] = count_ref[s, pl.ds(row, chunk), :].astype(F32)

    return pl.pallas_call(
        kernel,
        out_shape=jax.ShapeDtypeStruct((chunk, docs), F32),
        in_specs=[SMEM, SMEM, SMEM, VMEM],
        out_specs=VMEM,
        compiler_params=call_params(),
        cost_estimate=cost(words * docs, 4 * words * docs),
        name="chunk_counts",
    )(here, in_hbm(tile_doc), in_hbm(tile_word), word_counts)


def ratio_chunk(parts, counts, word_tile):
    def kernel(*refs):
        part_refs, count_ref, out_ref = refs[:-2], refs[-2], refs[-1]
        rate = part_refs[0][...].astype(F32)
        for ref in part_refs[1:]:
            rate += ref[...].astype(F32)
        out_ref[...] = (count_ref[...] / (word_tile * rate)).astype(BF16)

    return pl.pallas_call(
        kernel,
        out_shape=jax.ShapeDtypeStruct(counts.shape, BF16),
        in_specs=[VMEM] * (len(parts) + 1),
        out_specs=VMEM,
        compiler_params=call_params(),
        cost_estimate=cost(10 * counts.size, 16 * counts.size),
        name="ratio_chunk",
    )(*parts, counts)


def join_ratio(sizes, here, chunks, order, after):
    rows, docs = chunks[0].shape
    count = sizes.topic

    def kernel(here_ref, *refs):
        topic_at = sizes.topic_at(here_ref)
        for s, ref in zip(order, refs):
            refs[-1][window(topic_at ^ s, rows), :] = ref[...]

    return pl.pallas_call(
        kernel,
        out_shape=jax.ShapeDtypeStruct((rows * count, docs), BF16),
        in_specs=[SMEM] + [VMEM] * count + [ANY] * len(after),
        out_specs=VMEM,
        compiler_params=call_params(),
        cost_estimate=cost(0, 4 * rows * docs * count),
        name="join_ratio",
    )(here, *chunks, *after)


def own_product(ratio, docs_held):
    words, docs = ratio.shape
    width = docs_held.shape[1]

    def kernel(ratio_ref, doc_ref, out_ref):
        out_ref[...] = jnp.dot(ratio_ref[...], doc_ref[...], preferred_element_type=F32)

    return pl.pallas_call(
        kernel,
        out_shape=jax.ShapeDtypeStruct((words, width), F32),
        in_specs=[VMEM, VMEM],
        out_specs=VMEM,
        compiler_params=call_params(),
        cost_estimate=cost(2 * words * docs * width, 2 * docs * width + 4 * words * width),
        name="own_product",
    )(ratio, docs_held)


def beta_pieces(sizes, here, product, ratio, docs_held, prob_held, flips):
    words, side_width = product.shape
    docs = docs_held.shape[0]
    rows = words // sum(map(len, flips))

    def kernel(here_ref, product_ref, ratio_ref, doc_ref, prob_ref, *out_refs):
        columns = window(sizes.side(here_ref), side_width)
        topic_at = sizes.topic_at(here_ref)
        summed = product_ref[...] + jnp.dot(ratio_ref[...], doc_ref[...], preferred_element_type=F32)
        chunk = 0
        for piece, out_ref in zip(flips, out_refs):
            for i, flip in enumerate(piece):
                prob = prob_ref[window(topic_at ^ flip, rows), columns].astype(F32)
                part = summed[chunk * rows : (chunk + 1) * rows, :]
                out_ref[i * rows : (i + 1) * rows, :] = (-prob * part).astype(BF16)
                chunk += 1

    return pl.pallas_call(
        kernel,
        out_shape=[jax.ShapeDtypeStruct((rows * len(piece), side_width), BF16) for piece in flips],
        in_specs=[SMEM] + [VMEM] * 4,
        out_specs=[VMEM] * len(flips),
        compiler_params=call_params(),
        cost_estimate=cost(2 * words * docs * side_width, 2 * (4 * words + docs) * side_width),
        name="beta_pieces",
    )(here, product, ratio, docs_held, prob_held)


def stack_rows(parts, after):
    rows, docs = parts[0].shape

    def kernel(*refs):
        for i, ref in enumerate(refs[: len(parts)]):
            refs[-1][i * rows : (i + 1) * rows, :] = ref[...]

    return pl.pallas_call(
        kernel,
        out_shape=jax.ShapeDtypeStruct((len(parts) * rows, docs), BF16),
        in_specs=[VMEM] * len(parts) + [ANY] * len(after),
        out_specs=VMEM,
        compiler_params=call_params(),
        cost_estimate=cost(0, 4 * len(parts) * rows * docs),
        name="stack_rows",
    )(*parts, *after)


def cut_rows(array, count, after):
    rows, width = array.shape[0] // count, array.shape[1]

    def kernel(in_ref, *rest):
        for i, out_ref in enumerate(rest[len(after) :]):
            out_ref[...] = in_ref[i * rows : (i + 1) * rows, :]

    return pl.pallas_call(
        kernel,
        out_shape=[jax.ShapeDtypeStruct((rows, width), array.dtype)] * count,
        in_specs=[VMEM] + [ANY] * len(after),
        out_specs=[VMEM] * count,
        compiler_params=call_params(),
        cost_estimate=cost(0, 4 * array.size),
        name="cut_rows",
    )(array, *after)


def add_pair(own, other, after=()):
    def kernel(own_ref, other_ref, *rest):
        rest[-1][...] = (own_ref[...].astype(F32) + other_ref[...].astype(F32)).astype(BF16)

    return pl.pallas_call(
        kernel,
        out_shape=jax.ShapeDtypeStruct(own.shape, BF16),
        in_specs=[VMEM, VMEM] + [ANY] * len(after),
        out_specs=VMEM,
        compiler_params=call_params(),
        cost_estimate=cost(own.size, 6 * own.size),
        name="add_pair",
    )(own, other, *after)


def hold(array, after, flops=1):
    def kernel(in_ref, *rest):
        rest[-1][...] = in_ref[...]

    return pl.pallas_call(
        kernel,
        out_shape=jax.ShapeDtypeStruct(array.shape, array.dtype),
        in_specs=[VMEM] + [ANY] * len(after),
        out_specs=VMEM,
        compiler_params=call_params(),
        cost_estimate=cost(flops, 4 * array.size),
        name="hold",
    )(array, *after)


def turn_ratios(sizes, here, ratio, far_ratios):
    words, docs = ratio.shape
    half = words // 2
    count = 1 + len(far_ratios)

    def kernel(here_ref, *refs):
        side = sizes.side(here_ref)
        for l, (ref, out_ref) in enumerate(zip(refs[:count], refs[count:])):
            for h, which in enumerate((side, 1 - side) if l else (0, 1)):
                rows = ref[window(which, half), :].astype(F32)
                out_ref[:, h * half : (h + 1) * half] = (-rows).T.astype(BF16)

    return pl.pallas_call(
        kernel,
        out_shape=[jax.ShapeDtypeStruct((docs, words), BF16)] * count,
        in_specs=[SMEM] + [VMEM] * count,
        out_specs=[VMEM] * count,
        compiler_params=call_params(),
        cost_estimate=cost(TURN_COST, 1),
        name="turn_ratios",
    )(here, ratio, *far_ratios)


def theta_grad(sizes, here, turned, prob_held, far_logits, log_norm):
    docs, words = turned[0].shape
    cuts = len(far_logits[0])
    rows, share = far_logits[0][0].shape
    count = len(turned)
    span = min(share, 512)
    blocks = share // span

    def kernel(here_ref, *refs):
        turned_refs, prob_ref = refs[:count], refs[count]
        logit_refs, norm_ref = refs[count + 1 : -3], refs[-3]
        out_ref, done_ref = refs[-2:]
        done_ref[...] = jnp.zeros_like(done_ref)
        summed = jnp.dot(turned_refs[0][...], prob_ref[...], preferred_element_type=F32)
        for l in range(count - 1):
            part = logit_refs[cuts * l : cuts * (l + 1)]
            prob = jnp.concatenate([jnp.exp(ref[...].astype(F32) - norm_ref[...]).astype(BF16) for ref in part], axis=0)
            summed += jnp.dot(turned_refs[l + 1][...], prob, preferred_element_type=F32)
        out_ref[...] = summed

    whole = lambda j, h: (0, 0)
    held = lambda j, h: (0, lax.rem(h[0], sizes.vocab) * blocks + j)
    column = lambda j, h: (0, j)
    return pl.pallas_call(
        kernel,
        out_shape=[jax.ShapeDtypeStruct((docs, share), F32), jax.ShapeDtypeStruct((8, 128), F32)],
        grid_spec=pltpu.PrefetchScalarGridSpec(
            num_scalar_prefetch=1,
            grid=(blocks,),
            in_specs=[pl.BlockSpec((docs, words), whole)] * count
            + [pl.BlockSpec((words, span), held)]
            + [pl.BlockSpec((rows, span), column)] * (cuts * (count - 1))
            + [pl.BlockSpec((1, span), held)],
            out_specs=[pl.BlockSpec((docs, span), column), pl.BlockSpec((8, 128), whole)],
        ),
        compiler_params=call_params(16),
        cost_estimate=cost(1, 1),
        name="theta_grad",
    )(here, *turned, prob_held, *sum(far_logits, []), log_norm)


def place_pieces(sizes, here, own, other, flips, shape):
    pieces = len(own)
    side_width = shape[1] // 2

    def kernel(here_ref, *refs):
        own_refs, other_refs, (out_ref, sems) = refs[:pieces], refs[pieces : 2 * pieces], refs[-2:]
        side, topic_at = sizes.side(here_ref), sizes.topic_at(here_ref)
        copies = []
        for p in range(pieces):
            rows = own_refs[p].shape[0] // len(flips[p])
            for h, (ref, which) in enumerate(((own_refs[p], side), (other_refs[p], 1 - side))):
                for i, flip in enumerate(flips[p]):
                    part = ref.at[pl.ds(i * rows, rows), :]
                    target = out_ref.at[window(topic_at ^ flip, rows), window(which, side_width)]
                    copies.append(pltpu.make_async_copy(part, target, sems.at[len(copies)]))
        for copy in copies:
            copy.start()
        for copy in copies:
            copy.wait()

    return pl.pallas_call(
        kernel,
        out_shape=jax.ShapeDtypeStruct(shape, BF16),
        in_specs=[SMEM] + [VMEM] * (2 * pieces),
        out_specs=HBM,
        scratch_shapes=[pltpu.SemaphoreType.DMA((2 * sum(map(len, flips)),))],
        compiler_params=call_params(),
        cost_estimate=cost(0, 4 * shape[0] * shape[1]),
        name="place_pieces",
    )(here, *own, *other)


def on_device(sizes, doc_topics, word_logits, log_norm, tile_doc, tile_word, word_counts):
    docs, width = doc_topics.shape
    words = word_logits.shape[0]
    word_tile = word_counts.shape[1]
    here = lax.axis_index(("doc", "topic", "vocab")).astype(jnp.int32)[None]

    def shift(array, by):
        return lax.ppermute(array, "vocab", [(i, (i + by) % sizes.vocab) for i in range(sizes.vocab)])

    def swap(array, axis, bits):
        count = {"doc": sizes.doc, "topic": sizes.topic}[axis]
        return lax.ppermute(array, axis, [(i, i ^ bits) for i in range(count)])

    parts, near_logits, docs_held, docs_sent, prob_held, norm_held = rate_partial(
        sizes, here, doc_topics, word_logits, log_norm[None, :]
    )
    sibling_docs = swap(docs_sent, "doc", 1)
    order = sorted(range(1, sizes.topic), key=lambda s: s < sizes.topic // 2)
    arrived = [swap(parts[s], "topic", s) for s in order]
    counts = chunk_counts(sizes, here, word_counts, tile_doc, tile_word, docs, words)
    own_ratio = ratio_chunk([parts[0]] + arrived, counts, word_tile)
    order.reverse()
    gathered = [swap(own_ratio, "topic", s) for s in order]
    far_bits = [1 << b for b in range(1, sizes.doc.bit_length() - 1)]

    def beta(ratio, flips, after):
        pieces = beta_pieces(
            sizes, here, own_product(ratio, docs_held), swap(ratio, "doc", 1), sibling_docs, prob_held, flips
        )
        for bit in far_bits[:-1]:
            pieces = [add_pair(part, swap(part, "doc", bit)) for part in pieces]
        sent = [hold(pieces[0], after, HOLD_COST) if after else pieces[0], *pieces[1:]]
        return [(part, swap(copy, "doc", far_bits[-1])) for part, copy in zip(pieces, sent)]

    flips = [[0]] + [piece for piece in (order[:-1], order[-1:]) if piece]
    pairs = beta(own_ratio, flips[:1], [])
    near_logits = [shift(hold(part, gathered[-1:]), s) for s, part in enumerate(near_logits, 1)]
    pairs += beta(stack_rows(gathered, []), flips[1:], [pairs[0][1]])

    ratio = join_ratio(sizes, here, [own_ratio] + gathered, [0] + order, [pairs[1][0]])
    far_ratios = [shift(ratio, s) for s in range(1, sizes.vocab)]
    far_logits = []
    for part in near_logits:
        pieces = list(cut_rows(part, 2, [pairs[1][0]]))
        far_logits.append(pieces + [swap(piece, "doc", 1) for piece in pieces])
    turned = turn_ratios(sizes, here, ratio, far_ratios)
    theta, theta_done = theta_grad(sizes, here, turned, prob_held, far_logits, norm_held)

    sums = [add_pair(*pair, [theta_done] if p else []) for p, pair in enumerate(pairs)]
    out = place_pieces(sizes, here, sums, [swap(part, "doc", 1) for part in sums], flips, word_logits.shape)
    return theta, out


def solution(mesh):
    placed = (
        P("doc", "topic"),
        P("vocab", "topic"),
        P("topic"),
        P(("doc", "vocab")),
        P(("doc", "vocab")),
        P(("doc", "vocab"), None, None),
    )
    return jax.shard_map(
        functools.partial(on_device, Sizes(mesh)),
        mesh=mesh,
        in_specs=placed,
        out_specs=(P("doc", ("topic", "vocab")), P("vocab", "topic")),
        check_vma=False,
    )
```

```python
import functools

import jax
import jax.numpy as jnp
from jax import lax
from jax.experimental import pallas as pl
from jax.experimental.pallas import tpu as pltpu
from jax.sharding import PartitionSpec as P

BF16 = jnp.bfloat16
F32 = jnp.float32
MIB = 1024 * 1024
HOLD_COST = 15 * 10**7
TURN_COST = 10**9
ANY = pl.BlockSpec(memory_space=pl.ANY)
HBM = pl.BlockSpec(memory_space=pltpu.HBM)
VMEM = pl.BlockSpec(memory_space=pltpu.VMEM)
SMEM = pl.BlockSpec(memory_space=pltpu.SMEM)


def call_params(mib=16):
    return pltpu.CompilerParams(vmem_limit_bytes=mib * MIB)


def cost(flops, bytes_accessed, transcendentals=0):
    return pl.CostEstimate(flops=flops, bytes_accessed=bytes_accessed, transcendentals=transcendentals)


def in_hbm(array):
    return pltpu.with_memory_space_constraint(array, pltpu.HBM)


def window(index, size):
    return pl.ds(pl.multiple_of(index * size, size), size)


class Sizes:
    def __init__(self, mesh):
        self.doc, self.topic, self.vocab = (mesh.shape[axis] for axis in ("doc", "topic", "vocab"))

    def vocab_at(self, here_ref):
        return lax.rem(here_ref[0], self.vocab)

    def topic_at(self, here_ref):
        return lax.rem(lax.div(here_ref[0], self.vocab), self.topic)

    def side(self, here_ref):
        return lax.rem(lax.div(here_ref[0], self.vocab * self.topic), 2)


def rate_partial(sizes, here, doc_topics, word_logits, log_norm):
    docs, width = doc_topics.shape
    words = word_logits.shape[0]
    side_width = width // 2
    span = min(side_width, 512)
    steps = side_width // span
    count, far = sizes.topic, sizes.vocab - 1
    chunk, half, share = words // count, words // 2, width // sizes.vocab

    def kernel(here_ref, doc_in, logit_in, norm_in, *rest):
        parts, halves = rest[:count], rest[count : count + far]
        own_ref, sibling_ref, prob_ref, norm_ref, logit_ref, acc, sems, norm_sem = rest[count + far :]
        side = sizes.side(here_ref)
        norm_copy = pltpu.make_async_copy(norm_in, norm_ref, norm_sem)
        norm_copy.start()

        def block(which, doc_ref, h, j):
            at = window(which * steps + j, span)
            held = doc_ref.at[:, window(j, span)]
            logit_copy = pltpu.make_async_copy(logit_in.at[:, at], logit_ref.at[:, at], sems.at[0, h * steps + j])
            return at, held, logit_copy, pltpu.make_async_copy(doc_in.at[:, at], held, sems.at[1, h * steps + j])

        sides = ((1 - side, sibling_ref), (side, own_ref))
        for h, (which, doc_ref) in enumerate(sides):
            @pl.loop(0, steps)
            def _(j):
                _, _, logit_copy, doc_copy = block(which, doc_ref, h, j)
                logit_copy.start()
                doc_copy.start()

        acc[...] = jnp.zeros_like(acc)
        norm_copy.wait()
        for h, (which, doc_ref) in enumerate(sides):
            @pl.loop(0, steps)
            def _(j):
                at, held, logit_copy, doc_copy = block(which, doc_ref, h, j)
                logit_copy.wait()
                prob = jnp.exp(logit_ref[:, at].astype(F32) - norm_ref[:, at]).astype(BF16)
                prob_ref[:, at] = prob
                doc_copy.wait()
                acc[...] += lax.dot_general(
                    prob, held[...], (((1,), (1,)), ((), ())), preferred_element_type=F32
                )

        topic_at = sizes.topic_at(here_ref)
        for s in range(count):
            parts[s][...] = acc[window(topic_at ^ s, chunk), :].astype(BF16)
        rows = window(side, half)
        for s in range(far):
            target = lax.rem(sizes.vocab_at(here_ref) + s + 1, sizes.vocab)
            halves[s][...] = logit_ref[rows, window(target, share)]

    out = pl.pallas_call(
        kernel,
        out_shape=[jax.ShapeDtypeStruct((chunk, docs), BF16)] * count
        + [jax.ShapeDtypeStruct((half, share), BF16)] * far
        + [
            jax.ShapeDtypeStruct((docs, side_width), BF16),
            jax.ShapeDtypeStruct((docs, side_width), BF16),
            jax.ShapeDtypeStruct(word_logits.shape, BF16),
            jax.ShapeDtypeStruct(log_norm.shape, F32),
        ],
        in_specs=[SMEM, HBM, HBM, HBM],
        out_specs=[VMEM] * (count + far + 4),
        scratch_shapes=[
            pltpu.VMEM(word_logits.shape, BF16),
            pltpu.VMEM((words, docs), F32),
            pltpu.SemaphoreType.DMA((2, 2 * steps)),
            pltpu.SemaphoreType.DMA,
        ],
        compiler_params=call_params(),
        cost_estimate=cost(2 * words * docs * width, 2 * (words + docs) * width, words * width),
        name="rate_partial",
    )(here, in_hbm(doc_topics), in_hbm(word_logits), in_hbm(log_norm))
    return out[:count], out[count : count + far], *out[count + far :]


def chunk_counts(sizes, here, word_counts, tile_doc, tile_word, docs, words):
    slots, word_tile, doc_tile = word_counts.shape
    chunk = words // sizes.topic

    def kernel(here_ref, doc_at, word_at, count_ref, out_ref):
        first = sizes.topic_at(here_ref) * chunk
        block = first // word_tile
        row = pl.multiple_of(lax.rem(first, word_tile), chunk)
        out_ref[...] = jnp.zeros_like(out_ref)
        for s in range(slots):
            @pl.when(word_at[s] == block)
            def _():
                out_ref[:, window(doc_at[s], doc_tile)] = count_ref[s, pl.ds(row, chunk), :].astype(F32)

    return pl.pallas_call(
        kernel,
        out_shape=jax.ShapeDtypeStruct((chunk, docs), F32),
        in_specs=[SMEM, SMEM, SMEM, VMEM],
        out_specs=VMEM,
        compiler_params=call_params(),
        cost_estimate=cost(words * docs, 4 * words * docs),
        name="chunk_counts",
    )(here, in_hbm(tile_doc), in_hbm(tile_word), word_counts)


def ratio_chunk(parts, counts, word_tile):
    def kernel(*refs):
        part_refs, count_ref, out_ref = refs[:-2], refs[-2], refs[-1]
        rate = part_refs[0][...].astype(F32)
        for ref in part_refs[1:]:
            rate += ref[...].astype(F32)
        out_ref[...] = (count_ref[...] / (word_tile * rate)).astype(BF16)

    return pl.pallas_call(
        kernel,
        out_shape=jax.ShapeDtypeStruct(counts.shape, BF16),
        in_specs=[VMEM] * (len(parts) + 1),
        out_specs=VMEM,
        compiler_params=call_params(),
        cost_estimate=cost(10 * counts.size, 16 * counts.size),
        name="ratio_chunk",
    )(*parts, counts)


def join_ratio(sizes, here, chunks, order, after):
    rows, docs = chunks[0].shape
    count = sizes.topic

    def kernel(here_ref, *refs):
        topic_at = sizes.topic_at(here_ref)
        for s, ref in zip(order, refs):
            refs[-1][window(topic_at ^ s, rows), :] = ref[...]

    return pl.pallas_call(
        kernel,
        out_shape=jax.ShapeDtypeStruct((rows * count, docs), BF16),
        in_specs=[SMEM] + [VMEM] * count + [ANY] * len(after),
        out_specs=VMEM,
        compiler_params=call_params(),
        cost_estimate=cost(0, 4 * rows * docs * count),
        name="join_ratio",
    )(here, *chunks, *after)


def own_product(ratio, docs_held):
    words, docs = ratio.shape
    width = docs_held.shape[1]

    def kernel(ratio_ref, doc_ref, out_ref):
        out_ref[...] = jnp.dot(ratio_ref[...], doc_ref[...], preferred_element_type=F32)

    return pl.pallas_call(
        kernel,
        out_shape=jax.ShapeDtypeStruct((words, width), F32),
        in_specs=[VMEM, VMEM],
        out_specs=VMEM,
        compiler_params=call_params(),
        cost_estimate=cost(2 * words * docs * width, 2 * docs * width + 4 * words * width),
        name="own_product",
    )(ratio, docs_held)


def beta_pieces(sizes, here, product, ratio, docs_held, prob_held, flips):
    words, side_width = product.shape
    docs = docs_held.shape[0]
    rows = words // sum(map(len, flips))

    def kernel(here_ref, product_ref, ratio_ref, doc_ref, prob_ref, *out_refs):
        columns = window(sizes.side(here_ref), side_width)
        topic_at = sizes.topic_at(here_ref)
        summed = product_ref[...] + jnp.dot(ratio_ref[...], doc_ref[...], preferred_element_type=F32)
        chunk = 0
        for piece, out_ref in zip(flips, out_refs):
            for i, flip in enumerate(piece):
                prob = prob_ref[window(topic_at ^ flip, rows), columns].astype(F32)
                part = summed[chunk * rows : (chunk + 1) * rows, :]
                out_ref[i * rows : (i + 1) * rows, :] = (-prob * part).astype(BF16)
                chunk += 1

    return pl.pallas_call(
        kernel,
        out_shape=[jax.ShapeDtypeStruct((rows * len(piece), side_width), BF16) for piece in flips],
        in_specs=[SMEM] + [VMEM] * 4,
        out_specs=[VMEM] * len(flips),
        compiler_params=call_params(),
        cost_estimate=cost(2 * words * docs * side_width, 2 * (4 * words + docs) * side_width),
        name="beta_pieces",
    )(here, product, ratio, docs_held, prob_held)


def stack_rows(parts, after):
    rows, docs = parts[0].shape

    def kernel(*refs):
        for i, ref in enumerate(refs[: len(parts)]):
            refs[-1][i * rows : (i + 1) * rows, :] = ref[...]

    return pl.pallas_call(
        kernel,
        out_shape=jax.ShapeDtypeStruct((len(parts) * rows, docs), BF16),
        in_specs=[VMEM] * len(parts) + [ANY] * len(after),
        out_specs=VMEM,
        compiler_params=call_params(),
        cost_estimate=cost(0, 4 * len(parts) * rows * docs),
        name="stack_rows",
    )(*parts, *after)


def cut_rows(array, count, after):
    rows, width = array.shape[0] // count, array.shape[1]

    def kernel(in_ref, *rest):
        for i, out_ref in enumerate(rest[len(after) :]):
            out_ref[...] = in_ref[i * rows : (i + 1) * rows, :]

    return pl.pallas_call(
        kernel,
        out_shape=[jax.ShapeDtypeStruct((rows, width), array.dtype)] * count,
        in_specs=[VMEM] + [ANY] * len(after),
        out_specs=[VMEM] * count,
        compiler_params=call_params(),
        cost_estimate=cost(0, 4 * array.size),
        name="cut_rows",
    )(array, *after)


def add_pair(own, other, after=()):
    def kernel(own_ref, other_ref, *rest):
        rest[-1][...] = (own_ref[...].astype(F32) + other_ref[...].astype(F32)).astype(BF16)

    return pl.pallas_call(
        kernel,
        out_shape=jax.ShapeDtypeStruct(own.shape, BF16),
        in_specs=[VMEM, VMEM] + [ANY] * len(after),
        out_specs=VMEM,
        compiler_params=call_params(),
        cost_estimate=cost(own.size, 6 * own.size),
        name="add_pair",
    )(own, other, *after)


def hold(array, after, flops=1):
    def kernel(in_ref, *rest):
        rest[-1][...] = in_ref[...]

    return pl.pallas_call(
        kernel,
        out_shape=jax.ShapeDtypeStruct(array.shape, array.dtype),
        in_specs=[VMEM] + [ANY] * len(after),
        out_specs=VMEM,
        compiler_params=call_params(),
        cost_estimate=cost(flops, 4 * array.size),
        name="hold",
    )(array, *after)


def turn_ratios(sizes, here, ratio, far_ratios):
    words, docs = ratio.shape
    half = words // 2
    count = 1 + len(far_ratios)

    def kernel(here_ref, *refs):
        side = sizes.side(here_ref)
        for l, (ref, out_ref) in enumerate(zip(refs[:count], refs[count:])):
            for h, which in enumerate((side, 1 - side) if l else (0, 1)):
                rows = ref[window(which, half), :].astype(F32)
                out_ref[:, h * half : (h + 1) * half] = (-rows).T.astype(BF16)

    return pl.pallas_call(
        kernel,
        out_shape=[jax.ShapeDtypeStruct((docs, words), BF16)] * count,
        in_specs=[SMEM] + [VMEM] * count,
        out_specs=[VMEM] * count,
        compiler_params=call_params(),
        cost_estimate=cost(TURN_COST, 1),
        name="turn_ratios",
    )(here, ratio, *far_ratios)


def theta_grad(sizes, here, turned, prob_held, far_logits, log_norm):
    docs, words = turned[0].shape
    cuts = len(far_logits[0])
    rows, share = far_logits[0][0].shape
    count = len(turned)
    span = min(share, 512)
    blocks = share // span

    def kernel(here_ref, *refs):
        turned_refs, prob_ref = refs[:count], refs[count]
        logit_refs, norm_ref = refs[count + 1 : -3], refs[-3]
        out_ref, done_ref = refs[-2:]
        done_ref[...] = jnp.zeros_like(done_ref)
        summed = jnp.dot(turned_refs[0][...], prob_ref[...], preferred_element_type=F32)
        for l in range(count - 1):
            part = logit_refs[cuts * l : cuts * (l + 1)]
            prob = jnp.concatenate([jnp.exp(ref[...].astype(F32) - norm_ref[...]).astype(BF16) for ref in part], axis=0)
            summed += jnp.dot(turned_refs[l + 1][...], prob, preferred_element_type=F32)
        out_ref[...] = summed

    whole = lambda j, h: (0, 0)
    held = lambda j, h: (0, lax.rem(h[0], sizes.vocab) * blocks + j)
    column = lambda j, h: (0, j)
    return pl.pallas_call(
        kernel,
        out_shape=[jax.ShapeDtypeStruct((docs, share), F32), jax.ShapeDtypeStruct((8, 128), F32)],
        grid_spec=pltpu.PrefetchScalarGridSpec(
            num_scalar_prefetch=1,
            grid=(blocks,),
            in_specs=[pl.BlockSpec((docs, words), whole)] * count
            + [pl.BlockSpec((words, span), held)]
            + [pl.BlockSpec((rows, span), column)] * (cuts * (count - 1))
            + [pl.BlockSpec((1, span), held)],
            out_specs=[pl.BlockSpec((docs, span), column), pl.BlockSpec((8, 128), whole)],
        ),
        compiler_params=call_params(16),
        cost_estimate=cost(1, 1),
        name="theta_grad",
    )(here, *turned, prob_held, *sum(far_logits, []), log_norm)


def place_pieces(sizes, here, own, other, flips, shape):
    pieces = len(own)
    side_width = shape[1] // 2

    def kernel(here_ref, *refs):
        own_refs, other_refs, (out_ref, sems) = refs[:pieces], refs[pieces : 2 * pieces], refs[-2:]
        side, topic_at = sizes.side(here_ref), sizes.topic_at(here_ref)
        copies = []
        for p in range(pieces):
            rows = own_refs[p].shape[0] // len(flips[p])
            for h, (ref, which) in enumerate(((own_refs[p], side), (other_refs[p], 1 - side))):
                for i, flip in enumerate(flips[p]):
                    part = ref.at[pl.ds(i * rows, rows), :]
                    target = out_ref.at[window(topic_at ^ flip, rows), window(which, side_width)]
                    copies.append(pltpu.make_async_copy(part, target, sems.at[len(copies)]))
        for copy in copies:
            copy.start()
        for copy in copies:
            copy.wait()

    return pl.pallas_call(
        kernel,
        out_shape=jax.ShapeDtypeStruct(shape, BF16),
        in_specs=[SMEM] + [VMEM] * (2 * pieces),
        out_specs=HBM,
        scratch_shapes=[pltpu.SemaphoreType.DMA((2 * sum(map(len, flips)),))],
        compiler_params=call_params(),
        cost_estimate=cost(0, 4 * shape[0] * shape[1]),
        name="place_pieces",
    )(here, *own, *other)


def on_device(sizes, doc_topics, word_logits, log_norm, tile_doc, tile_word, word_counts):
    docs, width = doc_topics.shape
    words = word_logits.shape[0]
    word_tile = word_counts.shape[1]
    here = lax.axis_index(("doc", "topic", "vocab")).astype(jnp.int32)[None]

    def shift(array, by):
        return lax.ppermute(array, "vocab", [(i, (i + by) % sizes.vocab) for i in range(sizes.vocab)])

    def swap(array, axis, bits):
        count = {"doc": sizes.doc, "topic": sizes.topic}[axis]
        return lax.ppermute(array, axis, [(i, i ^ bits) for i in range(count)])

    parts, near_logits, docs_held, docs_sent, prob_held, norm_held = rate_partial(
        sizes, here, doc_topics, word_logits, log_norm[None, :]
    )
    sibling_docs = swap(docs_sent, "doc", 1)
    order = sorted(range(1, sizes.topic), key=lambda s: s < sizes.topic // 2)
    arrived = [swap(parts[s], "topic", s) for s in order]
    counts = chunk_counts(sizes, here, word_counts, tile_doc, tile_word, docs, words)
    own_ratio = ratio_chunk([parts[0]] + arrived, counts, word_tile)
    order.reverse()
    gathered = [swap(own_ratio, "topic", s) for s in order]
    far_bits = [1 << b for b in range(1, sizes.doc.bit_length() - 1)]

    def beta(ratio, flips, after):
        pieces = beta_pieces(
            sizes, here, own_product(ratio, docs_held), swap(ratio, "doc", 1), sibling_docs, prob_held, flips
        )
        for bit in far_bits[:-1]:
            pieces = [add_pair(part, swap(part, "doc", bit)) for part in pieces]
        sent = [hold(pieces[0], after, HOLD_COST) if after else pieces[0], *pieces[1:]]
        return [(part, swap(copy, "doc", far_bits[-1])) for part, copy in zip(pieces, sent)]

    flips = [[0]] + [piece for piece in (order[:-1], order[-1:]) if piece]
    pairs = beta(own_ratio, flips[:1], [])
    near_logits = [shift(hold(part, gathered[-1:]), s) for s, part in enumerate(near_logits, 1)]
    pairs += beta(stack_rows(gathered, []), flips[1:], [pairs[0][1]])

    ratio = join_ratio(sizes, here, [own_ratio] + gathered, [0] + order, [pairs[1][0]])
    far_ratios = [shift(ratio, s) for s in range(1, sizes.vocab)]
    far_logits = []
    for part in near_logits:
        pieces = list(cut_rows(part, 2, [pairs[1][0]]))
        far_logits.append(pieces + [swap(piece, "doc", 1) for piece in pieces])
    turned = turn_ratios(sizes, here, ratio, far_ratios)
    theta, theta_done = theta_grad(sizes, here, turned, prob_held, far_logits, norm_held)

    sums = [add_pair(*pair, [theta_done] if p else []) for p, pair in enumerate(pairs)]
    out = place_pieces(sizes, here, sums, [swap(part, "doc", 1) for part in sums], flips, word_logits.shape)
    return theta, out


def solution(mesh):
    placed = (
        P("doc", "topic"),
        P("vocab", "topic"),
        P("topic"),
        P(("doc", "vocab")),
        P(("doc", "vocab")),
        P(("doc", "vocab"), None, None),
    )
    return jax.shard_map(
        functools.partial(on_device, Sizes(mesh)),
        mesh=mesh,
        in_specs=placed,
        out_specs=(P("doc", ("topic", "vocab")), P("vocab", "topic")),
        check_vma=False,
    )
```

```python
import functools

import jax
import jax.numpy as jnp
from jax import lax
from jax.experimental import pallas as pl
from jax.experimental.pallas import tpu as pltpu
from jax.sharding import PartitionSpec as P

BF16 = jnp.bfloat16
F32 = jnp.float32
MIB = 1024 * 1024
HOLD_COST = 15 * 10**7
TURN_COST = 10**9
ANY = pl.BlockSpec(memory_space=pl.ANY)
HBM = pl.BlockSpec(memory_space=pltpu.HBM)
VMEM = pl.BlockSpec(memory_space=pltpu.VMEM)
SMEM = pl.BlockSpec(memory_space=pltpu.SMEM)


def call_params(mib=16):
    return pltpu.CompilerParams(vmem_limit_bytes=mib * MIB)


def cost(flops, bytes_accessed, transcendentals=0):
    return pl.CostEstimate(flops=flops, bytes_accessed=bytes_accessed, transcendentals=transcendentals)


def in_hbm(array):
    return pltpu.with_memory_space_constraint(array, pltpu.HBM)


def window(index, size):
    return pl.ds(pl.multiple_of(index * size, size), size)


class Sizes:
    def __init__(self, mesh):
        self.doc, self.topic, self.vocab = (mesh.shape[axis] for axis in ("doc", "topic", "vocab"))

    def vocab_at(self, here_ref):
        return lax.rem(here_ref[0], self.vocab)

    def topic_at(self, here_ref):
        return lax.rem(lax.div(here_ref[0], self.vocab), self.topic)

    def side(self, here_ref):
        return lax.rem(lax.div(here_ref[0], self.vocab * self.topic), 2)


def rate_partial(sizes, here, doc_topics, word_logits, log_norm):
    docs, width = doc_topics.shape
    words = word_logits.shape[0]
    side_width = width // 2
    word_rows, doc_rows = words // 4, min(docs, 256)
    steps = docs // doc_rows
    count, far = sizes.topic, sizes.vocab - 1
    chunk, half, share = words // count, words // 2, width // sizes.vocab

    def kernel(here_ref, doc_in, logit_in, norm_in, *rest):
        parts, halves = rest[:count], rest[count : count + far]
        own_ref, sibling_ref, prob_ref, norm_ref, logit_ref, acc, logit_sems, doc_sems, norm_sem = rest[count + far :]
        side = sizes.side(here_ref)
        sides = ((0, 1 - side, sibling_ref), (1, side, own_ref))

        def logit_copy(i):
            at = window(i, word_rows)
            return pltpu.make_async_copy(logit_in.at[at, :], logit_ref.at[at, :], logit_sems.at[i])

        def doc_copy(h, which, doc_ref, i):
            at = window(i, doc_rows)
            return pltpu.make_async_copy(
                doc_in.at[at, window(which, side_width)], doc_ref.at[at, :], doc_sems.at[h, i]
            )

        norm_copy = pltpu.make_async_copy(norm_in, norm_ref, norm_sem)
        norm_copy.start()
        for i in range(words // word_rows):
            logit_copy(i).start()
        for i in range(steps):
            for h, which, doc_ref in sides:
                doc_copy(h, which, doc_ref, i).start()
        norm_copy.wait()

        @pl.loop(0, words // word_rows)
        def _(i):
            logit_copy(i).wait()
            at = window(i, word_rows)
            prob_ref[at, :] = jnp.exp(logit_ref[at, :].astype(F32) - norm_ref[...]).astype(BF16)

        topic_at = sizes.topic_at(here_ref)

        @pl.loop(0, steps)
        def _(i):
            at = window(i, doc_rows)
            rate = None
            for h, which, doc_ref in sides:
                doc_copy(h, which, doc_ref, i).wait()
                part = lax.dot_general(
                    prob_ref[:, window(which, side_width)],
                    doc_ref[at, :],
                    (((1,), (1,)), ((), ())),
                    preferred_element_type=F32,
                )
                rate = part if rate is None else rate + part
            acc[:, at] = rate

        for s in range(count):
            parts[s][...] = acc[window(topic_at ^ s, chunk), :].astype(BF16)
        rows = window(side, half)
        for s in range(far):
            target = lax.rem(sizes.vocab_at(here_ref) + s + 1, sizes.vocab)
            halves[s][...] = logit_ref[rows, window(target, share)]

    out = pl.pallas_call(
        kernel,
        out_shape=[jax.ShapeDtypeStruct((chunk, docs), BF16)] * count
        + [jax.ShapeDtypeStruct((half, share), BF16)] * far
        + [
            jax.ShapeDtypeStruct((docs, side_width), BF16),
            jax.ShapeDtypeStruct((docs, side_width), BF16),
            jax.ShapeDtypeStruct(word_logits.shape, BF16),
            jax.ShapeDtypeStruct(log_norm.shape, F32),
        ],
        in_specs=[SMEM, HBM, HBM, HBM],
        out_specs=[VMEM] * (count + far + 4),
        scratch_shapes=[
            pltpu.VMEM(word_logits.shape, BF16),
            pltpu.VMEM((words, docs), F32),
            pltpu.SemaphoreType.DMA((words // word_rows,)),
            pltpu.SemaphoreType.DMA((2, steps)),
            pltpu.SemaphoreType.DMA,
        ],
        compiler_params=call_params(),
        cost_estimate=cost(2 * words * docs * width, 2 * (words + docs) * width, words * width),
        name="rate_partial",
    )(here, in_hbm(doc_topics), in_hbm(word_logits), in_hbm(log_norm))
    return out[:count], out[count : count + far], *out[count + far :]


def chunk_counts(sizes, here, word_counts, tile_doc, tile_word, docs, words):
    slots, word_tile, doc_tile = word_counts.shape
    chunk = words // sizes.topic

    def kernel(here_ref, doc_at, word_at, count_ref, out_ref):
        first = sizes.topic_at(here_ref) * chunk
        block = first // word_tile
        row = pl.multiple_of(lax.rem(first, word_tile), chunk)
        out_ref[...] = jnp.zeros_like(out_ref)
        for s in range(slots):
            @pl.when(word_at[s] == block)
            def _():
                out_ref[:, window(doc_at[s], doc_tile)] = count_ref[s, pl.ds(row, chunk), :].astype(F32)

    return pl.pallas_call(
        kernel,
        out_shape=jax.ShapeDtypeStruct((chunk, docs), F32),
        in_specs=[SMEM, SMEM, SMEM, VMEM],
        out_specs=VMEM,
        compiler_params=call_params(),
        cost_estimate=cost(words * docs, 4 * words * docs),
        name="chunk_counts",
    )(here, in_hbm(tile_doc), in_hbm(tile_word), word_counts)


def ratio_chunk(parts, counts, word_tile):
    def kernel(*refs):
        part_refs, count_ref, out_ref = refs[:-2], refs[-2], refs[-1]
        rate = part_refs[0][...].astype(F32)
        for ref in part_refs[1:]:
            rate += ref[...].astype(F32)
        out_ref[...] = (count_ref[...] / (word_tile * rate)).astype(BF16)

    return pl.pallas_call(
        kernel,
        out_shape=jax.ShapeDtypeStruct(counts.shape, BF16),
        in_specs=[VMEM] * (len(parts) + 1),
        out_specs=VMEM,
        compiler_params=call_params(),
        cost_estimate=cost(10 * counts.size, 16 * counts.size),
        name="ratio_chunk",
    )(*parts, counts)


def join_ratio(sizes, here, chunks, order, after):
    rows, docs = chunks[0].shape
    count = sizes.topic

    def kernel(here_ref, *refs):
        topic_at = sizes.topic_at(here_ref)
        for s, ref in zip(order, refs):
            refs[-1][window(topic_at ^ s, rows), :] = ref[...]

    return pl.pallas_call(
        kernel,
        out_shape=jax.ShapeDtypeStruct((rows * count, docs), BF16),
        in_specs=[SMEM] + [VMEM] * count + [ANY] * len(after),
        out_specs=VMEM,
        compiler_params=call_params(),
        cost_estimate=cost(0, 4 * rows * docs * count),
        name="join_ratio",
    )(here, *chunks, *after)


def own_product(ratio, docs_held):
    words, docs = ratio.shape
    width = docs_held.shape[1]

    def kernel(ratio_ref, doc_ref, out_ref):
        out_ref[...] = jnp.dot(ratio_ref[...], doc_ref[...], preferred_element_type=F32)

    return pl.pallas_call(
        kernel,
        out_shape=jax.ShapeDtypeStruct((words, width), F32),
        in_specs=[VMEM, VMEM],
        out_specs=VMEM,
        compiler_params=call_params(),
        cost_estimate=cost(2 * words * docs * width, 2 * docs * width + 4 * words * width),
        name="own_product",
    )(ratio, docs_held)


def beta_pieces(sizes, here, product, ratio, docs_held, prob_held, flips):
    words, side_width = product.shape
    docs = docs_held.shape[0]
    rows = words // sum(map(len, flips))

    def kernel(here_ref, product_ref, ratio_ref, doc_ref, prob_ref, *out_refs):
        columns = window(sizes.side(here_ref), side_width)
        topic_at = sizes.topic_at(here_ref)
        summed = product_ref[...] + jnp.dot(ratio_ref[...], doc_ref[...], preferred_element_type=F32)
        chunk = 0
        for piece, out_ref in zip(flips, out_refs):
            for i, flip in enumerate(piece):
                prob = prob_ref[window(topic_at ^ flip, rows), columns].astype(F32)
                part = summed[chunk * rows : (chunk + 1) * rows, :]
                out_ref[i * rows : (i + 1) * rows, :] = (-prob * part).astype(BF16)
                chunk += 1

    return pl.pallas_call(
        kernel,
        out_shape=[jax.ShapeDtypeStruct((rows * len(piece), side_width), BF16) for piece in flips],
        in_specs=[SMEM] + [VMEM] * 4,
        out_specs=[VMEM] * len(flips),
        compiler_params=call_params(),
        cost_estimate=cost(2 * words * docs * side_width, 2 * (4 * words + docs) * side_width),
        name="beta_pieces",
    )(here, product, ratio, docs_held, prob_held)


def stack_rows(parts, after):
    rows, docs = parts[0].shape

    def kernel(*refs):
        for i, ref in enumerate(refs[: len(parts)]):
            refs[-1][i * rows : (i + 1) * rows, :] = ref[...]

    return pl.pallas_call(
        kernel,
        out_shape=jax.ShapeDtypeStruct((len(parts) * rows, docs), BF16),
        in_specs=[VMEM] * len(parts) + [ANY] * len(after),
        out_specs=VMEM,
        compiler_params=call_params(),
        cost_estimate=cost(0, 4 * len(parts) * rows * docs),
        name="stack_rows",
    )(*parts, *after)


def cut_rows(array, count, after):
    rows, width = array.shape[0] // count, array.shape[1]

    def kernel(in_ref, *rest):
        for i, out_ref in enumerate(rest[len(after) :]):
            out_ref[...] = in_ref[i * rows : (i + 1) * rows, :]

    return pl.pallas_call(
        kernel,
        out_shape=[jax.ShapeDtypeStruct((rows, width), array.dtype)] * count,
        in_specs=[VMEM] + [ANY] * len(after),
        out_specs=[VMEM] * count,
        compiler_params=call_params(),
        cost_estimate=cost(0, 4 * array.size),
        name="cut_rows",
    )(array, *after)


def add_pair(own, other, after=()):
    def kernel(own_ref, other_ref, *rest):
        rest[-1][...] = (own_ref[...].astype(F32) + other_ref[...].astype(F32)).astype(BF16)

    return pl.pallas_call(
        kernel,
        out_shape=jax.ShapeDtypeStruct(own.shape, BF16),
        in_specs=[VMEM, VMEM] + [ANY] * len(after),
        out_specs=VMEM,
        compiler_params=call_params(),
        cost_estimate=cost(own.size, 6 * own.size),
        name="add_pair",
    )(own, other, *after)


def hold(array, after, flops=1):
    def kernel(in_ref, *rest):
        rest[-1][...] = in_ref[...]

    return pl.pallas_call(
        kernel,
        out_shape=jax.ShapeDtypeStruct(array.shape, array.dtype),
        in_specs=[VMEM] + [ANY] * len(after),
        out_specs=VMEM,
        compiler_params=call_params(),
        cost_estimate=cost(flops, 4 * array.size),
        name="hold",
    )(array, *after)


def turn_ratios(sizes, here, ratio, far_ratios):
    words, docs = ratio.shape
    half = words // 2
    count = 1 + len(far_ratios)

    def kernel(here_ref, *refs):
        side = sizes.side(here_ref)
        for l, (ref, out_ref) in enumerate(zip(refs[:count], refs[count:])):
            for h, which in enumerate((side, 1 - side) if l else (0, 1)):
                rows = ref[window(which, half), :].astype(F32)
                out_ref[:, h * half : (h + 1) * half] = (-rows).T.astype(BF16)

    return pl.pallas_call(
        kernel,
        out_shape=[jax.ShapeDtypeStruct((docs, words), BF16)] * count,
        in_specs=[SMEM] + [VMEM] * count,
        out_specs=[VMEM] * count,
        compiler_params=call_params(),
        cost_estimate=cost(TURN_COST, 1),
        name="turn_ratios",
    )(here, ratio, *far_ratios)


def theta_grad(sizes, here, turned, prob_held, far_logits, log_norm):
    docs, words = turned[0].shape
    cuts = len(far_logits[0])
    rows, share = far_logits[0][0].shape
    count = len(turned)
    span = min(share, 512)
    blocks = share // span

    def kernel(here_ref, *refs):
        turned_refs, prob_ref = refs[:count], refs[count]
        logit_refs, norm_ref = refs[count + 1 : -3], refs[-3]
        out_ref, done_ref = refs[-2:]
        done_ref[...] = jnp.zeros_like(done_ref)
        summed = jnp.dot(turned_refs[0][...], prob_ref[...], preferred_element_type=F32)
        for l in range(count - 1):
            part = logit_refs[cuts * l : cuts * (l + 1)]
            prob = jnp.concatenate([jnp.exp(ref[...].astype(F32) - norm_ref[...]).astype(BF16) for ref in part], axis=0)
            summed += jnp.dot(turned_refs[l + 1][...], prob, preferred_element_type=F32)
        out_ref[...] = summed

    whole = lambda j, h: (0, 0)
    held = lambda j, h: (0, lax.rem(h[0], sizes.vocab) * blocks + j)
    column = lambda j, h: (0, j)
    return pl.pallas_call(
        kernel,
        out_shape=[jax.ShapeDtypeStruct((docs, share), F32), jax.ShapeDtypeStruct((8, 128), F32)],
        grid_spec=pltpu.PrefetchScalarGridSpec(
            num_scalar_prefetch=1,
            grid=(blocks,),
            in_specs=[pl.BlockSpec((docs, words), whole)] * count
            + [pl.BlockSpec((words, span), held)]
            + [pl.BlockSpec((rows, span), column)] * (cuts * (count - 1))
            + [pl.BlockSpec((1, span), held)],
            out_specs=[pl.BlockSpec((docs, span), column), pl.BlockSpec((8, 128), whole)],
        ),
        compiler_params=call_params(16),
        cost_estimate=cost(1, 1),
        name="theta_grad",
    )(here, *turned, prob_held, *sum(far_logits, []), log_norm)


def place_pieces(sizes, here, own, other, flips, shape):
    pieces = len(own)
    side_width = shape[1] // 2

    def kernel(here_ref, *refs):
        own_refs, other_refs, (out_ref, sems) = refs[:pieces], refs[pieces : 2 * pieces], refs[-2:]
        side, topic_at = sizes.side(here_ref), sizes.topic_at(here_ref)
        copies = []
        for p in range(pieces):
            rows = own_refs[p].shape[0] // len(flips[p])
            for h, (ref, which) in enumerate(((own_refs[p], side), (other_refs[p], 1 - side))):
                for i, flip in enumerate(flips[p]):
                    part = ref.at[pl.ds(i * rows, rows), :]
                    target = out_ref.at[window(topic_at ^ flip, rows), window(which, side_width)]
                    copies.append(pltpu.make_async_copy(part, target, sems.at[len(copies)]))
        for copy in copies:
            copy.start()
        for copy in copies:
            copy.wait()

    return pl.pallas_call(
        kernel,
        out_shape=jax.ShapeDtypeStruct(shape, BF16),
        in_specs=[SMEM] + [VMEM] * (2 * pieces),
        out_specs=HBM,
        scratch_shapes=[pltpu.SemaphoreType.DMA((2 * sum(map(len, flips)),))],
        compiler_params=call_params(),
        cost_estimate=cost(0, 4 * shape[0] * shape[1]),
        name="place_pieces",
    )(here, *own, *other)


def on_device(sizes, doc_topics, word_logits, log_norm, tile_doc, tile_word, word_counts):
    docs, width = doc_topics.shape
    words = word_logits.shape[0]
    word_tile = word_counts.shape[1]
    here = lax.axis_index(("doc", "topic", "vocab")).astype(jnp.int32)[None]

    def shift(array, by):
        return lax.ppermute(array, "vocab", [(i, (i + by) % sizes.vocab) for i in range(sizes.vocab)])

    def swap(array, axis, bits):
        count = {"doc": sizes.doc, "topic": sizes.topic}[axis]
        return lax.ppermute(array, axis, [(i, i ^ bits) for i in range(count)])

    parts, near_logits, docs_held, docs_sent, prob_held, norm_held = rate_partial(
        sizes, here, doc_topics, word_logits, log_norm[None, :]
    )
    sibling_docs = swap(docs_sent, "doc", 1)
    order = sorted(range(1, sizes.topic), key=lambda s: s < sizes.topic // 2)
    arrived = [swap(parts[s], "topic", s) for s in order]
    counts = chunk_counts(sizes, here, word_counts, tile_doc, tile_word, docs, words)
    own_ratio = ratio_chunk([parts[0]] + arrived, counts, word_tile)
    order.reverse()
    gathered = [swap(own_ratio, "topic", s) for s in order]
    far_bits = [1 << b for b in range(1, sizes.doc.bit_length() - 1)]

    def beta(ratio, flips, after):
        pieces = beta_pieces(
            sizes, here, own_product(ratio, docs_held), swap(ratio, "doc", 1), sibling_docs, prob_held, flips
        )
        for bit in far_bits[:-1]:
            pieces = [add_pair(part, swap(part, "doc", bit)) for part in pieces]
        sent = [hold(pieces[0], after, HOLD_COST) if after else pieces[0], *pieces[1:]]
        return [(part, swap(copy, "doc", far_bits[-1])) for part, copy in zip(pieces, sent)]

    flips = [[0]] + [piece for piece in (order[:-1], order[-1:]) if piece]
    pairs = beta(own_ratio, flips[:1], [])
    near_logits = [shift(hold(part, gathered[-1:]), s) for s, part in enumerate(near_logits, 1)]
    pairs += beta(stack_rows(gathered, []), flips[1:], [pairs[0][1]])

    ratio = join_ratio(sizes, here, [own_ratio] + gathered, [0] + order, [pairs[1][0]])
    far_ratios = [shift(ratio, s) for s in range(1, sizes.vocab)]
    far_logits = []
    for part in near_logits:
        pieces = list(cut_rows(part, 2, [pairs[1][0]]))
        far_logits.append(pieces + [swap(piece, "doc", 1) for piece in pieces])
    turned = turn_ratios(sizes, here, ratio, far_ratios)
    theta, theta_done = theta_grad(sizes, here, turned, prob_held, far_logits, norm_held)

    sums = [add_pair(*pair, [theta_done] if p else []) for p, pair in enumerate(pairs)]
    out = place_pieces(sizes, here, sums, [swap(part, "doc", 1) for part in sums], flips, word_logits.shape)
    return theta, out


def solution(mesh):
    placed = (
        P("doc", "topic"),
        P("vocab", "topic"),
        P("topic"),
        P(("doc", "vocab")),
        P(("doc", "vocab")),
        P(("doc", "vocab"), None, None),
    )
    return jax.shard_map(
        functools.partial(on_device, Sizes(mesh)),
        mesh=mesh,
        in_specs=placed,
        out_specs=(P("doc", ("topic", "vocab")), P("vocab", "topic")),
        check_vma=False,
    )
```

```python
import functools

import jax
import jax.numpy as jnp
from jax import lax
from jax.experimental import pallas as pl
from jax.experimental.pallas import tpu as pltpu
from jax.sharding import PartitionSpec as P

BF16 = jnp.bfloat16
F32 = jnp.float32
MIB = 1024 * 1024
ADD_COST = 22 * 10**8
KERNEL_COST = 125 * 10**7
TURN_COST = 10**9
ANY = pl.BlockSpec(memory_space=pl.ANY)
HBM = pl.BlockSpec(memory_space=pltpu.HBM)
VMEM = pl.BlockSpec(memory_space=pltpu.VMEM)
SMEM = pl.BlockSpec(memory_space=pltpu.SMEM)


def call_params(mib=16):
    return pltpu.CompilerParams(vmem_limit_bytes=mib * MIB)


def cost(flops, bytes_accessed, transcendentals=0):
    return pl.CostEstimate(flops=flops, bytes_accessed=bytes_accessed, transcendentals=transcendentals)


def in_hbm(array):
    return pltpu.with_memory_space_constraint(array, pltpu.HBM)


def window(index, size):
    return pl.ds(pl.multiple_of(index * size, size), size)


class Sizes:
    def __init__(self, mesh):
        self.doc, self.topic, self.vocab = (mesh.shape[axis] for axis in ("doc", "topic", "vocab"))

    def vocab_at(self, here_ref):
        return lax.rem(here_ref[0], self.vocab)

    def topic_at(self, here_ref):
        return lax.rem(lax.div(here_ref[0], self.vocab), self.topic)

    def side(self, here_ref):
        return lax.rem(lax.div(here_ref[0], self.vocab * self.topic), 2)


def rate_partial(sizes, here, doc_topics, word_logits, log_norm):
    docs, width = doc_topics.shape
    words = word_logits.shape[0]
    side_width = width // 2
    span = min(side_width, 512)
    steps = side_width // span
    count, far = sizes.topic, sizes.vocab - 1
    chunk, half, share = words // count, words // 2, width // sizes.vocab

    def kernel(here_ref, doc_in, logit_in, norm_in, *rest):
        parts, halves = rest[:count], rest[count : count + far]
        own_ref, sibling_ref, prob_ref, norm_ref, logit_ref, acc, sems, norm_sem = rest[count + far :]
        side = sizes.side(here_ref)
        norm_copy = pltpu.make_async_copy(norm_in, norm_ref, norm_sem)
        norm_copy.start()

        def block(which, doc_ref, h, j):
            at = window(which * steps + j, span)
            held = doc_ref.at[:, window(j, span)]
            logit_copy = pltpu.make_async_copy(logit_in.at[:, at], logit_ref.at[:, at], sems.at[0, h * steps + j])
            return at, held, logit_copy, pltpu.make_async_copy(doc_in.at[:, at], held, sems.at[1, h * steps + j])

        sides = ((1 - side, sibling_ref), (side, own_ref))
        for h, (which, doc_ref) in enumerate(sides):
            @pl.loop(0, steps)
            def _(j):
                _, _, logit_copy, doc_copy = block(which, doc_ref, h, j)
                logit_copy.start()
                doc_copy.start()

        acc[...] = jnp.zeros_like(acc)
        norm_copy.wait()
        for h, (which, doc_ref) in enumerate(sides):
            @pl.loop(0, steps)
            def _(j):
                at, held, logit_copy, doc_copy = block(which, doc_ref, h, j)
                logit_copy.wait()
                prob = jnp.exp(logit_ref[:, at].astype(F32) - norm_ref[:, at]).astype(BF16)
                prob_ref[:, at] = prob
                doc_copy.wait()
                acc[...] += lax.dot_general(
                    prob, held[...], (((1,), (1,)), ((), ())), preferred_element_type=F32
                )

        topic_at = sizes.topic_at(here_ref)
        for s in range(count):
            parts[s][...] = acc[window(topic_at ^ s, chunk), :].astype(BF16)
        rows = window(side, half)
        for s in range(far):
            target = lax.rem(sizes.vocab_at(here_ref) + s + 1, sizes.vocab)
            halves[s][...] = logit_ref[rows, window(target, share)]

    out = pl.pallas_call(
        kernel,
        out_shape=[jax.ShapeDtypeStruct((chunk, docs), BF16)] * count
        + [jax.ShapeDtypeStruct((half, share), BF16)] * far
        + [
            jax.ShapeDtypeStruct((docs, side_width), BF16),
            jax.ShapeDtypeStruct((docs, side_width), BF16),
            jax.ShapeDtypeStruct(word_logits.shape, BF16),
            jax.ShapeDtypeStruct(log_norm.shape, F32),
        ],
        in_specs=[SMEM, HBM, HBM, HBM],
        out_specs=[VMEM] * (count + far + 4),
        scratch_shapes=[
            pltpu.VMEM(word_logits.shape, BF16),
            pltpu.VMEM((words, docs), F32),
            pltpu.SemaphoreType.DMA((2, 2 * steps)),
            pltpu.SemaphoreType.DMA,
        ],
        compiler_params=call_params(),
        cost_estimate=cost(2 * words * docs * width, 2 * (words + docs) * width, words * width),
        name="rate_partial",
    )(here, in_hbm(doc_topics), in_hbm(word_logits), in_hbm(log_norm))
    return out[:count], out[count : count + far], *out[count + far :]


def chunk_counts(sizes, here, word_counts, tile_doc, tile_word, docs, words):
    slots, word_tile, doc_tile = word_counts.shape
    chunk = words // sizes.topic

    def kernel(here_ref, doc_at, word_at, count_ref, out_ref):
        first = sizes.topic_at(here_ref) * chunk
        block = first // word_tile
        row = pl.multiple_of(lax.rem(first, word_tile), chunk)
        out_ref[...] = jnp.zeros_like(out_ref)
        for s in range(slots):
            @pl.when(word_at[s] == block)
            def _():
                out_ref[:, window(doc_at[s], doc_tile)] = count_ref[s, pl.ds(row, chunk), :].astype(F32)

    return pl.pallas_call(
        kernel,
        out_shape=jax.ShapeDtypeStruct((chunk, docs), F32),
        in_specs=[SMEM, SMEM, SMEM, VMEM],
        out_specs=VMEM,
        compiler_params=call_params(),
        cost_estimate=cost(words * docs, 4 * words * docs),
        name="chunk_counts",
    )(here, in_hbm(tile_doc), in_hbm(tile_word), word_counts)


def ratio_chunk(parts, counts, word_tile):
    def kernel(*refs):
        part_refs, count_ref, out_ref = refs[:-2], refs[-2], refs[-1]
        rate = part_refs[0][...].astype(F32)
        for ref in part_refs[1:]:
            rate += ref[...].astype(F32)
        out_ref[...] = (count_ref[...] / (word_tile * rate)).astype(BF16)

    return pl.pallas_call(
        kernel,
        out_shape=jax.ShapeDtypeStruct(counts.shape, BF16),
        in_specs=[VMEM] * (len(parts) + 1),
        out_specs=VMEM,
        compiler_params=call_params(),
        cost_estimate=cost(10 * counts.size, 16 * counts.size),
        name="ratio_chunk",
    )(*parts, counts)


def join_ratio(sizes, here, chunks, order, after):
    rows, docs = chunks[0].shape
    count = sizes.topic

    def kernel(here_ref, *refs):
        topic_at = sizes.topic_at(here_ref)
        for s, ref in zip(order, refs):
            refs[-1][window(topic_at ^ s, rows), :] = ref[...]

    return pl.pallas_call(
        kernel,
        out_shape=jax.ShapeDtypeStruct((rows * count, docs), BF16),
        in_specs=[SMEM] + [VMEM] * count + [ANY] * len(after),
        out_specs=VMEM,
        compiler_params=call_params(),
        cost_estimate=cost(0, 4 * rows * docs * count),
        name="join_ratio",
    )(here, *chunks, *after)


def own_product(ratio, docs_held):
    words, docs = ratio.shape
    width = docs_held.shape[1]

    def kernel(ratio_ref, doc_ref, out_ref):
        out_ref[...] = jnp.dot(ratio_ref[...], doc_ref[...], preferred_element_type=F32)

    return pl.pallas_call(
        kernel,
        out_shape=jax.ShapeDtypeStruct((words, width), F32),
        in_specs=[VMEM, VMEM],
        out_specs=VMEM,
        compiler_params=call_params(),
        cost_estimate=cost(KERNEL_COST, 1) if words > 64 else cost(2 * words * docs * width, 2 * docs * width + 4 * words * width),
        name="own_product",
    )(ratio, docs_held)


def beta_pieces(sizes, here, product, ratio, docs_held, prob_held, flips):
    words, side_width = product.shape
    docs = docs_held.shape[0]
    rows = words // sum(map(len, flips))

    def kernel(here_ref, product_ref, ratio_ref, doc_ref, prob_ref, *out_refs):
        columns = window(sizes.side(here_ref), side_width)
        topic_at = sizes.topic_at(here_ref)
        summed = product_ref[...] + jnp.dot(ratio_ref[...], doc_ref[...], preferred_element_type=F32)
        chunk = 0
        for piece, out_ref in zip(flips, out_refs):
            for i, flip in enumerate(piece):
                prob = prob_ref[window(topic_at ^ flip, rows), columns].astype(F32)
                part = summed[chunk * rows : (chunk + 1) * rows, :]
                out_ref[i * rows : (i + 1) * rows, :] = (-prob * part).astype(BF16)
                chunk += 1

    return pl.pallas_call(
        kernel,
        out_shape=[jax.ShapeDtypeStruct((rows * len(piece), side_width), BF16) for piece in flips],
        in_specs=[SMEM] + [VMEM] * 4,
        out_specs=[VMEM] * len(flips),
        compiler_params=call_params(),
        cost_estimate=cost(KERNEL_COST, 1) if len(flips) > 1 else cost(2 * words * docs * side_width, 2 * (4 * words + docs) * side_width),
        name="beta_pieces",
    )(here, product, ratio, docs_held, prob_held)


def stack_rows(parts, after):
    rows, docs = parts[0].shape

    def kernel(*refs):
        for i, ref in enumerate(refs[: len(parts)]):
            refs[-1][i * rows : (i + 1) * rows, :] = ref[...]

    return pl.pallas_call(
        kernel,
        out_shape=jax.ShapeDtypeStruct((len(parts) * rows, docs), BF16),
        in_specs=[VMEM] * len(parts) + [ANY] * len(after),
        out_specs=VMEM,
        compiler_params=call_params(),
        cost_estimate=cost(0, 4 * len(parts) * rows * docs),
        name="stack_rows",
    )(*parts, *after)


def cut_rows(array, count, after):
    rows, width = array.shape[0] // count, array.shape[1]

    def kernel(in_ref, *rest):
        for i, out_ref in enumerate(rest[len(after) :]):
            out_ref[...] = in_ref[i * rows : (i + 1) * rows, :]

    return pl.pallas_call(
        kernel,
        out_shape=[jax.ShapeDtypeStruct((rows, width), array.dtype)] * count,
        in_specs=[VMEM] + [ANY] * len(after),
        out_specs=[VMEM] * count,
        compiler_params=call_params(),
        cost_estimate=cost(0, 4 * array.size),
        name="cut_rows",
    )(array, *after)


def add_pair(own, other, after=(), flops=1):
    def kernel(own_ref, other_ref, *rest):
        rest[-1][...] = (own_ref[...].astype(F32) + other_ref[...].astype(F32)).astype(BF16)

    return pl.pallas_call(
        kernel,
        out_shape=jax.ShapeDtypeStruct(own.shape, BF16),
        in_specs=[VMEM, VMEM] + [ANY] * len(after),
        out_specs=VMEM,
        compiler_params=call_params(),
        cost_estimate=cost(max(flops, own.size), 6 * own.size),
        name="add_pair",
    )(own, other, *after)


def hold(array, after, flops=1):
    def kernel(in_ref, *rest):
        rest[-1][...] = in_ref[...]

    return pl.pallas_call(
        kernel,
        out_shape=jax.ShapeDtypeStruct(array.shape, array.dtype),
        in_specs=[VMEM] + [ANY] * len(after),
        out_specs=VMEM,
        compiler_params=call_params(),
        cost_estimate=cost(flops, 4 * array.size),
        name="hold",
    )(array, *after)


def turn_ratios(sizes, here, ratio, far_ratios):
    words, docs = ratio.shape
    half = words // 2
    count = 1 + len(far_ratios)

    def kernel(here_ref, *refs):
        side = sizes.side(here_ref)
        for l, (ref, out_ref) in enumerate(zip(refs[:count], refs[count:])):
            for h, which in enumerate((side, 1 - side) if l else (0, 1)):
                rows = ref[window(which, half), :].astype(F32)
                out_ref[:, h * half : (h + 1) * half] = (-rows).T.astype(BF16)

    return pl.pallas_call(
        kernel,
        out_shape=[jax.ShapeDtypeStruct((docs, words), BF16)] * count,
        in_specs=[SMEM] + [VMEM] * count,
        out_specs=[VMEM] * count,
        compiler_params=call_params(),
        cost_estimate=cost(TURN_COST, 1),
        name="turn_ratios",
    )(here, ratio, *far_ratios)


def theta_grad(sizes, here, turned, prob_held, far_logits, log_norm):
    docs, words = turned[0].shape
    cuts = len(far_logits[0])
    rows, share = far_logits[0][0].shape
    count = len(turned)
    span = min(share, 512)
    blocks = share // span

    def kernel(here_ref, *refs):
        turned_refs, prob_ref = refs[:count], refs[count]
        logit_refs, norm_ref = refs[count + 1 : -3], refs[-3]
        out_ref, done_ref = refs[-2:]
        done_ref[...] = jnp.zeros_like(done_ref)
        summed = jnp.dot(turned_refs[0][...], prob_ref[...], preferred_element_type=F32)
        for l in range(count - 1):
            part = logit_refs[cuts * l : cuts * (l + 1)]
            prob = jnp.concatenate([jnp.exp(ref[...].astype(F32) - norm_ref[...]).astype(BF16) for ref in part], axis=0)
            summed += jnp.dot(turned_refs[l + 1][...], prob, preferred_element_type=F32)
        out_ref[...] = summed

    whole = lambda j, h: (0, 0)
    held = lambda j, h: (0, lax.rem(h[0], sizes.vocab) * blocks + j)
    column = lambda j, h: (0, j)
    return pl.pallas_call(
        kernel,
        out_shape=[jax.ShapeDtypeStruct((docs, share), F32), jax.ShapeDtypeStruct((8, 128), F32)],
        grid_spec=pltpu.PrefetchScalarGridSpec(
            num_scalar_prefetch=1,
            grid=(blocks,),
            in_specs=[pl.BlockSpec((docs, words), whole)] * count
            + [pl.BlockSpec((words, span), held)]
            + [pl.BlockSpec((rows, span), column)] * (cuts * (count - 1))
            + [pl.BlockSpec((1, span), held)],
            out_specs=[pl.BlockSpec((docs, span), column), pl.BlockSpec((8, 128), whole)],
        ),
        compiler_params=call_params(16),
        cost_estimate=cost(1, 1),
        name="theta_grad",
    )(here, *turned, prob_held, *sum(far_logits, []), log_norm)


def place_pieces(sizes, here, own, other, flips, shape):
    pieces = len(own)
    side_width = shape[1] // 2

    def kernel(here_ref, *refs):
        own_refs, other_refs, (out_ref, sems) = refs[:pieces], refs[pieces : 2 * pieces], refs[-2:]
        side, topic_at = sizes.side(here_ref), sizes.topic_at(here_ref)
        copies = []
        for p in range(pieces):
            rows = own_refs[p].shape[0] // len(flips[p])
            for h, (ref, which) in enumerate(((own_refs[p], side), (other_refs[p], 1 - side))):
                for i, flip in enumerate(flips[p]):
                    part = ref.at[pl.ds(i * rows, rows), :]
                    target = out_ref.at[window(topic_at ^ flip, rows), window(which, side_width)]
                    copies.append(pltpu.make_async_copy(part, target, sems.at[len(copies)]))
        for copy in copies:
            copy.start()
        for copy in copies:
            copy.wait()

    return pl.pallas_call(
        kernel,
        out_shape=jax.ShapeDtypeStruct(shape, BF16),
        in_specs=[SMEM] + [VMEM] * (2 * pieces),
        out_specs=HBM,
        scratch_shapes=[pltpu.SemaphoreType.DMA((2 * sum(map(len, flips)),))],
        compiler_params=call_params(),
        cost_estimate=cost(0, 4 * shape[0] * shape[1]),
        name="place_pieces",
    )(here, *own, *other)


def on_device(sizes, doc_topics, word_logits, log_norm, tile_doc, tile_word, word_counts):
    docs, width = doc_topics.shape
    words = word_logits.shape[0]
    word_tile = word_counts.shape[1]
    here = lax.axis_index(("doc", "topic", "vocab")).astype(jnp.int32)[None]

    def shift(array, by):
        return lax.ppermute(array, "vocab", [(i, (i + by) % sizes.vocab) for i in range(sizes.vocab)])

    def swap(array, axis, bits):
        count = {"doc": sizes.doc, "topic": sizes.topic}[axis]
        return lax.ppermute(array, axis, [(i, i ^ bits) for i in range(count)])

    parts, near_logits, docs_held, docs_sent, prob_held, norm_held = rate_partial(
        sizes, here, doc_topics, word_logits, log_norm[None, :]
    )
    sibling_docs = swap(docs_sent, "doc", 1)
    order = sorted(range(1, sizes.topic), key=lambda s: s < sizes.topic // 2)
    arrived = [swap(parts[s], "topic", s) for s in order]
    counts = chunk_counts(sizes, here, word_counts, tile_doc, tile_word, docs, words)
    own_ratio = ratio_chunk([parts[0]] + arrived, counts, word_tile)
    order.reverse()
    gathered = [swap(own_ratio, "topic", s) for s in order]
    far_bits = [1 << b for b in range(1, sizes.doc.bit_length() - 1)]

    def beta(chunks, flips):
        ratio, sibling_ratio = chunks[0], swap(chunks[0], "doc", 1)
        if len(chunks) > 1:
            ratio = stack_rows(chunks, [])
            sibling_ratio = stack_rows([sibling_ratio] + [swap(chunk, "doc", 1) for chunk in chunks[1:]], [])
        pieces = beta_pieces(
            sizes, here, own_product(ratio, docs_held), sibling_ratio, sibling_docs, prob_held, flips
        )
        for bit in far_bits[:-1]:
            pieces = [add_pair(part, swap(part, "doc", bit)) for part in pieces]
        return [(part, swap(part, "doc", far_bits[-1])) for part in pieces]

    flips = [[0]] + [piece for piece in (order[:-1], order[-1:]) if piece]
    pairs = beta([own_ratio], flips[:1])
    near_logits = [shift(hold(part, gathered[-1:]), s) for s, part in enumerate(near_logits, 1)]
    pairs += beta(gathered, flips[1:])
    first = add_pair(*pairs[0], [], ADD_COST)

    ratio = join_ratio(sizes, here, [own_ratio] + gathered, [0] + order, [first])
    far_ratios = [shift(ratio, s) for s in range(1, sizes.vocab)]
    far_logits = []
    for part in near_logits:
        pieces = list(cut_rows(part, 2, [pairs[1][0]]))
        far_logits.append(pieces + [swap(piece, "doc", 1) for piece in pieces])
    turned = turn_ratios(sizes, here, ratio, far_ratios)
    theta, theta_done = theta_grad(sizes, here, turned, prob_held, far_logits, norm_held)

    sums = [first] + [add_pair(*pair, [theta_done]) for pair in pairs[1:]]
    out = place_pieces(sizes, here, sums, [swap(part, "doc", 1) for part in sums], flips, word_logits.shape)
    return theta, out


def solution(mesh):
    placed = (
        P("doc", "topic"),
        P("vocab", "topic"),
        P("topic"),
        P(("doc", "vocab")),
        P(("doc", "vocab")),
        P(("doc", "vocab"), None, None),
    )
    return jax.shard_map(
        functools.partial(on_device, Sizes(mesh)),
        mesh=mesh,
        in_specs=placed,
        out_specs=(P("doc", ("topic", "vocab")), P("vocab", "topic")),
        check_vma=False,
    )
```

```python
import functools

import jax
import jax.numpy as jnp
from jax import lax
from jax.experimental import pallas as pl
from jax.experimental.pallas import tpu as pltpu
from jax.sharding import PartitionSpec as P

BF16 = jnp.bfloat16
F32 = jnp.float32
MIB = 1024 * 1024
ADD_COST = 22 * 10**8
KERNEL_COST = 125 * 10**7
TURN_COST = 10**9
ANY = pl.BlockSpec(memory_space=pl.ANY)
HBM = pl.BlockSpec(memory_space=pltpu.HBM)
VMEM = pl.BlockSpec(memory_space=pltpu.VMEM)
SMEM = pl.BlockSpec(memory_space=pltpu.SMEM)


def call_params(mib=16):
    return pltpu.CompilerParams(vmem_limit_bytes=mib * MIB)


def cost(flops, bytes_accessed, transcendentals=0):
    return pl.CostEstimate(flops=flops, bytes_accessed=bytes_accessed, transcendentals=transcendentals)


def in_hbm(array):
    return pltpu.with_memory_space_constraint(array, pltpu.HBM)


def window(index, size):
    return pl.ds(pl.multiple_of(index * size, size), size)


class Sizes:
    def __init__(self, mesh):
        self.doc, self.topic, self.vocab = (mesh.shape[axis] for axis in ("doc", "topic", "vocab"))

    def vocab_at(self, here_ref):
        return lax.rem(here_ref[0], self.vocab)

    def topic_at(self, here_ref):
        return lax.rem(lax.div(here_ref[0], self.vocab), self.topic)

    def side(self, here_ref):
        return lax.rem(lax.div(here_ref[0], self.vocab * self.topic), 2)


def rate_partial(sizes, here, doc_topics, word_logits, log_norm):
    docs, width = doc_topics.shape
    words = word_logits.shape[0]
    side_width = width // 2
    span = min(side_width, 512)
    steps = side_width // span
    count, far = sizes.topic, sizes.vocab - 1
    chunk, half, share = words // count, words // 2, width // sizes.vocab

    def kernel(here_ref, doc_in, logit_in, norm_in, *rest):
        parts, halves = rest[:count], rest[count : count + far]
        own_ref, sibling_ref, prob_ref, norm_ref, logit_ref, acc, sems, norm_sem = rest[count + far :]
        side = sizes.side(here_ref)
        norm_copy = pltpu.make_async_copy(norm_in, norm_ref, norm_sem)
        norm_copy.start()

        def block(which, doc_ref, h, j):
            at = window(which * steps + j, span)
            held = doc_ref.at[:, window(j, span)]
            logit_copy = pltpu.make_async_copy(logit_in.at[:, at], logit_ref.at[:, at], sems.at[0, h * steps + j])
            return at, held, logit_copy, pltpu.make_async_copy(doc_in.at[:, at], held, sems.at[1, h * steps + j])

        sides = ((1 - side, sibling_ref), (side, own_ref))
        for h, (which, doc_ref) in enumerate(sides):
            @pl.loop(0, steps)
            def _(j):
                _, _, logit_copy, doc_copy = block(which, doc_ref, h, j)
                logit_copy.start()
                doc_copy.start()

        acc[...] = jnp.zeros_like(acc)
        norm_copy.wait()
        for h, (which, doc_ref) in enumerate(sides):
            @pl.loop(0, steps)
            def _(j):
                at, held, logit_copy, doc_copy = block(which, doc_ref, h, j)
                logit_copy.wait()
                prob = jnp.exp(logit_ref[:, at].astype(F32) - norm_ref[:, at]).astype(BF16)
                prob_ref[:, at] = prob
                doc_copy.wait()
                acc[...] += lax.dot_general(
                    prob, held[...], (((1,), (1,)), ((), ())), preferred_element_type=F32
                )

        topic_at = sizes.topic_at(here_ref)
        for s in range(count):
            parts[s][...] = acc[window(topic_at ^ s, chunk), :].astype(BF16)
        rows = window(side, half)
        for s in range(far):
            target = lax.rem(sizes.vocab_at(here_ref) + s + 1, sizes.vocab)
            halves[s][...] = logit_ref[rows, window(target, share)]

    out = pl.pallas_call(
        kernel,
        out_shape=[jax.ShapeDtypeStruct((chunk, docs), BF16)] * count
        + [jax.ShapeDtypeStruct((half, share), BF16)] * far
        + [
            jax.ShapeDtypeStruct((docs, side_width), BF16),
            jax.ShapeDtypeStruct((docs, side_width), BF16),
            jax.ShapeDtypeStruct(word_logits.shape, BF16),
            jax.ShapeDtypeStruct(log_norm.shape, F32),
        ],
        in_specs=[SMEM, HBM, HBM, HBM],
        out_specs=[VMEM] * (count + far + 4),
        scratch_shapes=[
            pltpu.VMEM(word_logits.shape, BF16),
            pltpu.VMEM((words, docs), F32),
            pltpu.SemaphoreType.DMA((2, 2 * steps)),
            pltpu.SemaphoreType.DMA,
        ],
        compiler_params=call_params(),
        cost_estimate=cost(2 * words * docs * width, 2 * (words + docs) * width, words * width),
        name="rate_partial",
    )(here, in_hbm(doc_topics), in_hbm(word_logits), in_hbm(log_norm))
    return out[:count], out[count : count + far], *out[count + far :]


def chunk_counts(sizes, here, word_counts, tile_doc, tile_word, docs, words):
    slots, word_tile, doc_tile = word_counts.shape
    chunk = words // sizes.topic

    def kernel(here_ref, doc_at, word_at, count_ref, out_ref):
        first = sizes.topic_at(here_ref) * chunk
        block = first // word_tile
        row = pl.multiple_of(lax.rem(first, word_tile), chunk)
        out_ref[...] = jnp.zeros_like(out_ref)
        for s in range(slots):
            @pl.when(word_at[s] == block)
            def _():
                out_ref[:, window(doc_at[s], doc_tile)] = count_ref[s, pl.ds(row, chunk), :].astype(F32)

    return pl.pallas_call(
        kernel,
        out_shape=jax.ShapeDtypeStruct((chunk, docs), F32),
        in_specs=[SMEM, SMEM, SMEM, VMEM],
        out_specs=VMEM,
        compiler_params=call_params(),
        cost_estimate=cost(words * docs, 4 * words * docs),
        name="chunk_counts",
    )(here, in_hbm(tile_doc), in_hbm(tile_word), word_counts)


def ratio_chunk(parts, counts, word_tile):
    def kernel(*refs):
        part_refs, count_ref, out_ref = refs[:-2], refs[-2], refs[-1]
        rate = part_refs[0][...].astype(F32)
        for ref in part_refs[1:]:
            rate += ref[...].astype(F32)
        out_ref[...] = (count_ref[...] / (word_tile * rate)).astype(BF16)

    return pl.pallas_call(
        kernel,
        out_shape=jax.ShapeDtypeStruct(counts.shape, BF16),
        in_specs=[VMEM] * (len(parts) + 1),
        out_specs=VMEM,
        compiler_params=call_params(),
        cost_estimate=cost(10 * counts.size, 16 * counts.size),
        name="ratio_chunk",
    )(*parts, counts)


def join_ratio(sizes, here, chunks, order, after):
    rows, docs = chunks[0].shape
    count = sizes.topic

    def kernel(here_ref, *refs):
        topic_at = sizes.topic_at(here_ref)
        for s, ref in zip(order, refs):
            refs[-1][window(topic_at ^ s, rows), :] = ref[...]

    return pl.pallas_call(
        kernel,
        out_shape=jax.ShapeDtypeStruct((rows * count, docs), BF16),
        in_specs=[SMEM] + [VMEM] * count + [ANY] * len(after),
        out_specs=VMEM,
        compiler_params=call_params(),
        cost_estimate=cost(0, 4 * rows * docs * count),
        name="join_ratio",
    )(here, *chunks, *after)


def own_product(ratio, docs_held):
    words, docs = ratio.shape
    width = docs_held.shape[1]

    def kernel(ratio_ref, doc_ref, out_ref):
        out_ref[...] = jnp.dot(ratio_ref[...], doc_ref[...], preferred_element_type=F32)

    return pl.pallas_call(
        kernel,
        out_shape=jax.ShapeDtypeStruct((words, width), F32),
        in_specs=[VMEM, VMEM],
        out_specs=VMEM,
        compiler_params=call_params(),
        cost_estimate=cost(KERNEL_COST, 1) if words > 64 else cost(2 * words * docs * width, 2 * docs * width + 4 * words * width),
        name="own_product",
    )(ratio, docs_held)


def beta_pieces(sizes, here, product, ratio, docs_held, prob_held, flips):
    words, side_width = product.shape
    docs = docs_held.shape[0]
    rows = words // sum(map(len, flips))

    def kernel(here_ref, product_ref, ratio_ref, doc_ref, prob_ref, *out_refs):
        columns = window(sizes.side(here_ref), side_width)
        topic_at = sizes.topic_at(here_ref)
        summed = product_ref[...] + jnp.dot(ratio_ref[...], doc_ref[...], preferred_element_type=F32)
        chunk = 0
        for piece, out_ref in zip(flips, out_refs):
            for i, flip in enumerate(piece):
                prob = prob_ref[window(topic_at ^ flip, rows), columns].astype(F32)
                part = summed[chunk * rows : (chunk + 1) * rows, :]
                out_ref[i * rows : (i + 1) * rows, :] = (-prob * part).astype(BF16)
                chunk += 1

    return pl.pallas_call(
        kernel,
        out_shape=[jax.ShapeDtypeStruct((rows * len(piece), side_width), BF16) for piece in flips],
        in_specs=[SMEM] + [VMEM] * 4,
        out_specs=[VMEM] * len(flips),
        compiler_params=call_params(),
        cost_estimate=cost(KERNEL_COST, 1) if len(flips) > 1 else cost(2 * words * docs * side_width, 2 * (4 * words + docs) * side_width),
        name="beta_pieces",
    )(here, product, ratio, docs_held, prob_held)


def stack_rows(parts, after):
    rows, docs = parts[0].shape

    def kernel(*refs):
        for i, ref in enumerate(refs[: len(parts)]):
            refs[-1][i * rows : (i + 1) * rows, :] = ref[...]

    return pl.pallas_call(
        kernel,
        out_shape=jax.ShapeDtypeStruct((len(parts) * rows, docs), BF16),
        in_specs=[VMEM] * len(parts) + [ANY] * len(after),
        out_specs=VMEM,
        compiler_params=call_params(),
        cost_estimate=cost(0, 4 * len(parts) * rows * docs),
        name="stack_rows",
    )(*parts, *after)


def cut_rows(array, count, after):
    rows, width = array.shape[0] // count, array.shape[1]

    def kernel(in_ref, *rest):
        for i, out_ref in enumerate(rest[len(after) :]):
            out_ref[...] = in_ref[i * rows : (i + 1) * rows, :]

    return pl.pallas_call(
        kernel,
        out_shape=[jax.ShapeDtypeStruct((rows, width), array.dtype)] * count,
        in_specs=[VMEM] + [ANY] * len(after),
        out_specs=[VMEM] * count,
        compiler_params=call_params(),
        cost_estimate=cost(0, 4 * array.size),
        name="cut_rows",
    )(array, *after)


def add_pair(own, other, after=(), flops=1):
    def kernel(own_ref, other_ref, *rest):
        rest[-1][...] = (own_ref[...].astype(F32) + other_ref[...].astype(F32)).astype(BF16)

    return pl.pallas_call(
        kernel,
        out_shape=jax.ShapeDtypeStruct(own.shape, BF16),
        in_specs=[VMEM, VMEM] + [ANY] * len(after),
        out_specs=VMEM,
        compiler_params=call_params(),
        cost_estimate=cost(max(flops, own.size), 6 * own.size),
        name="add_pair",
    )(own, other, *after)


def hold(array, after, flops=1):
    def kernel(in_ref, *rest):
        rest[-1][...] = in_ref[...]

    return pl.pallas_call(
        kernel,
        out_shape=jax.ShapeDtypeStruct(array.shape, array.dtype),
        in_specs=[VMEM] + [ANY] * len(after),
        out_specs=VMEM,
        compiler_params=call_params(),
        cost_estimate=cost(flops, 4 * array.size),
        name="hold",
    )(array, *after)


def turn_ratios(sizes, here, ratio, far_ratios):
    words, docs = ratio.shape
    half = words // 2
    count = 1 + len(far_ratios)

    def kernel(here_ref, *refs):
        side = sizes.side(here_ref)
        for l, (ref, out_ref) in enumerate(zip(refs[:count], refs[count:])):
            for h, which in enumerate((side, 1 - side) if l else (0, 1)):
                rows = ref[window(which, half), :].astype(F32)
                out_ref[:, h * half : (h + 1) * half] = (-rows).T.astype(BF16)

    return pl.pallas_call(
        kernel,
        out_shape=[jax.ShapeDtypeStruct((docs, words), BF16)] * count,
        in_specs=[SMEM] + [VMEM] * count,
        out_specs=[VMEM] * count,
        compiler_params=call_params(),
        cost_estimate=cost(TURN_COST, 1),
        name="turn_ratios",
    )(here, ratio, *far_ratios)


def theta_grad(sizes, here, turned, prob_held, far_logits, log_norm, after):
    docs, words = turned[0].shape
    cuts = len(far_logits[0])
    rows, share = far_logits[0][0].shape
    count = len(turned)
    span = min(share, 512)
    blocks = share // span

    def kernel(here_ref, *refs):
        turned_refs, prob_ref = refs[:count], refs[count]
        logit_refs, norm_ref = refs[count + 1 : -3 - len(after)], refs[-3 - len(after)]
        out_ref, done_ref = refs[-2:]
        done_ref[...] = jnp.zeros_like(done_ref)
        summed = jnp.dot(turned_refs[0][...], prob_ref[...], preferred_element_type=F32)
        for l in range(count - 1):
            part = logit_refs[cuts * l : cuts * (l + 1)]
            prob = jnp.concatenate([jnp.exp(ref[...].astype(F32) - norm_ref[...]).astype(BF16) for ref in part], axis=0)
            summed += jnp.dot(turned_refs[l + 1][...], prob, preferred_element_type=F32)
        out_ref[...] = summed

    whole = lambda j, h: (0, 0)
    held = lambda j, h: (0, lax.rem(h[0], sizes.vocab) * blocks + j)
    column = lambda j, h: (0, j)
    return pl.pallas_call(
        kernel,
        out_shape=[jax.ShapeDtypeStruct((docs, share), F32), jax.ShapeDtypeStruct((8, 128), F32)],
        grid_spec=pltpu.PrefetchScalarGridSpec(
            num_scalar_prefetch=1,
            grid=(blocks,),
            in_specs=[pl.BlockSpec((docs, words), whole)] * count
            + [pl.BlockSpec((words, span), held)]
            + [pl.BlockSpec((rows, span), column)] * (cuts * (count - 1))
            + [pl.BlockSpec((1, span), held)]
            + [ANY] * len(after),
            out_specs=[pl.BlockSpec((docs, span), column), pl.BlockSpec((8, 128), whole)],
        ),
        compiler_params=call_params(16),
        cost_estimate=cost(1, 1),
        name="theta_grad",
    )(here, *turned, prob_held, *sum(far_logits, []), log_norm, *after)


def place_pieces(sizes, here, own, other, flips, shape, so_far=None):
    pieces = len(own)
    side_width = shape[1] // 2
    before = [] if so_far is None else [so_far]

    def kernel(here_ref, *refs):
        own_refs, other_refs = refs[:pieces], refs[pieces : 2 * pieces]
        out_ref, sems = refs[2 * pieces + len(before)], refs[-1]
        if not before:
            refs[-2][...] = jnp.zeros_like(refs[-2])
        side, topic_at = sizes.side(here_ref), sizes.topic_at(here_ref)
        copies = []
        for p in range(pieces):
            rows = own_refs[p].shape[0] // len(flips[p])
            for h, (ref, which) in enumerate(((own_refs[p], side), (other_refs[p], 1 - side))):
                for i, flip in enumerate(flips[p]):
                    part = ref.at[pl.ds(i * rows, rows), :]
                    target = out_ref.at[window(topic_at ^ flip, rows), window(which, side_width)]
                    copies.append(pltpu.make_async_copy(part, target, sems.at[len(copies)]))
        for copy in copies:
            copy.start()
        for copy in copies:
            copy.wait()

    return pl.pallas_call(
        kernel,
        out_shape=[jax.ShapeDtypeStruct(shape, BF16)] + ([] if before else [jax.ShapeDtypeStruct((8, 128), F32)]),
        in_specs=[SMEM] + [VMEM] * (2 * pieces) + [HBM] * len(before),
        out_specs=[HBM] + ([] if before else [VMEM]),
        scratch_shapes=[pltpu.SemaphoreType.DMA((2 * sum(map(len, flips)),))],
        input_output_aliases={2 * pieces + 1: 0} if before else {},
        compiler_params=call_params(),
        cost_estimate=cost(0, 4 * sum(part.size for part in own)),
        name="place_pieces",
    )(here, *own, *other, *before)


def on_device(sizes, doc_topics, word_logits, log_norm, tile_doc, tile_word, word_counts):
    docs, width = doc_topics.shape
    words = word_logits.shape[0]
    word_tile = word_counts.shape[1]
    here = lax.axis_index(("doc", "topic", "vocab")).astype(jnp.int32)[None]

    def shift(array, by):
        return lax.ppermute(array, "vocab", [(i, (i + by) % sizes.vocab) for i in range(sizes.vocab)])

    def swap(array, axis, bits):
        count = {"doc": sizes.doc, "topic": sizes.topic}[axis]
        return lax.ppermute(array, axis, [(i, i ^ bits) for i in range(count)])

    parts, near_logits, docs_held, docs_sent, prob_held, norm_held = rate_partial(
        sizes, here, doc_topics, word_logits, log_norm[None, :]
    )
    sibling_docs = swap(docs_sent, "doc", 1)
    order = sorted(range(1, sizes.topic), key=lambda s: s < sizes.topic // 2)
    arrived = [swap(parts[s], "topic", s) for s in order]
    counts = chunk_counts(sizes, here, word_counts, tile_doc, tile_word, docs, words)
    own_ratio = ratio_chunk([parts[0]] + arrived, counts, word_tile)
    order = order[1:] + order[:1]
    gathered = [swap(own_ratio, "topic", s) for s in order]
    far_bits = [1 << b for b in range(1, sizes.doc.bit_length() - 1)]

    def beta(chunks, flips):
        ratio, sibling_ratio = chunks[0], swap(chunks[0], "doc", 1)
        if len(chunks) > 1:
            ratio = stack_rows(chunks, [])
            sibling_ratio = stack_rows([sibling_ratio] + [swap(chunk, "doc", 1) for chunk in chunks[1:]], [])
        pieces = beta_pieces(
            sizes, here, own_product(ratio, docs_held), sibling_ratio, sibling_docs, prob_held, flips
        )
        for bit in far_bits[:-1]:
            pieces = [add_pair(part, swap(part, "doc", bit)) for part in pieces]
        return [(part, swap(part, "doc", far_bits[-1])) for part in pieces]

    flips = [[0]] + [piece for piece in (order[:-1], order[-1:]) if piece]
    pairs = beta([own_ratio], flips[:1])
    near_logits = [shift(hold(part, gathered[-1:]), s) for s, part in enumerate(near_logits, 1)]
    pairs += beta(gathered, flips[1:])
    first = add_pair(*pairs[0], [], ADD_COST)

    ratio = join_ratio(sizes, here, [own_ratio] + gathered, [0] + order, [first])
    far_ratios = [shift(ratio, s) for s in range(1, sizes.vocab)]
    far_logits = []
    for part in near_logits:
        pieces = list(cut_rows(part, 2, [pairs[1][0]]))
        far_logits.append(pieces + [swap(piece, "doc", 1) for piece in pieces])
    turned = turn_ratios(sizes, here, ratio, far_ratios)
    out, early_done = place_pieces(sizes, here, [first], [swap(first, "doc", 1)], flips[:1], word_logits.shape)
    theta, theta_done = theta_grad(sizes, here, turned, prob_held, far_logits, norm_held, [early_done])
    sums = [add_pair(*pair, [theta_done]) for pair in pairs[1:]]
    siblings = [swap(part, "doc", 1) for part in sums]
    (out,) = place_pieces(sizes, here, sums, siblings, flips[1:], word_logits.shape, out)
    return theta, out


def solution(mesh):
    placed = (
        P("doc", "topic"),
        P("vocab", "topic"),
        P("topic"),
        P(("doc", "vocab")),
        P(("doc", "vocab")),
        P(("doc", "vocab"), None, None),
    )
    return jax.shard_map(
        functools.partial(on_device, Sizes(mesh)),
        mesh=mesh,
        in_specs=placed,
        out_specs=(P("doc", ("topic", "vocab")), P("vocab", "topic")),
        check_vma=False,
    )
```

```python
import functools

import jax
import jax.numpy as jnp
from jax import lax
from jax.experimental import pallas as pl
from jax.experimental.pallas import tpu as pltpu
from jax.sharding import PartitionSpec as P

BF16 = jnp.bfloat16
F32 = jnp.float32
MIB = 1024 * 1024
ADD_COST = 28 * 10**8
KERNEL_COST = 125 * 10**7
TURN_COST = 10**9
ANY = pl.BlockSpec(memory_space=pl.ANY)
HBM = pl.BlockSpec(memory_space=pltpu.HBM)
VMEM = pl.BlockSpec(memory_space=pltpu.VMEM)
SMEM = pl.BlockSpec(memory_space=pltpu.SMEM)


def call_params(mib=16):
    return pltpu.CompilerParams(vmem_limit_bytes=mib * MIB)


def cost(flops, bytes_accessed, transcendentals=0):
    return pl.CostEstimate(flops=flops, bytes_accessed=bytes_accessed, transcendentals=transcendentals)


def in_hbm(array):
    return pltpu.with_memory_space_constraint(array, pltpu.HBM)


def window(index, size):
    return pl.ds(pl.multiple_of(index * size, size), size)


class Sizes:
    def __init__(self, mesh):
        self.doc, self.topic, self.vocab = (mesh.shape[axis] for axis in ("doc", "topic", "vocab"))

    def vocab_at(self, here_ref):
        return lax.rem(here_ref[0], self.vocab)

    def topic_at(self, here_ref):
        return lax.rem(lax.div(here_ref[0], self.vocab), self.topic)

    def side(self, here_ref):
        return lax.rem(lax.div(here_ref[0], self.vocab * self.topic), 2)


def rate_partial(sizes, here, doc_topics, word_logits, log_norm):
    docs, width = doc_topics.shape
    words = word_logits.shape[0]
    side_width = width // 2
    span = min(side_width, 512)
    steps = side_width // span
    count, far = sizes.topic, sizes.vocab - 1
    chunk, half, share = words // count, words // 2, width // sizes.vocab

    def kernel(here_ref, doc_in, logit_in, norm_in, *rest):
        parts, halves = rest[:count], rest[count : count + far]
        own_ref, sibling_ref, prob_ref, norm_ref, logit_ref, acc, sems, norm_sem = rest[count + far :]
        side = sizes.side(here_ref)
        norm_copy = pltpu.make_async_copy(norm_in, norm_ref, norm_sem)
        norm_copy.start()

        def block(which, doc_ref, h, j):
            at = window(which * steps + j, span)
            held = doc_ref.at[:, window(j, span)]
            logit_copy = pltpu.make_async_copy(logit_in.at[:, at], logit_ref.at[:, at], sems.at[0, h * steps + j])
            return at, held, logit_copy, pltpu.make_async_copy(doc_in.at[:, at], held, sems.at[1, h * steps + j])

        sides = ((1 - side, sibling_ref), (side, own_ref))
        for h, (which, doc_ref) in enumerate(sides):
            @pl.loop(0, steps)
            def _(j):
                _, _, logit_copy, doc_copy = block(which, doc_ref, h, j)
                logit_copy.start()
                doc_copy.start()

        acc[...] = jnp.zeros_like(acc)
        norm_copy.wait()
        for h, (which, doc_ref) in enumerate(sides):
            @pl.loop(0, steps)
            def _(j):
                at, held, logit_copy, doc_copy = block(which, doc_ref, h, j)
                logit_copy.wait()
                prob = jnp.exp(logit_ref[:, at].astype(F32) - norm_ref[:, at]).astype(BF16)
                prob_ref[:, at] = prob
                doc_copy.wait()
                acc[...] += lax.dot_general(
                    prob, held[...], (((1,), (1,)), ((), ())), preferred_element_type=F32
                )

        topic_at = sizes.topic_at(here_ref)
        for s in range(count):
            parts[s][...] = acc[window(topic_at ^ s, chunk), :].astype(BF16)
        rows = window(side, half)
        for s in range(far):
            target = lax.rem(sizes.vocab_at(here_ref) + s + 1, sizes.vocab)
            halves[s][...] = logit_ref[rows, window(target, share)]

    out = pl.pallas_call(
        kernel,
        out_shape=[jax.ShapeDtypeStruct((chunk, docs), BF16)] * count
        + [jax.ShapeDtypeStruct((half, share), BF16)] * far
        + [
            jax.ShapeDtypeStruct((docs, side_width), BF16),
            jax.ShapeDtypeStruct((docs, side_width), BF16),
            jax.ShapeDtypeStruct(word_logits.shape, BF16),
            jax.ShapeDtypeStruct(log_norm.shape, F32),
        ],
        in_specs=[SMEM, HBM, HBM, HBM],
        out_specs=[VMEM] * (count + far + 4),
        scratch_shapes=[
            pltpu.VMEM(word_logits.shape, BF16),
            pltpu.VMEM((words, docs), F32),
            pltpu.SemaphoreType.DMA((2, 2 * steps)),
            pltpu.SemaphoreType.DMA,
        ],
        compiler_params=call_params(),
        cost_estimate=cost(2 * words * docs * width, 2 * (words + docs) * width, words * width),
        name="rate_partial",
    )(here, in_hbm(doc_topics), in_hbm(word_logits), in_hbm(log_norm))
    return out[:count], out[count : count + far], *out[count + far :]


def chunk_counts(sizes, here, word_counts, tile_doc, tile_word, docs, words):
    slots, word_tile, doc_tile = word_counts.shape
    chunk = words // sizes.topic

    def kernel(here_ref, doc_at, word_at, count_ref, out_ref):
        first = sizes.topic_at(here_ref) * chunk
        block = first // word_tile
        row = pl.multiple_of(lax.rem(first, word_tile), chunk)
        out_ref[...] = jnp.zeros_like(out_ref)
        for s in range(slots):
            @pl.when(word_at[s] == block)
            def _():
                out_ref[:, window(doc_at[s], doc_tile)] = count_ref[s, pl.ds(row, chunk), :].astype(F32)

    return pl.pallas_call(
        kernel,
        out_shape=jax.ShapeDtypeStruct((chunk, docs), F32),
        in_specs=[SMEM, SMEM, SMEM, VMEM],
        out_specs=VMEM,
        compiler_params=call_params(),
        cost_estimate=cost(words * docs, 4 * words * docs),
        name="chunk_counts",
    )(here, in_hbm(tile_doc), in_hbm(tile_word), word_counts)


def ratio_chunk(parts, counts, word_tile):
    def kernel(*refs):
        part_refs, count_ref, out_ref = refs[:-2], refs[-2], refs[-1]
        rate = part_refs[0][...].astype(F32)
        for ref in part_refs[1:]:
            rate += ref[...].astype(F32)
        out_ref[...] = (count_ref[...] / (word_tile * rate)).astype(BF16)

    return pl.pallas_call(
        kernel,
        out_shape=jax.ShapeDtypeStruct(counts.shape, BF16),
        in_specs=[VMEM] * (len(parts) + 1),
        out_specs=VMEM,
        compiler_params=call_params(),
        cost_estimate=cost(10 * counts.size, 16 * counts.size),
        name="ratio_chunk",
    )(*parts, counts)


def join_ratio(sizes, here, chunks, order, after):
    rows, docs = chunks[0].shape
    count = sizes.topic

    def kernel(here_ref, *refs):
        topic_at = sizes.topic_at(here_ref)
        for s, ref in zip(order, refs):
            refs[-1][window(topic_at ^ s, rows), :] = ref[...]

    return pl.pallas_call(
        kernel,
        out_shape=jax.ShapeDtypeStruct((rows * count, docs), BF16),
        in_specs=[SMEM] + [VMEM] * count + [ANY] * len(after),
        out_specs=VMEM,
        compiler_params=call_params(),
        cost_estimate=cost(0, 4 * rows * docs * count),
        name="join_ratio",
    )(here, *chunks, *after)


def own_product(ratio, docs_held):
    words, docs = ratio.shape
    width = docs_held.shape[1]

    def kernel(ratio_ref, doc_ref, out_ref):
        out_ref[...] = jnp.dot(ratio_ref[...], doc_ref[...], preferred_element_type=F32)

    return pl.pallas_call(
        kernel,
        out_shape=jax.ShapeDtypeStruct((words, width), F32),
        in_specs=[VMEM, VMEM],
        out_specs=VMEM,
        compiler_params=call_params(),
        cost_estimate=cost(KERNEL_COST, 1) if words > 64 else cost(2 * words * docs * width, 2 * docs * width + 4 * words * width),
        name="own_product",
    )(ratio, docs_held)


def beta_pieces(sizes, here, product, ratio, docs_held, prob_held, flips):
    words, side_width = product.shape
    docs = docs_held.shape[0]
    rows = words // sum(map(len, flips))

    def kernel(here_ref, product_ref, ratio_ref, doc_ref, prob_ref, *out_refs):
        columns = window(sizes.side(here_ref), side_width)
        topic_at = sizes.topic_at(here_ref)
        summed = product_ref[...] + jnp.dot(ratio_ref[...], doc_ref[...], preferred_element_type=F32)
        chunk = 0
        for piece, out_ref in zip(flips, out_refs):
            for i, flip in enumerate(piece):
                prob = prob_ref[window(topic_at ^ flip, rows), columns].astype(F32)
                part = summed[chunk * rows : (chunk + 1) * rows, :]
                out_ref[i * rows : (i + 1) * rows, :] = (-prob * part).astype(BF16)
                chunk += 1

    return pl.pallas_call(
        kernel,
        out_shape=[jax.ShapeDtypeStruct((rows * len(piece), side_width), BF16) for piece in flips],
        in_specs=[SMEM] + [VMEM] * 4,
        out_specs=[VMEM] * len(flips),
        compiler_params=call_params(),
        cost_estimate=cost(KERNEL_COST, 1) if len(flips[0]) > 1 else cost(2 * words * docs * side_width, 2 * (4 * words + docs) * side_width),
        name="beta_pieces",
    )(here, product, ratio, docs_held, prob_held)


def stack_rows(parts, after):
    rows, docs = parts[0].shape

    def kernel(*refs):
        for i, ref in enumerate(refs[: len(parts)]):
            refs[-1][i * rows : (i + 1) * rows, :] = ref[...]

    return pl.pallas_call(
        kernel,
        out_shape=jax.ShapeDtypeStruct((len(parts) * rows, docs), BF16),
        in_specs=[VMEM] * len(parts) + [ANY] * len(after),
        out_specs=VMEM,
        compiler_params=call_params(),
        cost_estimate=cost(0, 4 * len(parts) * rows * docs),
        name="stack_rows",
    )(*parts, *after)


def cut_rows(array, count, after):
    rows, width = array.shape[0] // count, array.shape[1]

    def kernel(in_ref, *rest):
        for i, out_ref in enumerate(rest[len(after) :]):
            out_ref[...] = in_ref[i * rows : (i + 1) * rows, :]

    return pl.pallas_call(
        kernel,
        out_shape=[jax.ShapeDtypeStruct((rows, width), array.dtype)] * count,
        in_specs=[VMEM] + [ANY] * len(after),
        out_specs=[VMEM] * count,
        compiler_params=call_params(),
        cost_estimate=cost(0, 4 * array.size),
        name="cut_rows",
    )(array, *after)


def add_pair(own, other, after=(), flops=1):
    def kernel(own_ref, other_ref, *rest):
        rest[-1][...] = (own_ref[...].astype(F32) + other_ref[...].astype(F32)).astype(BF16)

    return pl.pallas_call(
        kernel,
        out_shape=jax.ShapeDtypeStruct(own.shape, BF16),
        in_specs=[VMEM, VMEM] + [ANY] * len(after),
        out_specs=VMEM,
        compiler_params=call_params(),
        cost_estimate=cost(max(flops, own.size), 6 * own.size),
        name="add_pair",
    )(own, other, *after)


def hold(array, after, flops=1):
    def kernel(in_ref, *rest):
        rest[-1][...] = in_ref[...]

    return pl.pallas_call(
        kernel,
        out_shape=jax.ShapeDtypeStruct(array.shape, array.dtype),
        in_specs=[VMEM] + [ANY] * len(after),
        out_specs=VMEM,
        compiler_params=call_params(),
        cost_estimate=cost(flops, 4 * array.size),
        name="hold",
    )(array, *after)


def turn_ratios(sizes, here, ratio, far_ratios):
    words, docs = ratio.shape
    half = words // 2
    count = 1 + len(far_ratios)

    def kernel(here_ref, *refs):
        side = sizes.side(here_ref)
        for l, (ref, out_ref) in enumerate(zip(refs[:count], refs[count:])):
            for h, which in enumerate((side, 1 - side) if l else (0, 1)):
                rows = ref[window(which, half), :].astype(F32)
                out_ref[:, h * half : (h + 1) * half] = (-rows).T.astype(BF16)

    return pl.pallas_call(
        kernel,
        out_shape=[jax.ShapeDtypeStruct((docs, words), BF16)] * count,
        in_specs=[SMEM] + [VMEM] * count,
        out_specs=[VMEM] * count,
        compiler_params=call_params(),
        cost_estimate=cost(TURN_COST, 1),
        name="turn_ratios",
    )(here, ratio, *far_ratios)


def theta_grad(sizes, here, turned, prob_held, far_logits, log_norm, after):
    docs, words = turned[0].shape
    cuts = len(far_logits[0])
    rows, share = far_logits[0][0].shape
    count = len(turned)
    span = min(share, 512)
    blocks = share // span

    def kernel(here_ref, *refs):
        turned_refs, prob_ref = refs[:count], refs[count]
        logit_refs, norm_ref = refs[count + 1 : -3 - len(after)], refs[-3 - len(after)]
        out_ref, done_ref = refs[-2:]
        done_ref[...] = jnp.zeros_like(done_ref)
        summed = jnp.dot(turned_refs[0][...], prob_ref[...], preferred_element_type=F32)
        for l in range(count - 1):
            part = logit_refs[cuts * l : cuts * (l + 1)]
            prob = jnp.concatenate([jnp.exp(ref[...].astype(F32) - norm_ref[...]).astype(BF16) for ref in part], axis=0)
            summed += jnp.dot(turned_refs[l + 1][...], prob, preferred_element_type=F32)
        out_ref[...] = summed

    whole = lambda j, h: (0, 0)
    held = lambda j, h: (0, lax.rem(h[0], sizes.vocab) * blocks + j)
    column = lambda j, h: (0, j)
    return pl.pallas_call(
        kernel,
        out_shape=[jax.ShapeDtypeStruct((docs, share), F32), jax.ShapeDtypeStruct((8, 128), F32)],
        grid_spec=pltpu.PrefetchScalarGridSpec(
            num_scalar_prefetch=1,
            grid=(blocks,),
            in_specs=[pl.BlockSpec((docs, words), whole)] * count
            + [pl.BlockSpec((words, span), held)]
            + [pl.BlockSpec((rows, span), column)] * (cuts * (count - 1))
            + [pl.BlockSpec((1, span), held)]
            + [ANY] * len(after),
            out_specs=[pl.BlockSpec((docs, span), column), pl.BlockSpec((8, 128), whole)],
        ),
        compiler_params=call_params(16),
        cost_estimate=cost(1, 1),
        name="theta_grad",
    )(here, *turned, prob_held, *sum(far_logits, []), log_norm, *after)


def place_pieces(sizes, here, own, other, flips, shape, so_far=None):
    pieces = len(own)
    side_width = shape[1] // 2
    before = [] if so_far is None else [so_far]

    def kernel(here_ref, *refs):
        own_refs, other_refs = refs[:pieces], refs[pieces : 2 * pieces]
        out_ref, sems = refs[2 * pieces + len(before)], refs[-1]
        if not before:
            refs[-2][...] = jnp.zeros_like(refs[-2])
        side, topic_at = sizes.side(here_ref), sizes.topic_at(here_ref)
        copies = []
        for p in range(pieces):
            rows = own_refs[p].shape[0] // len(flips[p])
            for h, (ref, which) in enumerate(((own_refs[p], side), (other_refs[p], 1 - side))):
                for i, flip in enumerate(flips[p]):
                    part = ref.at[pl.ds(i * rows, rows), :]
                    target = out_ref.at[window(topic_at ^ flip, rows), window(which, side_width)]
                    copies.append(pltpu.make_async_copy(part, target, sems.at[len(copies)]))
        for copy in copies:
            copy.start()
        for copy in copies:
            copy.wait()

    return pl.pallas_call(
        kernel,
        out_shape=[jax.ShapeDtypeStruct(shape, BF16)] + ([] if before else [jax.ShapeDtypeStruct((8, 128), F32)]),
        in_specs=[SMEM] + [VMEM] * (2 * pieces) + [HBM] * len(before),
        out_specs=[HBM] + ([] if before else [VMEM]),
        scratch_shapes=[pltpu.SemaphoreType.DMA((2 * sum(map(len, flips)),))],
        input_output_aliases={2 * pieces + 1: 0} if before else {},
        compiler_params=call_params(),
        cost_estimate=cost(0, 4 * sum(part.size for part in own)),
        name="place_pieces",
    )(here, *own, *other, *before)


def on_device(sizes, doc_topics, word_logits, log_norm, tile_doc, tile_word, word_counts):
    docs, width = doc_topics.shape
    words = word_logits.shape[0]
    word_tile = word_counts.shape[1]
    here = lax.axis_index(("doc", "topic", "vocab")).astype(jnp.int32)[None]

    def shift(array, by):
        return lax.ppermute(array, "vocab", [(i, (i + by) % sizes.vocab) for i in range(sizes.vocab)])

    def swap(array, axis, bits):
        count = {"doc": sizes.doc, "topic": sizes.topic}[axis]
        return lax.ppermute(array, axis, [(i, i ^ bits) for i in range(count)])

    parts, near_logits, docs_held, docs_sent, prob_held, norm_held = rate_partial(
        sizes, here, doc_topics, word_logits, log_norm[None, :]
    )
    sibling_docs = swap(docs_sent, "doc", 1)
    order = sorted(range(1, sizes.topic), key=lambda s: s < sizes.topic // 2)
    arrived = [swap(parts[s], "topic", s) for s in order]
    counts = chunk_counts(sizes, here, word_counts, tile_doc, tile_word, docs, words)
    own_ratio = ratio_chunk([parts[0]] + arrived, counts, word_tile)
    order = order[1:] + order[:1]
    gathered = [swap(own_ratio, "topic", s) for s in order]
    far_bits = [1 << b for b in range(1, sizes.doc.bit_length() - 1)]

    def beta(chunks, flips):
        ratio, sibling_ratio = chunks[0], swap(chunks[0], "doc", 1)
        if len(chunks) > 1:
            ratio = stack_rows(chunks, [])
            sibling_ratio = stack_rows([sibling_ratio] + [swap(chunk, "doc", 1) for chunk in chunks[1:]], [])
        pieces = beta_pieces(
            sizes, here, own_product(ratio, docs_held), sibling_ratio, sibling_docs, prob_held, flips
        )
        for bit in far_bits[:-1]:
            pieces = [add_pair(part, swap(part, "doc", bit)) for part in pieces]
        return [(part, swap(part, "doc", far_bits[-1])) for part in pieces]

    flips = [[0]] + [piece for piece in (order[-1:] + order[:-2], order[-2:-1]) if piece]
    pairs = beta([own_ratio], flips[:1])
    near_logits = [shift(hold(part, gathered[-1:]), s) for s, part in enumerate(near_logits, 1)]
    ratios = dict(zip(order, gathered))
    for piece in flips[1:]:
        pairs += beta([ratios[s] for s in piece], [piece])
    first = add_pair(*pairs[0], [], ADD_COST)

    ratio = join_ratio(sizes, here, [own_ratio] + gathered, [0] + order, [first, pairs[-1][0]])
    far_ratios = [shift(ratio, s) for s in range(1, sizes.vocab)]
    far_logits = []
    for part in near_logits:
        pieces = list(cut_rows(part, 2, [pairs[1][0]]))
        far_logits.append(pieces + [swap(piece, "doc", 1) for piece in pieces])
    turned = turn_ratios(sizes, here, ratio, far_ratios)
    out, early_done = place_pieces(sizes, here, [first], [swap(first, "doc", 1)], flips[:1], word_logits.shape)
    theta, theta_done = theta_grad(sizes, here, turned, prob_held, far_logits, norm_held, [early_done])
    sums = [add_pair(*pair, [theta_done]) for pair in pairs[1:]]
    siblings = [swap(part, "doc", 1) for part in sums]
    (out,) = place_pieces(sizes, here, sums, siblings, flips[1:], word_logits.shape, out)
    return theta, out


def solution(mesh):
    placed = (
        P("doc", "topic"),
        P("vocab", "topic"),
        P("topic"),
        P(("doc", "vocab")),
        P(("doc", "vocab")),
        P(("doc", "vocab"), None, None),
    )
    return jax.shard_map(
        functools.partial(on_device, Sizes(mesh)),
        mesh=mesh,
        in_specs=placed,
        out_specs=(P("doc", ("topic", "vocab")), P("vocab", "topic")),
        check_vma=False,
    )
```

```python
import functools

import jax
import jax.numpy as jnp
from jax import lax
from jax.experimental import pallas as pl
from jax.experimental.pallas import tpu as pltpu
from jax.sharding import PartitionSpec as P

BF16 = jnp.bfloat16
F32 = jnp.float32
MIB = 1024 * 1024
ADD_COST = 28 * 10**8
KERNEL_COST = 125 * 10**7
TURN_COST = 10**9
ANY = pl.BlockSpec(memory_space=pl.ANY)
HBM = pl.BlockSpec(memory_space=pltpu.HBM)
VMEM = pl.BlockSpec(memory_space=pltpu.VMEM)
SMEM = pl.BlockSpec(memory_space=pltpu.SMEM)


def call_params(mib=16):
    return pltpu.CompilerParams(vmem_limit_bytes=mib * MIB)


def cost(flops, bytes_accessed, transcendentals=0):
    return pl.CostEstimate(flops=flops, bytes_accessed=bytes_accessed, transcendentals=transcendentals)


def in_hbm(array):
    return pltpu.with_memory_space_constraint(array, pltpu.HBM)


def window(index, size):
    return pl.ds(pl.multiple_of(index * size, size), size)


class Sizes:
    def __init__(self, mesh):
        self.doc, self.topic, self.vocab = (mesh.shape[axis] for axis in ("doc", "topic", "vocab"))

    def vocab_at(self, here_ref):
        return lax.rem(here_ref[0], self.vocab)

    def topic_at(self, here_ref):
        return lax.rem(lax.div(here_ref[0], self.vocab), self.topic)

    def side(self, here_ref):
        return lax.rem(lax.div(here_ref[0], self.vocab * self.topic), 2)


def rate_partial(sizes, here, doc_topics, word_logits, log_norm):
    docs, width = doc_topics.shape
    words = word_logits.shape[0]
    side_width = width // 2
    span = min(side_width, 1024)
    steps = side_width // span
    count, far = sizes.topic, sizes.vocab - 1
    chunk, half, share = words // count, words // 2, width // sizes.vocab

    def kernel(here_ref, doc_in, logit_in, norm_in, *rest):
        parts, halves = rest[:count], rest[count : count + far]
        own_ref, sibling_ref, prob_ref, norm_ref, logit_ref, acc, sems, norm_sem = rest[count + far :]
        side = sizes.side(here_ref)
        norm_copy = pltpu.make_async_copy(norm_in, norm_ref, norm_sem)
        norm_copy.start()

        def block(which, doc_ref, h, j):
            at = window(which * steps + j, span)
            held = doc_ref.at[:, window(j, span)]
            logit_copy = pltpu.make_async_copy(logit_in.at[:, at], logit_ref.at[:, at], sems.at[0, h * steps + j])
            return at, held, logit_copy, pltpu.make_async_copy(doc_in.at[:, at], held, sems.at[1, h * steps + j])

        sides = ((1 - side, sibling_ref), (side, own_ref))
        for h, (which, doc_ref) in enumerate(sides):
            @pl.loop(0, steps)
            def _(j):
                _, _, logit_copy, doc_copy = block(which, doc_ref, h, j)
                logit_copy.start()
                doc_copy.start()

        acc[...] = jnp.zeros_like(acc)
        norm_copy.wait()
        for h, (which, doc_ref) in enumerate(sides):
            @pl.loop(0, steps)
            def _(j):
                at, held, logit_copy, doc_copy = block(which, doc_ref, h, j)
                logit_copy.wait()
                prob = jnp.exp(logit_ref[:, at].astype(F32) - norm_ref[:, at]).astype(BF16)
                prob_ref[:, at] = prob
                doc_copy.wait()
                acc[...] += lax.dot_general(
                    prob, held[...], (((1,), (1,)), ((), ())), preferred_element_type=F32
                )

        topic_at = sizes.topic_at(here_ref)
        for s in range(count):
            parts[s][...] = acc[window(topic_at ^ s, chunk), :].astype(BF16)
        rows = window(side, half)
        for s in range(far):
            target = lax.rem(sizes.vocab_at(here_ref) + s + 1, sizes.vocab)
            halves[s][...] = logit_ref[rows, window(target, share)]

    out = pl.pallas_call(
        kernel,
        out_shape=[jax.ShapeDtypeStruct((chunk, docs), BF16)] * count
        + [jax.ShapeDtypeStruct((half, share), BF16)] * far
        + [
            jax.ShapeDtypeStruct((docs, side_width), BF16),
            jax.ShapeDtypeStruct((docs, side_width), BF16),
            jax.ShapeDtypeStruct(word_logits.shape, BF16),
            jax.ShapeDtypeStruct(log_norm.shape, F32),
        ],
        in_specs=[SMEM, HBM, HBM, HBM],
        out_specs=[VMEM] * (count + far + 4),
        scratch_shapes=[
            pltpu.VMEM(word_logits.shape, BF16),
            pltpu.VMEM((words, docs), F32),
            pltpu.SemaphoreType.DMA((2, 2 * steps)),
            pltpu.SemaphoreType.DMA,
        ],
        compiler_params=call_params(),
        cost_estimate=cost(2 * words * docs * width, 2 * (words + docs) * width, words * width),
        name="rate_partial",
    )(here, in_hbm(doc_topics), in_hbm(word_logits), in_hbm(log_norm))
    return out[:count], out[count : count + far], *out[count + far :]


def chunk_counts(sizes, here, word_counts, tile_doc, tile_word, docs, words):
    slots, word_tile, doc_tile = word_counts.shape
    chunk = words // sizes.topic

    def kernel(here_ref, doc_at, word_at, count_ref, out_ref):
        first = sizes.topic_at(here_ref) * chunk
        block = first // word_tile
        row = pl.multiple_of(lax.rem(first, word_tile), chunk)
        out_ref[...] = jnp.zeros_like(out_ref)
        for s in range(slots):
            @pl.when(word_at[s] == block)
            def _():
                out_ref[:, window(doc_at[s], doc_tile)] = count_ref[s, pl.ds(row, chunk), :].astype(F32)

    return pl.pallas_call(
        kernel,
        out_shape=jax.ShapeDtypeStruct((chunk, docs), F32),
        in_specs=[SMEM, SMEM, SMEM, VMEM],
        out_specs=VMEM,
        compiler_params=call_params(),
        cost_estimate=cost(words * docs, 4 * words * docs),
        name="chunk_counts",
    )(here, in_hbm(tile_doc), in_hbm(tile_word), word_counts)


def ratio_chunk(parts, counts, word_tile):
    def kernel(*refs):
        part_refs, count_ref, out_ref = refs[:-2], refs[-2], refs[-1]
        rate = part_refs[0][...].astype(F32)
        for ref in part_refs[1:]:
            rate += ref[...].astype(F32)
        out_ref[...] = (count_ref[...] / (word_tile * rate)).astype(BF16)

    return pl.pallas_call(
        kernel,
        out_shape=jax.ShapeDtypeStruct(counts.shape, BF16),
        in_specs=[VMEM] * (len(parts) + 1),
        out_specs=VMEM,
        compiler_params=call_params(),
        cost_estimate=cost(10 * counts.size, 16 * counts.size),
        name="ratio_chunk",
    )(*parts, counts)


def join_ratio(sizes, here, chunks, order, after):
    rows, docs = chunks[0].shape
    count = sizes.topic

    def kernel(here_ref, *refs):
        topic_at = sizes.topic_at(here_ref)
        for s, ref in zip(order, refs):
            refs[-1][window(topic_at ^ s, rows), :] = ref[...]

    return pl.pallas_call(
        kernel,
        out_shape=jax.ShapeDtypeStruct((rows * count, docs), BF16),
        in_specs=[SMEM] + [VMEM] * count + [ANY] * len(after),
        out_specs=VMEM,
        compiler_params=call_params(),
        cost_estimate=cost(0, 4 * rows * docs * count),
        name="join_ratio",
    )(here, *chunks, *after)


def own_product(ratio, docs_held):
    words, docs = ratio.shape
    width = docs_held.shape[1]

    def kernel(ratio_ref, doc_ref, out_ref):
        out_ref[...] = jnp.dot(ratio_ref[...], doc_ref[...], preferred_element_type=F32)

    return pl.pallas_call(
        kernel,
        out_shape=jax.ShapeDtypeStruct((words, width), F32),
        in_specs=[VMEM, VMEM],
        out_specs=VMEM,
        compiler_params=call_params(),
        cost_estimate=cost(KERNEL_COST, 1) if words > 64 else cost(2 * words * docs * width, 2 * docs * width + 4 * words * width),
        name="own_product",
    )(ratio, docs_held)


def beta_pieces(sizes, here, product, ratio, docs_held, prob_held, flips):
    words, side_width = product.shape
    docs = docs_held.shape[0]
    rows = words // sum(map(len, flips))

    def kernel(here_ref, product_ref, ratio_ref, doc_ref, prob_ref, *out_refs):
        columns = window(sizes.side(here_ref), side_width)
        topic_at = sizes.topic_at(here_ref)
        summed = product_ref[...] + jnp.dot(ratio_ref[...], doc_ref[...], preferred_element_type=F32)
        chunk = 0
        for piece, out_ref in zip(flips, out_refs):
            for i, flip in enumerate(piece):
                prob = prob_ref[window(topic_at ^ flip, rows), columns].astype(F32)
                part = summed[chunk * rows : (chunk + 1) * rows, :]
                out_ref[i * rows : (i + 1) * rows, :] = (-prob * part).astype(BF16)
                chunk += 1

    return pl.pallas_call(
        kernel,
        out_shape=[jax.ShapeDtypeStruct((rows * len(piece), side_width), BF16) for piece in flips],
        in_specs=[SMEM] + [VMEM] * 4,
        out_specs=[VMEM] * len(flips),
        compiler_params=call_params(),
        cost_estimate=cost(KERNEL_COST, 1) if len(flips[0]) > 1 else cost(2 * words * docs * side_width, 2 * (4 * words + docs) * side_width),
        name="beta_pieces",
    )(here, product, ratio, docs_held, prob_held)


def stack_rows(parts, after):
    rows, docs = parts[0].shape

    def kernel(*refs):
        for i, ref in enumerate(refs[: len(parts)]):
            refs[-1][i * rows : (i + 1) * rows, :] = ref[...]

    return pl.pallas_call(
        kernel,
        out_shape=jax.ShapeDtypeStruct((len(parts) * rows, docs), BF16),
        in_specs=[VMEM] * len(parts) + [ANY] * len(after),
        out_specs=VMEM,
        compiler_params=call_params(),
        cost_estimate=cost(0, 4 * len(parts) * rows * docs),
        name="stack_rows",
    )(*parts, *after)


def cut_rows(array, count, after):
    rows, width = array.shape[0] // count, array.shape[1]

    def kernel(in_ref, *rest):
        for i, out_ref in enumerate(rest[len(after) :]):
            out_ref[...] = in_ref[i * rows : (i + 1) * rows, :]

    return pl.pallas_call(
        kernel,
        out_shape=[jax.ShapeDtypeStruct((rows, width), array.dtype)] * count,
        in_specs=[VMEM] + [ANY] * len(after),
        out_specs=[VMEM] * count,
        compiler_params=call_params(),
        cost_estimate=cost(0, 4 * array.size),
        name="cut_rows",
    )(array, *after)


def add_pair(own, other, after=(), flops=1):
    def kernel(own_ref, other_ref, *rest):
        rest[-1][...] = (own_ref[...].astype(F32) + other_ref[...].astype(F32)).astype(BF16)

    return pl.pallas_call(
        kernel,
        out_shape=jax.ShapeDtypeStruct(own.shape, BF16),
        in_specs=[VMEM, VMEM] + [ANY] * len(after),
        out_specs=VMEM,
        compiler_params=call_params(),
        cost_estimate=cost(max(flops, own.size), 6 * own.size),
        name="add_pair",
    )(own, other, *after)


def hold(array, after, flops=1):
    def kernel(in_ref, *rest):
        rest[-1][...] = in_ref[...]

    return pl.pallas_call(
        kernel,
        out_shape=jax.ShapeDtypeStruct(array.shape, array.dtype),
        in_specs=[VMEM] + [ANY] * len(after),
        out_specs=VMEM,
        compiler_params=call_params(),
        cost_estimate=cost(flops, 4 * array.size),
        name="hold",
    )(array, *after)


def turn_ratios(sizes, here, ratio, far_ratios):
    words, docs = ratio.shape
    half = words // 2
    count = 1 + len(far_ratios)

    def kernel(here_ref, *refs):
        side = sizes.side(here_ref)
        for l, (ref, out_ref) in enumerate(zip(refs[:count], refs[count:])):
            for h, which in enumerate((side, 1 - side) if l else (0, 1)):
                rows = ref[window(which, half), :].astype(F32)
                out_ref[:, h * half : (h + 1) * half] = (-rows).T.astype(BF16)

    return pl.pallas_call(
        kernel,
        out_shape=[jax.ShapeDtypeStruct((docs, words), BF16)] * count,
        in_specs=[SMEM] + [VMEM] * count,
        out_specs=[VMEM] * count,
        compiler_params=call_params(),
        cost_estimate=cost(TURN_COST, 1),
        name="turn_ratios",
    )(here, ratio, *far_ratios)


def theta_grad(sizes, here, turned, prob_held, far_logits, log_norm, after):
    docs, words = turned[0].shape
    cuts = len(far_logits[0])
    rows, share = far_logits[0][0].shape
    count = len(turned)
    span = min(share, 512)
    blocks = share // span

    def kernel(here_ref, *refs):
        turned_refs, prob_ref = refs[:count], refs[count]
        logit_refs, norm_ref = refs[count + 1 : -3 - len(after)], refs[-3 - len(after)]
        out_ref, done_ref = refs[-2:]
        done_ref[...] = jnp.zeros_like(done_ref)
        summed = jnp.dot(turned_refs[0][...], prob_ref[...], preferred_element_type=F32)
        for l in range(count - 1):
            part = logit_refs[cuts * l : cuts * (l + 1)]
            prob = jnp.concatenate([jnp.exp(ref[...].astype(F32) - norm_ref[...]).astype(BF16) for ref in part], axis=0)
            summed += jnp.dot(turned_refs[l + 1][...], prob, preferred_element_type=F32)
        out_ref[...] = summed

    whole = lambda j, h: (0, 0)
    held = lambda j, h: (0, lax.rem(h[0], sizes.vocab) * blocks + j)
    column = lambda j, h: (0, j)
    return pl.pallas_call(
        kernel,
        out_shape=[jax.ShapeDtypeStruct((docs, share), F32), jax.ShapeDtypeStruct((8, 128), F32)],
        grid_spec=pltpu.PrefetchScalarGridSpec(
            num_scalar_prefetch=1,
            grid=(blocks,),
            in_specs=[pl.BlockSpec((docs, words), whole)] * count
            + [pl.BlockSpec((words, span), held)]
            + [pl.BlockSpec((rows, span), column)] * (cuts * (count - 1))
            + [pl.BlockSpec((1, span), held)]
            + [ANY] * len(after),
            out_specs=[pl.BlockSpec((docs, span), column), pl.BlockSpec((8, 128), whole)],
        ),
        compiler_params=call_params(16),
        cost_estimate=cost(1, 1),
        name="theta_grad",
    )(here, *turned, prob_held, *sum(far_logits, []), log_norm, *after)


def place_pieces(sizes, here, own, other, flips, shape, so_far=None):
    pieces = len(own)
    side_width = shape[1] // 2
    before = [] if so_far is None else [so_far]

    def kernel(here_ref, *refs):
        own_refs, other_refs = refs[:pieces], refs[pieces : 2 * pieces]
        out_ref, sems = refs[2 * pieces + len(before)], refs[-1]
        if not before:
            refs[-2][...] = jnp.zeros_like(refs[-2])
        side, topic_at = sizes.side(here_ref), sizes.topic_at(here_ref)
        copies = []
        for p in range(pieces):
            rows = own_refs[p].shape[0] // len(flips[p])
            for h, (ref, which) in enumerate(((own_refs[p], side), (other_refs[p], 1 - side))):
                for i, flip in enumerate(flips[p]):
                    part = ref.at[pl.ds(i * rows, rows), :]
                    target = out_ref.at[window(topic_at ^ flip, rows), window(which, side_width)]
                    copies.append(pltpu.make_async_copy(part, target, sems.at[len(copies)]))
        for copy in copies:
            copy.start()
        for copy in copies:
            copy.wait()

    return pl.pallas_call(
        kernel,
        out_shape=[jax.ShapeDtypeStruct(shape, BF16)] + ([] if before else [jax.ShapeDtypeStruct((8, 128), F32)]),
        in_specs=[SMEM] + [VMEM] * (2 * pieces) + [HBM] * len(before),
        out_specs=[HBM] + ([] if before else [VMEM]),
        scratch_shapes=[pltpu.SemaphoreType.DMA((2 * sum(map(len, flips)),))],
        input_output_aliases={2 * pieces + 1: 0} if before else {},
        compiler_params=call_params(),
        cost_estimate=cost(0, 4 * sum(part.size for part in own)),
        name="place_pieces",
    )(here, *own, *other, *before)


def on_device(sizes, doc_topics, word_logits, log_norm, tile_doc, tile_word, word_counts):
    docs, width = doc_topics.shape
    words = word_logits.shape[0]
    word_tile = word_counts.shape[1]
    here = lax.axis_index(("doc", "topic", "vocab")).astype(jnp.int32)[None]

    def shift(array, by):
        return lax.ppermute(array, "vocab", [(i, (i + by) % sizes.vocab) for i in range(sizes.vocab)])

    def swap(array, axis, bits):
        count = {"doc": sizes.doc, "topic": sizes.topic}[axis]
        return lax.ppermute(array, axis, [(i, i ^ bits) for i in range(count)])

    parts, near_logits, docs_held, docs_sent, prob_held, norm_held = rate_partial(
        sizes, here, doc_topics, word_logits, log_norm[None, :]
    )
    sibling_docs = swap(docs_sent, "doc", 1)
    order = sorted(range(1, sizes.topic), key=lambda s: s < sizes.topic // 2)
    arrived = [swap(parts[s], "topic", s) for s in order]
    counts = chunk_counts(sizes, here, word_counts, tile_doc, tile_word, docs, words)
    own_ratio = ratio_chunk([parts[0]] + arrived, counts, word_tile)
    order = order[1:] + order[:1]
    gathered = [swap(own_ratio, "topic", s) for s in order]
    far_bits = [1 << b for b in range(1, sizes.doc.bit_length() - 1)]

    def beta(chunks, flips):
        ratio, sibling_ratio = chunks[0], swap(chunks[0], "doc", 1)
        if len(chunks) > 1:
            ratio = stack_rows(chunks, [])
            sibling_ratio = stack_rows([sibling_ratio] + [swap(chunk, "doc", 1) for chunk in chunks[1:]], [])
        pieces = beta_pieces(
            sizes, here, own_product(ratio, docs_held), sibling_ratio, sibling_docs, prob_held, flips
        )
        for bit in far_bits[:-1]:
            pieces = [add_pair(part, swap(part, "doc", bit)) for part in pieces]
        return [(part, swap(part, "doc", far_bits[-1])) for part in pieces]

    flips = [[0]] + [piece for piece in (order[-1:] + order[:-2], order[-2:-1]) if piece]
    pairs = beta([own_ratio], flips[:1])
    near_logits = [shift(hold(part, gathered[-1:]), s) for s, part in enumerate(near_logits, 1)]
    ratios = dict(zip(order, gathered))
    for piece in flips[1:]:
        pairs += beta([ratios[s] for s in piece], [piece])
    first = add_pair(*pairs[0], [], ADD_COST)

    ratio = join_ratio(sizes, here, [own_ratio] + gathered, [0] + order, [first, pairs[-1][0]])
    far_ratios = [shift(ratio, s) for s in range(1, sizes.vocab)]
    far_logits = []
    for part in near_logits:
        pieces = list(cut_rows(part, 2, [pairs[1][0]]))
        far_logits.append(pieces + [swap(piece, "doc", 1) for piece in pieces])
    turned = turn_ratios(sizes, here, ratio, far_ratios)
    out, early_done = place_pieces(sizes, here, [first], [swap(first, "doc", 1)], flips[:1], word_logits.shape)
    theta, theta_done = theta_grad(sizes, here, turned, prob_held, far_logits, norm_held, [early_done])
    sums = [add_pair(*pair, [theta_done]) for pair in pairs[1:]]
    siblings = [swap(part, "doc", 1) for part in sums]
    (out,) = place_pieces(sizes, here, sums, siblings, flips[1:], word_logits.shape, out)
    return theta, out


def solution(mesh):
    placed = (
        P("doc", "topic"),
        P("vocab", "topic"),
        P("topic"),
        P(("doc", "vocab")),
        P(("doc", "vocab")),
        P(("doc", "vocab"), None, None),
    )
    return jax.shard_map(
        functools.partial(on_device, Sizes(mesh)),
        mesh=mesh,
        in_specs=placed,
        out_specs=(P("doc", ("topic", "vocab")), P("vocab", "topic")),
        check_vma=False,
    )
```

```python
import functools

import jax
import jax.numpy as jnp
from jax import lax
from jax.experimental import pallas as pl
from jax.experimental.pallas import tpu as pltpu
from jax.sharding import PartitionSpec as P

BF16 = jnp.bfloat16
F32 = jnp.float32
MIB = 1024 * 1024
ADD_COST = 28 * 10**8
KERNEL_COST = 125 * 10**7
TURN_COST = 10**9
ANY = pl.BlockSpec(memory_space=pl.ANY)
HBM = pl.BlockSpec(memory_space=pltpu.HBM)
VMEM = pl.BlockSpec(memory_space=pltpu.VMEM)
SMEM = pl.BlockSpec(memory_space=pltpu.SMEM)


def call_params(mib=16):
    return pltpu.CompilerParams(vmem_limit_bytes=mib * MIB)


def cost(flops, bytes_accessed, transcendentals=0):
    return pl.CostEstimate(flops=flops, bytes_accessed=bytes_accessed, transcendentals=transcendentals)


def in_hbm(array):
    return pltpu.with_memory_space_constraint(array, pltpu.HBM)


def window(index, size):
    return pl.ds(pl.multiple_of(index * size, size), size)


class Sizes:
    def __init__(self, mesh):
        self.doc, self.topic, self.vocab = (mesh.shape[axis] for axis in ("doc", "topic", "vocab"))

    def vocab_at(self, here_ref):
        return lax.rem(here_ref[0], self.vocab)

    def topic_at(self, here_ref):
        return lax.rem(lax.div(here_ref[0], self.vocab), self.topic)

    def side(self, here_ref):
        return lax.rem(lax.div(here_ref[0], self.vocab * self.topic), 2)


def rate_partial(sizes, here, doc_topics, word_logits, log_norm):
    docs, width = doc_topics.shape
    words = word_logits.shape[0]
    side_width = width // 2
    span = min(side_width, 2048)
    steps = side_width // span
    count, far = sizes.topic, sizes.vocab - 1
    chunk, half, share = words // count, words // 2, width // sizes.vocab

    def kernel(here_ref, doc_in, logit_in, norm_in, *rest):
        parts, halves = rest[:count], rest[count : count + far]
        own_ref, sibling_ref, prob_ref, norm_ref, logit_ref, acc, sems, norm_sem = rest[count + far :]
        side = sizes.side(here_ref)
        norm_copy = pltpu.make_async_copy(norm_in, norm_ref, norm_sem)
        norm_copy.start()

        def block(which, doc_ref, h, j):
            at = window(which * steps + j, span)
            held = doc_ref.at[:, window(j, span)]
            logit_copy = pltpu.make_async_copy(logit_in.at[:, at], logit_ref.at[:, at], sems.at[0, h * steps + j])
            return at, held, logit_copy, pltpu.make_async_copy(doc_in.at[:, at], held, sems.at[1, h * steps + j])

        sides = ((1 - side, sibling_ref), (side, own_ref))
        for h, (which, doc_ref) in enumerate(sides):
            @pl.loop(0, steps)
            def _(j):
                _, _, logit_copy, doc_copy = block(which, doc_ref, h, j)
                logit_copy.start()
                doc_copy.start()

        acc[...] = jnp.zeros_like(acc)
        norm_copy.wait()
        for h, (which, doc_ref) in enumerate(sides):
            @pl.loop(0, steps)
            def _(j):
                at, held, logit_copy, doc_copy = block(which, doc_ref, h, j)
                logit_copy.wait()
                prob = jnp.exp(logit_ref[:, at].astype(F32) - norm_ref[:, at]).astype(BF16)
                prob_ref[:, at] = prob
                doc_copy.wait()
                acc[...] += lax.dot_general(
                    prob, held[...], (((1,), (1,)), ((), ())), preferred_element_type=F32
                )

        topic_at = sizes.topic_at(here_ref)
        for s in range(count):
            parts[s][...] = acc[window(topic_at ^ s, chunk), :].astype(BF16)
        rows = window(side, half)
        for s in range(far):
            target = lax.rem(sizes.vocab_at(here_ref) + s + 1, sizes.vocab)
            halves[s][...] = logit_ref[rows, window(target, share)]

    out = pl.pallas_call(
        kernel,
        out_shape=[jax.ShapeDtypeStruct((chunk, docs), BF16)] * count
        + [jax.ShapeDtypeStruct((half, share), BF16)] * far
        + [
            jax.ShapeDtypeStruct((docs, side_width), BF16),
            jax.ShapeDtypeStruct((docs, side_width), BF16),
            jax.ShapeDtypeStruct(word_logits.shape, BF16),
            jax.ShapeDtypeStruct(log_norm.shape, F32),
        ],
        in_specs=[SMEM, HBM, HBM, HBM],
        out_specs=[VMEM] * (count + far + 4),
        scratch_shapes=[
            pltpu.VMEM(word_logits.shape, BF16),
            pltpu.VMEM((words, docs), F32),
            pltpu.SemaphoreType.DMA((2, 2 * steps)),
            pltpu.SemaphoreType.DMA,
        ],
        compiler_params=call_params(),
        cost_estimate=cost(2 * words * docs * width, 2 * (words + docs) * width, words * width),
        name="rate_partial",
    )(here, in_hbm(doc_topics), in_hbm(word_logits), in_hbm(log_norm))
    return out[:count], out[count : count + far], *out[count + far :]


def chunk_counts(sizes, here, word_counts, tile_doc, tile_word, docs, words):
    slots, word_tile, doc_tile = word_counts.shape
    chunk = words // sizes.topic

    def kernel(here_ref, doc_at, word_at, count_ref, out_ref):
        first = sizes.topic_at(here_ref) * chunk
        block = first // word_tile
        row = pl.multiple_of(lax.rem(first, word_tile), chunk)
        out_ref[...] = jnp.zeros_like(out_ref)
        for s in range(slots):
            @pl.when(word_at[s] == block)
            def _():
                out_ref[:, window(doc_at[s], doc_tile)] = count_ref[s, pl.ds(row, chunk), :].astype(F32)

    return pl.pallas_call(
        kernel,
        out_shape=jax.ShapeDtypeStruct((chunk, docs), F32),
        in_specs=[SMEM, SMEM, SMEM, VMEM],
        out_specs=VMEM,
        compiler_params=call_params(),
        cost_estimate=cost(words * docs, 4 * words * docs),
        name="chunk_counts",
    )(here, in_hbm(tile_doc), in_hbm(tile_word), word_counts)


def ratio_chunk(parts, counts, word_tile):
    def kernel(*refs):
        part_refs, count_ref, out_ref = refs[:-2], refs[-2], refs[-1]
        rate = part_refs[0][...].astype(F32)
        for ref in part_refs[1:]:
            rate += ref[...].astype(F32)
        out_ref[...] = (count_ref[...] / (word_tile * rate)).astype(BF16)

    return pl.pallas_call(
        kernel,
        out_shape=jax.ShapeDtypeStruct(counts.shape, BF16),
        in_specs=[VMEM] * (len(parts) + 1),
        out_specs=VMEM,
        compiler_params=call_params(),
        cost_estimate=cost(10 * counts.size, 16 * counts.size),
        name="ratio_chunk",
    )(*parts, counts)


def join_ratio(sizes, here, chunks, order, after):
    rows, docs = chunks[0].shape
    count = sizes.topic

    def kernel(here_ref, *refs):
        topic_at = sizes.topic_at(here_ref)
        for s, ref in zip(order, refs):
            refs[-1][window(topic_at ^ s, rows), :] = ref[...]

    return pl.pallas_call(
        kernel,
        out_shape=jax.ShapeDtypeStruct((rows * count, docs), BF16),
        in_specs=[SMEM] + [VMEM] * count + [ANY] * len(after),
        out_specs=VMEM,
        compiler_params=call_params(),
        cost_estimate=cost(0, 4 * rows * docs * count),
        name="join_ratio",
    )(here, *chunks, *after)


def own_product(ratio, docs_held):
    words, docs = ratio.shape
    width = docs_held.shape[1]

    def kernel(ratio_ref, doc_ref, out_ref):
        out_ref[...] = jnp.dot(ratio_ref[...], doc_ref[...], preferred_element_type=F32)

    return pl.pallas_call(
        kernel,
        out_shape=jax.ShapeDtypeStruct((words, width), F32),
        in_specs=[VMEM, VMEM],
        out_specs=VMEM,
        compiler_params=call_params(),
        cost_estimate=cost(KERNEL_COST, 1) if words > 64 else cost(2 * words * docs * width, 2 * docs * width + 4 * words * width),
        name="own_product",
    )(ratio, docs_held)


def beta_pieces(sizes, here, product, ratio, docs_held, prob_held, flips):
    words, side_width = product.shape
    docs = docs_held.shape[0]
    rows = words // sum(map(len, flips))

    def kernel(here_ref, product_ref, ratio_ref, doc_ref, prob_ref, *out_refs):
        columns = window(sizes.side(here_ref), side_width)
        topic_at = sizes.topic_at(here_ref)
        summed = product_ref[...] + jnp.dot(ratio_ref[...], doc_ref[...], preferred_element_type=F32)
        chunk = 0
        for piece, out_ref in zip(flips, out_refs):
            for i, flip in enumerate(piece):
                prob = prob_ref[window(topic_at ^ flip, rows), columns].astype(F32)
                part = summed[chunk * rows : (chunk + 1) * rows, :]
                out_ref[i * rows : (i + 1) * rows, :] = (-prob * part).astype(BF16)
                chunk += 1

    return pl.pallas_call(
        kernel,
        out_shape=[jax.ShapeDtypeStruct((rows * len(piece), side_width), BF16) for piece in flips],
        in_specs=[SMEM] + [VMEM] * 4,
        out_specs=[VMEM] * len(flips),
        compiler_params=call_params(),
        cost_estimate=cost(KERNEL_COST, 1) if len(flips[0]) > 1 else cost(2 * words * docs * side_width, 2 * (4 * words + docs) * side_width),
        name="beta_pieces",
    )(here, product, ratio, docs_held, prob_held)


def stack_rows(parts, after):
    rows, docs = parts[0].shape

    def kernel(*refs):
        for i, ref in enumerate(refs[: len(parts)]):
            refs[-1][i * rows : (i + 1) * rows, :] = ref[...]

    return pl.pallas_call(
        kernel,
        out_shape=jax.ShapeDtypeStruct((len(parts) * rows, docs), BF16),
        in_specs=[VMEM] * len(parts) + [ANY] * len(after),
        out_specs=VMEM,
        compiler_params=call_params(),
        cost_estimate=cost(0, 4 * len(parts) * rows * docs),
        name="stack_rows",
    )(*parts, *after)


def cut_rows(array, count, after):
    rows, width = array.shape[0] // count, array.shape[1]

    def kernel(in_ref, *rest):
        for i, out_ref in enumerate(rest[len(after) :]):
            out_ref[...] = in_ref[i * rows : (i + 1) * rows, :]

    return pl.pallas_call(
        kernel,
        out_shape=[jax.ShapeDtypeStruct((rows, width), array.dtype)] * count,
        in_specs=[VMEM] + [ANY] * len(after),
        out_specs=[VMEM] * count,
        compiler_params=call_params(),
        cost_estimate=cost(0, 4 * array.size),
        name="cut_rows",
    )(array, *after)


def add_pair(own, other, after=(), flops=1):
    def kernel(own_ref, other_ref, *rest):
        rest[-1][...] = (own_ref[...].astype(F32) + other_ref[...].astype(F32)).astype(BF16)

    return pl.pallas_call(
        kernel,
        out_shape=jax.ShapeDtypeStruct(own.shape, BF16),
        in_specs=[VMEM, VMEM] + [ANY] * len(after),
        out_specs=VMEM,
        compiler_params=call_params(),
        cost_estimate=cost(max(flops, own.size), 6 * own.size),
        name="add_pair",
    )(own, other, *after)


def hold(array, after, flops=1):
    def kernel(in_ref, *rest):
        rest[-1][...] = in_ref[...]

    return pl.pallas_call(
        kernel,
        out_shape=jax.ShapeDtypeStruct(array.shape, array.dtype),
        in_specs=[VMEM] + [ANY] * len(after),
        out_specs=VMEM,
        compiler_params=call_params(),
        cost_estimate=cost(flops, 4 * array.size),
        name="hold",
    )(array, *after)


def turn_ratios(sizes, here, ratio, far_ratios):
    words, docs = ratio.shape
    half = words // 2
    count = 1 + len(far_ratios)

    def kernel(here_ref, *refs):
        side = sizes.side(here_ref)
        for l, (ref, out_ref) in enumerate(zip(refs[:count], refs[count:])):
            for h, which in enumerate((side, 1 - side) if l else (0, 1)):
                rows = ref[window(which, half), :].astype(F32)
                out_ref[:, h * half : (h + 1) * half] = (-rows).T.astype(BF16)

    return pl.pallas_call(
        kernel,
        out_shape=[jax.ShapeDtypeStruct((docs, words), BF16)] * count,
        in_specs=[SMEM] + [VMEM] * count,
        out_specs=[VMEM] * count,
        compiler_params=call_params(),
        cost_estimate=cost(TURN_COST, 1),
        name="turn_ratios",
    )(here, ratio, *far_ratios)


def theta_grad(sizes, here, turned, prob_held, far_logits, log_norm, after):
    docs, words = turned[0].shape
    cuts = len(far_logits[0])
    rows, share = far_logits[0][0].shape
    count = len(turned)
    span = min(share, 512)
    blocks = share // span

    def kernel(here_ref, *refs):
        turned_refs, prob_ref = refs[:count], refs[count]
        logit_refs, norm_ref = refs[count + 1 : -3 - len(after)], refs[-3 - len(after)]
        out_ref, done_ref = refs[-2:]
        done_ref[...] = jnp.zeros_like(done_ref)
        summed = jnp.dot(turned_refs[0][...], prob_ref[...], preferred_element_type=F32)
        for l in range(count - 1):
            part = logit_refs[cuts * l : cuts * (l + 1)]
            prob = jnp.concatenate([jnp.exp(ref[...].astype(F32) - norm_ref[...]).astype(BF16) for ref in part], axis=0)
            summed += jnp.dot(turned_refs[l + 1][...], prob, preferred_element_type=F32)
        out_ref[...] = summed

    whole = lambda j, h: (0, 0)
    held = lambda j, h: (0, lax.rem(h[0], sizes.vocab) * blocks + j)
    column = lambda j, h: (0, j)
    return pl.pallas_call(
        kernel,
        out_shape=[jax.ShapeDtypeStruct((docs, share), F32), jax.ShapeDtypeStruct((8, 128), F32)],
        grid_spec=pltpu.PrefetchScalarGridSpec(
            num_scalar_prefetch=1,
            grid=(blocks,),
            in_specs=[pl.BlockSpec((docs, words), whole)] * count
            + [pl.BlockSpec((words, span), held)]
            + [pl.BlockSpec((rows, span), column)] * (cuts * (count - 1))
            + [pl.BlockSpec((1, span), held)]
            + [ANY] * len(after),
            out_specs=[pl.BlockSpec((docs, span), column), pl.BlockSpec((8, 128), whole)],
        ),
        compiler_params=call_params(16),
        cost_estimate=cost(1, 1),
        name="theta_grad",
    )(here, *turned, prob_held, *sum(far_logits, []), log_norm, *after)


def place_pieces(sizes, here, own, other, flips, shape, so_far=None):
    pieces = len(own)
    side_width = shape[1] // 2
    before = [] if so_far is None else [so_far]

    def kernel(here_ref, *refs):
        own_refs, other_refs = refs[:pieces], refs[pieces : 2 * pieces]
        out_ref, sems = refs[2 * pieces + len(before)], refs[-1]
        if not before:
            refs[-2][...] = jnp.zeros_like(refs[-2])
        side, topic_at = sizes.side(here_ref), sizes.topic_at(here_ref)
        copies = []
        for p in range(pieces):
            rows = own_refs[p].shape[0] // len(flips[p])
            for h, (ref, which) in enumerate(((own_refs[p], side), (other_refs[p], 1 - side))):
                for i, flip in enumerate(flips[p]):
                    part = ref.at[pl.ds(i * rows, rows), :]
                    target = out_ref.at[window(topic_at ^ flip, rows), window(which, side_width)]
                    copies.append(pltpu.make_async_copy(part, target, sems.at[len(copies)]))
        for copy in copies:
            copy.start()
        for copy in copies:
            copy.wait()

    return pl.pallas_call(
        kernel,
        out_shape=[jax.ShapeDtypeStruct(shape, BF16)] + ([] if before else [jax.ShapeDtypeStruct((8, 128), F32)]),
        in_specs=[SMEM] + [VMEM] * (2 * pieces) + [HBM] * len(before),
        out_specs=[HBM] + ([] if before else [VMEM]),
        scratch_shapes=[pltpu.SemaphoreType.DMA((2 * sum(map(len, flips)),))],
        input_output_aliases={2 * pieces + 1: 0} if before else {},
        compiler_params=call_params(),
        cost_estimate=cost(0, 4 * sum(part.size for part in own)),
        name="place_pieces",
    )(here, *own, *other, *before)


def on_device(sizes, doc_topics, word_logits, log_norm, tile_doc, tile_word, word_counts):
    docs, width = doc_topics.shape
    words = word_logits.shape[0]
    word_tile = word_counts.shape[1]
    here = lax.axis_index(("doc", "topic", "vocab")).astype(jnp.int32)[None]

    def shift(array, by):
        return lax.ppermute(array, "vocab", [(i, (i + by) % sizes.vocab) for i in range(sizes.vocab)])

    def swap(array, axis, bits):
        count = {"doc": sizes.doc, "topic": sizes.topic}[axis]
        return lax.ppermute(array, axis, [(i, i ^ bits) for i in range(count)])

    parts, near_logits, docs_held, docs_sent, prob_held, norm_held = rate_partial(
        sizes, here, doc_topics, word_logits, log_norm[None, :]
    )
    sibling_docs = swap(docs_sent, "doc", 1)
    order = sorted(range(1, sizes.topic), key=lambda s: s < sizes.topic // 2)
    arrived = [swap(parts[s], "topic", s) for s in order]
    counts = chunk_counts(sizes, here, word_counts, tile_doc, tile_word, docs, words)
    own_ratio = ratio_chunk([parts[0]] + arrived, counts, word_tile)
    order = order[1:] + order[:1]
    gathered = [swap(own_ratio, "topic", s) for s in order]
    far_bits = [1 << b for b in range(1, sizes.doc.bit_length() - 1)]

    def beta(chunks, flips):
        ratio, sibling_ratio = chunks[0], swap(chunks[0], "doc", 1)
        if len(chunks) > 1:
            ratio = stack_rows(chunks, [])
            sibling_ratio = stack_rows([sibling_ratio] + [swap(chunk, "doc", 1) for chunk in chunks[1:]], [])
        pieces = beta_pieces(
            sizes, here, own_product(ratio, docs_held), sibling_ratio, sibling_docs, prob_held, flips
        )
        for bit in far_bits[:-1]:
            pieces = [add_pair(part, swap(part, "doc", bit)) for part in pieces]
        return [(part, swap(part, "doc", far_bits[-1])) for part in pieces]

    flips = [[0]] + [piece for piece in (order[-1:] + order[:-2], order[-2:-1]) if piece]
    pairs = beta([own_ratio], flips[:1])
    near_logits = [shift(hold(part, gathered[-1:]), s) for s, part in enumerate(near_logits, 1)]
    ratios = dict(zip(order, gathered))
    for piece in flips[1:]:
        pairs += beta([ratios[s] for s in piece], [piece])
    first = add_pair(*pairs[0], [], ADD_COST)

    ratio = join_ratio(sizes, here, [own_ratio] + gathered, [0] + order, [first, pairs[-1][0]])
    far_ratios = [shift(ratio, s) for s in range(1, sizes.vocab)]
    far_logits = []
    for part in near_logits:
        pieces = list(cut_rows(part, 2, [pairs[1][0]]))
        far_logits.append(pieces + [swap(piece, "doc", 1) for piece in pieces])
    turned = turn_ratios(sizes, here, ratio, far_ratios)
    out, early_done = place_pieces(sizes, here, [first], [swap(first, "doc", 1)], flips[:1], word_logits.shape)
    theta, theta_done = theta_grad(sizes, here, turned, prob_held, far_logits, norm_held, [early_done])
    sums = [add_pair(*pair, [theta_done]) for pair in pairs[1:]]
    siblings = [swap(part, "doc", 1) for part in sums]
    (out,) = place_pieces(sizes, here, sums, siblings, flips[1:], word_logits.shape, out)
    return theta, out


def solution(mesh):
    placed = (
        P("doc", "topic"),
        P("vocab", "topic"),
        P("topic"),
        P(("doc", "vocab")),
        P(("doc", "vocab")),
        P(("doc", "vocab"), None, None),
    )
    return jax.shard_map(
        functools.partial(on_device, Sizes(mesh)),
        mesh=mesh,
        in_specs=placed,
        out_specs=(P("doc", ("topic", "vocab")), P("vocab", "topic")),
        check_vma=False,
    )
```
